32 devices in a mesh: groups: 2 (over x), blk: 8 (over z, y), split: 2 (over core).
Axes of the slice: x: 2, y: 2, z: 4, core: 2. Of those that a mesh axis runs over, the one named last changes fastest.
Arguments:
- embeddings: bfloat16 [32768, 768], P(('groups', 'blk', 'split')), parts along dimension 0, may hold values from -6 to 6
- cluster_of: int32 [32768], P(('groups', 'blk', 'split')), parts along dimension 0, may hold values from 0 to 15, as said below
- target_pos: int32 [32768], P(('groups', 'blk', 'split')), parts along dimension 0, may hold values from 0 to 16383, as said below
Outputs:
- best: float32 [32768], P(('groups', 'blk', 'split')), parts along dimension 0
The draws below stay inside these ranges and needn't reach their ends.
There are 2 independent parts, one for each index of `groups`. The reference program is written for one: setup_inputs(seed, part) draws one part's arguments, and reference() takes and returns one part's arrays. A program takes and returns all parts, laid end to end along the dimension named above; each array names one. Nothing has to cross between parts.
Inputs may be any that keep to these rules, and one draw needn't show every extreme that they name: `cluster_of`: ordering the members by target_pos lists cluster 0 first, then cluster 1 and so on, each cluster's members contiguous; every cluster has 2 to 4096 members and one has exactly 4096. `target_pos`: A permutation of the rows. For every aligned block of 1024 positions, each device's 1024 data-order rows hold exactly 64 of its positions.
All inputs are finite; a program needn't handle non-finite values.
Results may differ from the reference program's by a relative error of at most 0.0025.
Values may be sent and summed in bfloat16 or wider, within the bound.
No kernel may reach another device: no remote copies, remote signals or barrier semaphores. Data moves between devices by JAX's collectives and lax.ppermute only.
A program may use at most 64 MiB of HBM per device.

```python
import jax
import jax.numpy as jnp
from jax import lax

D = 768
ROWS_DEV = 1024
DEVS_PART = 16
ROWS = 16384
CLUSTERS = 16
MOST = 4096


def layout_draw(key):
    key = jax.random.fold_in(key, 7)
    key_big, key_weights, key_blocks, key_shuffle = jax.random.split(key, 4)
    count = DEVS_PART
    rows = ROWS_DEV
    total = ROWS
    index = jnp.arange(CLUSTERS, dtype=jnp.int32)
    big = jax.random.randint(key_big, (), 0, CLUSTERS)
    weights = jax.random.randint(key_weights, (CLUSTERS,), 4, 8)
    others = index != big
    weights = jnp.where(others, weights, 0)
    spare = total - MOST - 2 * (CLUSTERS - 1)
    share = weights * spare // jnp.sum(weights)
    leftover = spare - jnp.sum(share)
    ranks = jnp.cumsum(others.astype(jnp.int32)) - 1
    extra = ((ranks < leftover) & others).astype(jnp.int32)
    sizes = jnp.where(others, 2 + share + extra, MOST).astype(jnp.int32)
    ends = jnp.cumsum(sizes)
    position = jnp.arange(total, dtype=jnp.int32)
    sorted_ids = jnp.sum((position[:, None] >= ends[None, :]).astype(jnp.int32), axis=1).astype(jnp.int32)
    perms = jax.vmap(lambda k: jax.random.permutation(k, rows))(jax.random.split(key_blocks, count))
    blocks = (jnp.arange(count, dtype=jnp.int32)[:, None] * rows + perms.astype(jnp.int32)).reshape(count, count, rows // count)
    by_source = jnp.transpose(blocks, (1, 0, 2)).reshape(count, rows)
    shuffle = jax.vmap(lambda k: jax.random.permutation(k, rows))(jax.random.split(key_shuffle, count))
    by_source = jnp.take_along_axis(by_source, shuffle.astype(jnp.int32), axis=1)
    target = by_source.reshape(total).astype(jnp.int32)
    return (sorted_ids[target], target)


def draw_cluster_of(key, part):
    return layout_draw(key)[0]


def draw_target_pos(key, part):
    return layout_draw(key)[1]


def block_scale(key, extent, shards, least, high):
    gain = 1.0
    for dim, parts in shards:
        steps = jax.random.uniform(jax.random.fold_in(jax.random.fold_in(key, 6), dim), (parts,), jnp.float32, least / len(shards), high / len(shards))
        gain = gain * jnp.repeat(jnp.exp(steps), extent[dim] // parts).reshape((-1,) + (1,) * (len(extent) - 1 - dim))
    return gain


def normal_values(key, dims, width, bound, cuts=(), held_as=jnp.bfloat16):
    loudness = block_scale(key, dims, cuts, -0.22, 0.18) if cuts else 1.0
    array = jax.random.normal(key, dims, jnp.float32) * width * loudness
    return jnp.minimum(jnp.maximum(array, -bound), bound).astype(held_as)


def setup_inputs(seed: int = 0, part: int = 0) -> dict:
    arg_keys = jax.random.split(jax.random.key(seed), 4)
    part_keys = jax.random.split(jax.random.fold_in(arg_keys[3], part), 4)
    embeddings = normal_values(part_keys[0], (ROWS, D), 1.0, 6.0, ((0, 16),))
    cluster_of = draw_cluster_of(jax.random.fold_in(jax.random.fold_in(arg_keys[3], part), 71), part)
    target_pos = draw_target_pos(jax.random.fold_in(jax.random.fold_in(arg_keys[3], part), 71), part)
    return {"embeddings": embeddings, "cluster_of": cluster_of, "target_pos": target_pos}


def reference(embeddings, cluster_of, target_pos):
    values = embeddings.astype(jnp.float32)
    unit = (values * lax.rsqrt(lax.optimization_barrier(jnp.sum(values * values, axis=1, keepdims=True)) + 1e-06)).astype(jnp.bfloat16)
    sorted_unit = jnp.zeros((ROWS, D), jnp.bfloat16).at[target_pos].set(unit)
    sorted_ids = jnp.zeros((ROWS,), jnp.int32).at[target_pos].set(cluster_of)
    margin = MOST
    span = ROWS_DEV + 2 * margin
    pad_unit = jnp.concatenate([jnp.zeros((margin, D), jnp.bfloat16), sorted_unit, jnp.zeros((margin, D), jnp.bfloat16)], axis=0)
    pad_ids = jnp.concatenate([jnp.full((margin,), -1, jnp.int32), sorted_ids, jnp.full((margin,), -1, jnp.int32)], axis=0)

    def one_block(block):
        start = (block * ROWS_DEV).astype(jnp.int32)
        rows = lax.dynamic_slice_in_dim(sorted_unit, start, ROWS_DEV, 0)
        row_ids = lax.dynamic_slice_in_dim(sorted_ids, start, ROWS_DEV, 0)
        window = lax.dynamic_slice_in_dim(pad_unit, start, span, 0)
        window_ids = lax.dynamic_slice_in_dim(pad_ids, start, span, 0)
        sims = jnp.dot(rows, window.T, preferred_element_type=jnp.float32)
        row_pos = start + jnp.arange(ROWS_DEV, dtype=jnp.int32)
        window_pos = start - margin + jnp.arange(span, dtype=jnp.int32)
        keep = (row_ids[:, None] == window_ids[None, :]) & (row_pos[:, None] != window_pos[None, :])
        return lax.optimization_barrier(jnp.max(jnp.where(keep, sims, -4.0), axis=1))
    best_sorted = lax.map(one_block, jnp.arange(ROWS // ROWS_DEV, dtype=jnp.int32)).reshape(ROWS)
    return best_sorted[target_pos]
```

```python
import functools

import jax
import jax.numpy as jnp
from jax import lax
from jax.experimental import pallas as pl
from jax.experimental.pallas import tpu as pltpu
from jax.sharding import PartitionSpec as P

MOST = 4096
FILL = -4.0
TAGS = 8
LANES = 128
VMEM = 48 * 1024 * 1024
WHOLE = pl.BlockSpec(memory_space=pltpu.VMEM)
SCALARS = pl.BlockSpec(memory_space=pltpu.SMEM)


def spread(row):
    return jnp.transpose(jnp.broadcast_to(row, (LANES, row.shape[1])))


def column_fold(scores):
    rows, columns = scores.shape
    return jnp.max(scores.reshape(rows // 8, 8, columns), axis=0)


def lane_fold(scores):
    best = scores[:, :LANES]
    for at in range(LANES, scores.shape[1], LANES):
        best = jnp.maximum(best, scores[:, at : at + LANES])
    return best


def order_kernel(parts, place_ref, rows_ref, ids_ref, pos_ref, *refs):
    outs, rank_ref, unit, pick, placed, tags = refs[:parts], *refs[parts:]
    count, width = rows_ref.shape
    slots = count // parts
    step = 256
    values = rows_ref[...].astype(jnp.float32)
    total = jnp.sum(values * values, axis=1, keepdims=True)
    unit[...] = (values * lax.rsqrt(total + 1e-06)).astype(jnp.bfloat16)
    pos = pos_ref[...].astype(jnp.float32)
    below = jnp.zeros((8, count), jnp.float32)
    for at in range(0, count, step):
        other = spread(pos[:, at : at + step])[:, :1]
        below += jnp.sum(jnp.where(other < pos, 1.0, 0.0).reshape(step // 8, 8, count), axis=0)
    rank = jnp.sum(below, axis=0, keepdims=True).astype(jnp.int32)
    rank_ref[...] = rank
    for at in range(0, count, step):
        slot = lax.broadcasted_iota(jnp.int32, (step, count), 0) + at
        pick[at : at + step, :] = jnp.where(slot == rank, 1.0, 0.0).astype(jnp.bfloat16)
    for at in range(0, count, step):
        placed[at : at + step, :] = jnp.dot(
            pick[at : at + step, :], unit[...], preferred_element_type=jnp.float32
        ).astype(jnp.bfloat16)
    ids = jnp.broadcast_to((ids_ref[...] + 1).astype(jnp.bfloat16), (16, count))
    sorted_ids = lax.dot_general(
        ids, pick[...], (((1,), (1,)), ((), ())), preferred_element_type=jnp.float32
    )
    for part in range(parts):
        tags[part, :, :slots] = sorted_ids[:, part * slots : (part + 1) * slots]
    for shift in range(parts):
        goal = lax.rem(place_ref[0] + shift, parts)
        outs[shift][:slots, :] = placed[pl.ds(pl.multiple_of(goal * slots, slots), slots), :]
        outs[shift][slots:, :slots] = tags[goal, :TAGS, :slots].astype(jnp.bfloat16)


def in_order(place, embeddings, ids, pos, parts):
    count, width = embeddings.shape
    slots = count // parts
    return pl.pallas_call(
        functools.partial(order_kernel, parts),
        out_shape=[jax.ShapeDtypeStruct((slots + TAGS, width), jnp.bfloat16)] * parts
        + [jax.ShapeDtypeStruct((1, count), jnp.int32)],
        in_specs=[SCALARS, WHOLE, WHOLE, WHOLE],
        out_specs=[WHOLE] * (parts + 1),
        scratch_shapes=[
            pltpu.VMEM((count, width), jnp.bfloat16),
            pltpu.VMEM((count, count), jnp.bfloat16),
            pltpu.VMEM((count, width), jnp.bfloat16),
            pltpu.VMEM((parts, 16, max(slots, LANES)), jnp.float32),
        ],
        compiler_params=pltpu.CompilerParams(vmem_limit_bytes=VMEM),
        cost_estimate=pl.CostEstimate(
            flops=2 * count * count * width, bytes_accessed=4 * count * width, transcendentals=count
        ),
        name="order",
    )(place, embeddings, ids.reshape(1, count), pos.reshape(1, count))


def gather_left(parts, buffer, ids):
    at = 0
    for ref, n in parts:
        buffer[at : at + n, :] = ref[:n, :]
        ids[:, at : at + n] = ref[n : n + TAGS, :n].astype(jnp.float32)
        at += n


def gather_right(parts, buffer, ids):
    at = 0
    for ref, n in parts:
        buffer[at : at + n, :] = ref[:n, :]
        ids[at : at + n, :] = spread(ref[n : n + 1, :n].astype(jnp.float32))
        at += n


def masked(left, left_ids, right, right_ids):
    scores = lax.dot_general(
        right, left, (((1,), (1,)), ((), ())), preferred_element_type=jnp.float32
    )
    return jnp.where(right_ids[:, :1] == left_ids[:1, :], scores, FILL)


def quarter_kernel(parts, others, step, *refs):
    own, rest = refs[:parts], refs[parts : parts + others]
    best_ref, left, left_ids, right, right_ids = refs[parts + others :]
    slots = own[0].shape[0] - TAGS
    gather_left([(r, slots) for r in own], left, left_ids)
    gather_right([(r, slots) for r in own] + [(r, slots) for r in rest], right, right_ids)
    count = left.shape[0]

    def turn(index, best, diagonal):
        at = pl.multiple_of(index * step, step)
        scores = masked(
            left[...], left_ids[...], right[pl.ds(at, step), :], right_ids[pl.ds(at, step), :]
        )
        if diagonal:
            down = lax.broadcasted_iota(jnp.int32, (step, count), 0) + at
            across = lax.broadcasted_iota(jnp.int32, (step, count), 1)
            scores = jnp.where(down == across, FILL, scores)
        return jnp.maximum(best, column_fold(scores))

    best = jnp.full((8, count), FILL, jnp.float32)
    best = lax.fori_loop(0, count // step, functools.partial(turn, diagonal=True), best)
    best = lax.fori_loop(
        count // step, right.shape[0] // step, functools.partial(turn, diagonal=False), best
    )
    best_ref[...] = jnp.max(best, axis=0, keepdims=True)


def quarter_best(own, rest):
    slots, width = own[0].shape[0] - TAGS, own[0].shape[1]
    count = slots * len(own)
    total = slots * (len(own) + len(rest))
    return pl.pallas_call(
        functools.partial(quarter_kernel, len(own), len(rest), 256),
        out_shape=jax.ShapeDtypeStruct((1, count), jnp.float32),
        in_specs=[WHOLE] * (len(own) + len(rest)),
        out_specs=WHOLE,
        scratch_shapes=[
            pltpu.VMEM((count, width), jnp.bfloat16),
            pltpu.VMEM((TAGS, count), jnp.float32),
            pltpu.VMEM((total, width), jnp.bfloat16),
            pltpu.VMEM((total, LANES), jnp.float32),
        ],
        compiler_params=pltpu.CompilerParams(vmem_limit_bytes=VMEM),
        cost_estimate=pl.CostEstimate(
            flops=2 * count * total * width, bytes_accessed=2 * total * width, transcendentals=0
        ),
        name="quarter",
    )(*own, *rest)


def border_kernel(parts, members, step, place_ref, *refs):
    quarter, refs = refs[: parts * members], refs[parts * members :]
    tails, own_tail, heads, own_head, best_ref = refs[:5]
    out_ref, left, left_ids, right, right_ids, right_best, left_best = refs[5:]
    slots = quarter[0].shape[0] - TAGS
    half = slots // 2
    around = parts * half
    gather_left([(r, slots) for r in quarter], left, left_ids)
    for base, moved, kept, cut in ((0, tails, own_tail, half), (around, heads, own_head, 0)):
        n = around - half
        gather_right(
            [(moved, n)], right.at[pl.ds(base, n), :], right_ids.at[pl.ds(base, n), :]
        )
        right[base + n : base + around, :] = kept[cut : cut + half, :]
        kept_ids = spread(kept[slots : slots + 1, :slots].astype(jnp.float32))
        right_ids[base + n : base + around, :] = kept_ids[cut : cut + half, :]
    total = 2 * around

    def turn(index, best):
        at = pl.multiple_of(index * step, step)
        scores = masked(
            left[...], left_ids[...], right[pl.ds(at, step), :], right_ids[pl.ds(at, step), :]
        )
        right_best[pl.ds(at, step), :] = lane_fold(scores)
        return jnp.maximum(best, column_fold(scores))

    best = lax.fori_loop(
        0, total // step, turn, jnp.full((8, left.shape[0]), FILL, jnp.float32)
    )
    left_best[...] = jnp.max(best, axis=0, keepdims=True)
    count = parts * slots
    left_best[:, :count] = jnp.maximum(left_best[:, :count], best_ref[...])
    visit = jnp.max(jnp.transpose(right_best[...]), axis=0, keepdims=True)
    mine, me_member, width = place_ref[0], place_ref[1], members
    out_ref[...] = jnp.full(out_ref.shape, FILL, jnp.float32)
    for member in range(members):
        whose = lax.bitwise_xor(me_member, member)
        for k in range(parts):
            source = lax.rem(mine - k + parts, parts)
            at = (member * parts + k) * slots
            out_ref[source * width + whose, :, :slots] = left_best[:, at : at + slots]
    for base, offset, kept in ((0, -1, parts - 1), (around, 1, 1)):
        order = [k for k in range(parts) if k != kept] + [kept]
        for index, k in enumerate(order):
            source = lax.rem(mine + offset - k + 2 * parts, parts)
            at = base + index * half
            lane = slots if base == 0 else slots + half
            out_ref[source * width + me_member, :, lane : lane + half] = visit[:, at : at + half]


def border_best(place, quarter, tails, own_tail, heads, own_head, best, parts):
    members = len(quarter) // parts
    slots, width = quarter[0].shape[0] - TAGS, quarter[0].shape[1]
    total, around = slots * len(quarter), parts * slots
    return pl.pallas_call(
        functools.partial(border_kernel, parts, members, 128),
        out_shape=jax.ShapeDtypeStruct((parts * members, 1, 2 * slots), jnp.float32),
        in_specs=[SCALARS] + [WHOLE] * (len(quarter) + 5),
        out_specs=WHOLE,
        scratch_shapes=[
            pltpu.VMEM((total, width), jnp.bfloat16),
            pltpu.VMEM((TAGS, total), jnp.float32),
            pltpu.VMEM((around, width), jnp.bfloat16),
            pltpu.VMEM((around, LANES), jnp.float32),
            pltpu.VMEM((around, LANES), jnp.float32),
            pltpu.VMEM((1, total), jnp.float32),
        ],
        compiler_params=pltpu.CompilerParams(vmem_limit_bytes=VMEM),
        cost_estimate=pl.CostEstimate(
            flops=2 * around * total * width, bytes_accessed=2 * total * width, transcendentals=0
        ),
        name="border",
    )(place, *quarter, tails, own_tail, heads, own_head, best)


def back_kernel(parts, members, got_ref, rank_ref, out_ref):
    slots = got_ref.shape[2] // 2
    half = slots // 2
    rows = []
    for part in range(parts):
        best = got_ref[part * members]
        for member in range(1, members):
            best = jnp.maximum(best, got_ref[part * members + member])
        rows.append(best)
    rank = rank_ref[...]
    nothing = jnp.full((1, half), FILL, jnp.float32)
    best = jnp.full((8, rank.shape[1]), FILL, jnp.float32)
    for part in range(parts):
        heads = rows[part - 1][:, slots + half :] if part > 0 else nothing
        tails = rows[part + 1][:, slots : slots + half] if part < parts - 1 else nothing
        values = jnp.maximum(rows[part][:, :slots], jnp.concatenate([heads, tails], axis=1))
        slot = lax.broadcasted_iota(jnp.int32, (slots, rank.shape[1]), 0) + part * slots
        found = jnp.where(slot == rank, spread(values)[:, :1], FILL)
        best = jnp.maximum(best, column_fold(found))
    out_ref[...] = jnp.max(best, axis=0, keepdims=True)


def in_data_order(got, rank, parts, members):
    return pl.pallas_call(
        functools.partial(back_kernel, parts, members),
        out_shape=jax.ShapeDtypeStruct(rank.shape, jnp.float32),
        in_specs=[WHOLE, WHOLE],
        out_specs=WHOLE,
        compiler_params=pltpu.CompilerParams(vmem_limit_bytes=VMEM),
        name="back",
    )(got, rank)


def halves(pieces, first, half):
    slots = 2 * half
    start = 0 if first else half
    rows = [p[start : start + half] for p in pieces]
    tags = jnp.concatenate([p[slots:, start : start + half] for p in pieces], axis=1)
    tags = jnp.pad(tags, ((0, 0), (0, pieces[0].shape[1] - tags.shape[1])))
    return jnp.concatenate(rows + [tags], axis=0)


def body(embeddings, cluster_of, target_pos):
    blocks, cores = lax.axis_size("blk"), lax.axis_size("split")
    rows, width = embeddings.shape
    members = MOST // rows
    chips = members // cores
    parts = blocks // chips
    half = rows // parts // 2
    chip, core = lax.axis_index("blk"), lax.axis_index("split")
    place = jnp.stack([chip // chips, (chip % chips) * cores + core]).astype(jnp.int32)

    def along(array, shift, wrap):
        route = []
        for part in range(parts):
            goal = part + shift
            if wrap or 0 <= goal < parts:
                for c in range(chips):
                    route.append((part * chips + c, goal % parts * chips + c))
        return lax.ppermute(array, "blk", route)

    def chip_swap(array):
        return lax.ppermute(array, "blk", [(b, b ^ 1) for b in range(blocks)])

    def core_swap(array):
        return lax.ppermute(array, "split", [(c, c ^ 1) for c in range(cores)])

    *pieces, rank = in_order(place, embeddings, cluster_of, target_pos, parts)
    mine = [pieces[0]] + [along(pieces[k], k, True) for k in range(1, parts)]
    tails = along(halves([mine[k] for k in range(parts) if k != parts - 1], False, half), 1, False)
    heads = along(halves([mine[k] for k in range(parts) if k != 1], True, half), -1, False)
    over = [chip_swap(piece) for piece in mine]
    beside = [core_swap(piece) for piece in mine]
    across = [core_swap(piece) for piece in over]
    best = quarter_best(mine, beside + over + across)
    found = border_best(
        place, mine + beside + over + across, tails, pieces[parts - 1], heads, pieces[1], best, parts
    )
    got = lax.all_to_all(found, ("blk", "split"), split_axis=0, concat_axis=0, tiled=True)
    return in_data_order(got, rank, parts, members).reshape(rows)


def solution(mesh):
    spec = P(("groups", "blk", "split"))
    return jax.shard_map(
        body,
        mesh=mesh,
        in_specs=(P(("groups", "blk", "split"), None), spec, spec),
        out_specs=spec,
        check_vma=False,
    )
```

```python
import functools

import jax
import jax.numpy as jnp
from jax import lax
from jax.experimental import pallas as pl
from jax.experimental.pallas import tpu as pltpu
from jax.sharding import PartitionSpec as P

MOST = 4096
FILL = -4.0
TAGS = 8
LANES = 128
MIB = 1024 * 1024
WHOLE = pl.BlockSpec(memory_space=pltpu.VMEM)
ANYWHERE = pl.BlockSpec(memory_space=pl.ANY)
SCALARS = pl.BlockSpec(memory_space=pltpu.SMEM)


def grant(mib):
    return pltpu.CompilerParams(vmem_limit_bytes=mib * MIB)


def spread(row):
    return jnp.transpose(jnp.broadcast_to(row, (LANES, row.shape[1])))


def column_fold(scores):
    rows, columns = scores.shape
    return jnp.max(scores.reshape(rows // 8, 8, columns), axis=0)


def lane_fold(scores):
    best = scores[:, :LANES]
    for at in range(LANES, scores.shape[1], LANES):
        best = jnp.maximum(best, scores[:, at : at + LANES])
    return best


def order_kernel(parts, place_ref, rows_ref, ids_ref, pos_ref, *refs):
    first, own, rank_ref = refs[:3]
    facing, turned = refs[3 : 1 + parts], refs[1 + parts : 2 * parts - 1]
    unit, pick, placed, tags = refs[2 * parts - 1 :]
    count, width = rows_ref.shape
    half = count // parts // 2
    step = 256
    values = rows_ref[...].astype(jnp.float32)
    total = jnp.sum(values * values, axis=1, keepdims=True)
    unit[...] = (values * lax.rsqrt(total + 1e-06)).astype(jnp.bfloat16)
    pos = pos_ref[...].astype(jnp.float32)
    below = jnp.zeros((8, count), jnp.float32)
    for at in range(0, count, step):
        other = spread(pos[:, at : at + step])[:, :1]
        below += jnp.sum(jnp.where(other < pos, 1.0, 0.0).reshape(step // 8, 8, count), axis=0)
    rank = jnp.sum(below, axis=0, keepdims=True).astype(jnp.int32)
    rank_ref[...] = rank
    for at in range(0, count, step):
        slot = lax.broadcasted_iota(jnp.int32, (step, count), 0) + at
        pick[at : at + step, :] = jnp.where(slot == rank, 1.0, 0.0).astype(jnp.bfloat16)
    for at in range(0, count, step):
        placed[at : at + step, :] = jnp.dot(
            pick[at : at + step, :], unit[...], preferred_element_type=jnp.float32
        ).astype(jnp.bfloat16)
    ids = jnp.broadcast_to((ids_ref[...] + 1).astype(jnp.bfloat16), (16, count))
    sorted_ids = lax.dot_general(
        ids, pick[...], (((1,), (1,)), ((), ())), preferred_element_type=jnp.float32
    )
    for at in range(2 * parts):
        tags[at, :, :half] = sorted_ids[:, at * half : (at + 1) * half]

    def put(out, at, quarter, faces):
        side = lax.rem(quarter, 2)
        which = 2 * quarter + (1 - side if faces else side)
        out[at : at + half, :] = placed[pl.ds(pl.multiple_of(which * half, half), half), :]
        out[out.shape[0] - TAGS :, at : at + half] = tags[which, :TAGS, :half].astype(jnp.bfloat16)

    part = place_ref[0]
    for out, quarter in ((first, lax.bitwise_xor(part, 1)), (own, part)):
        put(out, 0, quarter, True)
        put(out, half, quarter, False)
    put(first, 2 * half, part, True)
    for k in range(2, parts):
        put(facing[k - 2], 0, lax.bitwise_xor(part, k), True)
        put(turned[k - 2], 0, lax.bitwise_xor(part, k), False)


def in_order(place, embeddings, ids, pos, parts):
    count, width = embeddings.shape
    half = count // parts // 2

    def block(rows):
        return jax.ShapeDtypeStruct((rows + TAGS, width), jnp.bfloat16)

    outs = [block(3 * half), block(2 * half), jax.ShapeDtypeStruct((1, count), jnp.int32)]
    outs += [block(half)] * (2 * (parts - 2))
    first, own, rank, *rest = pl.pallas_call(
        functools.partial(order_kernel, parts),
        out_shape=outs,
        in_specs=[SCALARS, WHOLE, WHOLE, WHOLE],
        out_specs=[WHOLE] * len(outs),
        scratch_shapes=[
            pltpu.VMEM((count, width), jnp.bfloat16),
            pltpu.VMEM((count, count), jnp.bfloat16),
            pltpu.VMEM((count, width), jnp.bfloat16),
            pltpu.VMEM((2 * parts, 16, max(half, LANES)), jnp.float32),
        ],
        compiler_params=grant(24),
        name="order",
    )(place, embeddings, ids.reshape(1, count), pos.reshape(1, count))
    return first, own, rank, rest[: parts - 2], rest[parts - 2 :]


def pack_kernel(plan, inputs, *refs):
    given, outs = refs[:inputs], refs[-len(plan) :]
    for out, pieces in zip(outs, plan):
        at = 0
        for index, start, rows in pieces:
            ref = given[index]
            out[at : at + rows, :] = ref[start : start + rows, :]
            out[out.shape[0] - TAGS :, at : at + rows] = ref[
                ref.shape[0] - TAGS :, start : start + rows
            ]
            at += rows


def pack(blocks, plan, held=()):
    width = blocks[0].shape[1]
    plan = [list(pieces) for pieces in plan]
    outs = [
        jax.ShapeDtypeStruct((sum(p[2] for p in pieces) + TAGS, width), jnp.bfloat16)
        for pieces in plan
    ]
    kept = [jax.ShapeDtypeStruct(h.shape, h.dtype) for h in held]

    def kernel(*refs):
        given = refs[: len(blocks)]
        made = refs[len(blocks) + 2 * len(held) :]
        pack_kernel(plan, len(given), *given, *made)

    return pl.pallas_call(
        kernel,
        out_shape=kept + outs,
        in_specs=[WHOLE] * len(blocks) + [ANYWHERE] * len(held),
        out_specs=[ANYWHERE] * len(held) + [WHOLE] * len(outs),
        input_output_aliases={len(blocks) + i: i for i in range(len(held))},
        compiler_params=grant(8),
        name="pack",
    )(*blocks, *held)


def after(held, earlier):
    return pl.pallas_call(
        lambda *refs: None,
        out_shape=[jax.ShapeDtypeStruct(h.shape, h.dtype) for h in held],
        in_specs=[ANYWHERE] * (len(held) + len(earlier)),
        out_specs=[ANYWHERE] * len(held),
        input_output_aliases={i: i for i in range(len(held))},
        compiler_params=grant(1),
        name="after",
    )(*held, *earlier)


def meet_kernel(plan_left, plan_right, inputs, step, own, visits, *refs):
    given = refs[:inputs]
    left_out = refs[inputs]
    right_out = refs[inputs + 1] if visits else None
    left, left_ids, right, right_ids = refs[inputs + 1 + visits : inputs + 5 + visits]
    at = 0
    for index, start, rows in plan_left:
        ref = given[index]
        left[at : at + rows, :] = ref[start : start + rows, :]
        tags = ref[ref.shape[0] - TAGS :, start : start + rows]
        left_ids[:, at : at + rows] = tags.astype(jnp.float32)
        at += rows
    at = 0
    for index, start, rows in plan_right:
        ref = given[index]
        right[at : at + rows, :] = ref[start : start + rows, :]
        tags = ref[ref.shape[0] - TAGS : ref.shape[0] - TAGS + 1, start : start + rows]
        right_ids[at : at + rows, :] = spread(tags.astype(jnp.float32))
        at += rows
    count, total = left.shape[0], right.shape[0]

    def turn(index, best, diagonal):
        at = pl.multiple_of(index * step, step)
        scores = lax.dot_general(
            right[pl.ds(at, step), :],
            left[...],
            (((1,), (1,)), ((), ())),
            preferred_element_type=jnp.float32,
        )
        scores = jnp.where(right_ids[pl.ds(at, step), :1] == left_ids[:1, :], scores, FILL)
        if diagonal:
            down = lax.broadcasted_iota(jnp.int32, (step, count), 0) + at
            across = lax.broadcasted_iota(jnp.int32, (step, count), 1)
            scores = jnp.where(down == across, FILL, scores)
        if visits:
            refs[-1][pl.ds(at, step), :] = lane_fold(scores)
        return jnp.maximum(best, column_fold(scores))

    best = jnp.full((8, count), FILL, jnp.float32)
    split = count // step if own else 0
    if own:
        best = lax.fori_loop(0, split, functools.partial(turn, diagonal=True), best)
    best = lax.fori_loop(split, total // step, functools.partial(turn, diagonal=False), best)
    left_out[...] = jnp.max(best, axis=0, keepdims=True)
    if visits:
        right_out[...] = jnp.max(jnp.transpose(refs[-1][...]), axis=0, keepdims=True)


def meet(left, right, own=False, visits=False):
    blocks = []

    def plan(pieces):
        out = []
        for block, start, rows in pieces:
            known = [i for i, b in enumerate(blocks) if b is block]
            if not known:
                blocks.append(block)
            out.append((known[0] if known else len(blocks) - 1, start, rows))
        return out

    plan_left, plan_right = plan(left), plan(right)
    width = blocks[0].shape[1]
    count, total = sum(p[2] for p in left), sum(p[2] for p in right)
    step = 8
    while step < 512 and total % (2 * step) == 0 and (count % (2 * step) == 0 or not own):
        if 2 * step * count * 4 > 4 * MIB:
            break
        step *= 2
    scratch = [
        pltpu.VMEM((count, width), jnp.bfloat16),
        pltpu.VMEM((TAGS, count), jnp.float32),
        pltpu.VMEM((total, width), jnp.bfloat16),
        pltpu.VMEM((total, LANES), jnp.float32),
    ]
    outs = [jax.ShapeDtypeStruct((1, count), jnp.float32)]
    if visits:
        scratch.append(pltpu.VMEM((total, LANES), jnp.float32))
        outs.append(jax.ShapeDtypeStruct((1, total), jnp.float32))
    return pl.pallas_call(
        functools.partial(
            meet_kernel, plan_left, plan_right, len(blocks), step, own, visits
        ),
        out_shape=outs,
        in_specs=[WHOLE] * len(blocks),
        out_specs=[WHOLE] * len(outs),
        scratch_shapes=scratch,
        compiler_params=grant(32),
        cost_estimate=pl.CostEstimate(
            flops=2 * count * total * width, bytes_accessed=0, transcendentals=0
        ),
        name="meet",
    )(*blocks)


def route_kernel(parts, members, half, near, place_ref, *refs):
    own_a, own_b, before_u, before_v, last, u_before, v_before, visit_last, out_ref = refs
    part, me = place_ref[0], place_ref[1]
    slots = 2 * half
    rest = (parts - 2) * half
    early = 2 * slots + rest
    out_ref[...] = jnp.full(out_ref.shape, FILL, jnp.float32)
    quarter = jnp.maximum(before_u[...], before_v[...])
    final = last[...]
    own = jnp.maximum(own_a[...], own_b[...])
    for member in range(members):
        whose = lax.bitwise_xor(me, member)
        block = quarter[:, member * early : (member + 1) * early]
        tail = final[:, member * rest : (member + 1) * rest]
        if member == 0:
            block = jnp.maximum(block, own[:, :early])
            tail = jnp.maximum(tail, own[:, early:])
        for k in range(parts):
            source = lax.bitwise_xor(part, k) * members + whose
            if k < 2:
                out_ref[source, :, :slots] = block[:, k * slots : (k + 1) * slots]
            else:
                at = (k - 2) * half
                out_ref[source, :, :half] = block[:, 2 * slots + at : 2 * slots + at + half]
                out_ref[source, :, half:slots] = tail[:, at : at + half]
    size = parts * half
    visit_u = jnp.maximum(u_before[...], visit_last[:, :size])
    visit_v = jnp.maximum(v_before[...], visit_last[:, size:])
    beyond = lax.rem(part + parts - 1 + 2 * lax.rem(part, 2), parts)
    if near:
        beyond = lax.bitwise_xor(part, 3)
    next_to = lax.bitwise_xor(part, 1)
    from_u = [next_to] + [lax.bitwise_xor(next_to, k) for k in range(2, parts)] + [part]
    from_v = [beyond, lax.bitwise_xor(beyond, 1)]
    from_v += [next_to, part] if near else [lax.bitwise_xor(beyond, k) for k in range(2, parts)]
    for visit, sources, lane in ((visit_u, from_u, slots), (visit_v, from_v, slots + half)):
        for index, source in enumerate(sources):
            at = index * half
            out_ref[source * members + me, :, lane : lane + half] = visit[:, at : at + half]


def back_kernel(parts, members, got_ref, rank_ref, out_ref):
    slots = got_ref.shape[2] // 2
    half = slots // 2
    rows = []
    for part in range(parts):
        best = got_ref[part * members]
        for member in range(1, members):
            best = jnp.maximum(best, got_ref[part * members + member])
        rows.append(best)
    rank = rank_ref[...]
    nothing = jnp.full((1, half), FILL, jnp.float32)
    best = jnp.full((8, rank.shape[1]), FILL, jnp.float32)
    for part in range(parts):
        beyond = part + 1 if part % 2 else part - 1
        there = 0 <= beyond < parts
        faces = jnp.maximum(rows[part][:, :half], rows[part ^ 1][:, slots : slots + half])
        turned = jnp.maximum(
            rows[part][:, half:slots], rows[beyond][:, slots + half :] if there else nothing
        )
        pair = [faces, turned] if part % 2 else [turned, faces]
        values = spread(jnp.concatenate(pair, axis=1))[:, :1]
        slot = lax.broadcasted_iota(jnp.int32, (slots, rank.shape[1]), 0) + part * slots
        best = jnp.maximum(best, column_fold(jnp.where(slot == rank, values, FILL)))
    out_ref[...] = jnp.max(best, axis=0, keepdims=True)


def in_data_order(got, rank, parts, members):
    return pl.pallas_call(
        functools.partial(back_kernel, parts, members),
        out_shape=jax.ShapeDtypeStruct(rank.shape, jnp.float32),
        in_specs=[WHOLE, WHOLE],
        out_specs=WHOLE,
        compiler_params=grant(16),
        name="back",
    )(got, rank)


def body(embeddings, cluster_of, target_pos):
    blocks, cores = lax.axis_size("blk"), lax.axis_size("split")
    rows, width = embeddings.shape
    members = MOST // rows
    chips = members // cores
    parts = blocks // chips
    half = rows // parts // 2
    slots = 2 * half
    rest = (parts - 2) * half
    chip, core = lax.axis_index("blk"), lax.axis_index("split")
    place = jnp.stack([chip // chips, (chip % chips) * cores + core]).astype(jnp.int32)

    def between(array, pairs):
        route = [(s * chips + c, t * chips + c) for s, t in pairs for c in range(chips)]
        return lax.ppermute(array, "blk", route)

    def swap(array, k):
        return between(array, [(part, part ^ k) for part in range(parts)])

    def chip_swap(array):
        return lax.ppermute(array, "blk", [(b, b ^ 1) for b in range(blocks)])

    def core_swap(array):
        return lax.ppermute(array, "split", [(c, c ^ 1) for c in range(cores)])

    borders = [(p, p + 1) for p in range(1, parts - 1, 2)]
    borders += [(t, s) for s, t in borders]
    near = all(s ^ t == 3 for s, t in borders)

    first, own_0, rank, facing, turned = in_order(place, embeddings, cluster_of, target_pos, parts)
    got_first = swap(first, 1)
    got_facing = [swap(facing[k - 2], k) for k in range(2, parts)]
    over_0 = chip_swap(own_0)
    beside_0 = core_swap(own_0)

    *held, own_1, border = pack(
        [got_first, own_0],
        [[(0, 0, slots)], [(1, half, half), (0, half, half)]],
        held=turned,
    )
    got_turned = [swap(held[k - 2], k) for k in range(2, parts)]
    over_1 = chip_swap(own_1)
    beside_1 = core_swap(own_1)

    (own_2,) = pack(got_facing, [[(i, 0, half) for i in range(parts - 2)]])
    over_2 = chip_swap(own_2)
    beside_2 = core_swap(own_2)
    passed = swap(own_2, 1)

    (border,) = after([border], [over_2])
    got_border = between(border, borders)
    if near:
        got_more = between(held[0], [(t ^ 1, t) for _, t in borders])

    (own_3,) = pack(got_turned, [[(i, 0, half) for i in range(parts - 2)]])
    over_3 = chip_swap(own_3)
    beside_3 = core_swap(own_3)

    across_0, across_1, across_2, across_3 = (
        core_swap(over) for over in (over_0, over_1, over_2, over_3)
    )

    def early(*three):
        return [(b, 0, n) for b, n in zip(three, (slots, slots, rest))]

    mine = early(own_0, own_1, own_2) + [(own_3, 0, rest)]
    others = early(beside_0, beside_1, beside_2)
    others += early(over_0, over_1, over_2) + early(across_0, across_1, across_2)
    (own_a,) = meet(mine, mine + others, own=True)
    visit_u = [(got_first, slots, half), (passed, 0, rest), (first, 0, half)]
    visit_v = [(got_border, 0, slots)]
    if near:
        visit_v += [(got_more, 0, half), (turned[1], 0, half)]
    else:
        visit_v += [(between(own_3, borders), 0, rest)]
    quarter = early(own_0, own_1, own_2) + others
    before_u, u_before = meet(quarter, visit_u, visits=True)
    before_v, v_before = meet(quarter, visit_v, visits=True)
    late = [(b, 0, rest) for b in (own_3, beside_3, over_3, across_3)]
    (own_b,) = meet(mine, late[1:])
    last, visit_last = meet(late, visit_u + visit_v, visits=True)
    found = pl.pallas_call(
        functools.partial(route_kernel, parts, members, half, near),
        out_shape=jax.ShapeDtypeStruct((parts * members, 1, 2 * slots), jnp.float32),
        in_specs=[SCALARS] + [WHOLE] * 8,
        out_specs=WHOLE,
        compiler_params=grant(8),
        name="route",
    )(place, own_a, own_b, before_u, before_v, last, u_before, v_before, visit_last)
    got = lax.all_to_all(found, ("blk", "split"), split_axis=0, concat_axis=0, tiled=True)
    return in_data_order(got, rank, parts, members).reshape(rows)


def solution(mesh):
    spec = P(("groups", "blk", "split"))
    return jax.shard_map(
        body,
        mesh=mesh,
        in_specs=(P(("groups", "blk", "split"), None), spec, spec),
        out_specs=spec,
        check_vma=False,
    )
```

```python
import functools

import jax
import jax.numpy as jnp
from jax import lax
from jax.experimental import pallas as pl
from jax.experimental.pallas import tpu as pltpu
from jax.sharding import PartitionSpec as P

MOST = 4096
FILL = -4.0
TAGS = 8
LANES = 128
MIB = 1024 * 1024
WHOLE = pl.BlockSpec(memory_space=pltpu.VMEM)
ANYWHERE = pl.BlockSpec(memory_space=pl.ANY)
REMAINS = pl.BlockSpec(memory_space=pltpu.HBM)
SCALARS = pl.BlockSpec(memory_space=pltpu.SMEM)


def grant(mib):
    return pltpu.CompilerParams(vmem_limit_bytes=mib * MIB)


def spread(row):
    return jnp.transpose(jnp.broadcast_to(row, (LANES, row.shape[1])))


def column_fold(scores):
    rows, columns = scores.shape
    return jnp.max(scores.reshape(rows // 8, 8, columns), axis=0)


def lane_fold(scores):
    best = scores[:, :LANES]
    for at in range(LANES, scores.shape[1], LANES):
        best = jnp.maximum(best, scores[:, at : at + LANES])
    return best


def order_kernel(parts, place_ref, rows_hbm, ids_hbm, pos_hbm, *refs):
    outs, rank_ref = refs[:parts], refs[parts]
    unit, pick, placed, tags, rows_ref, ids_ref, pos_ref, sems = refs[parts + 1 :]
    count, width = rows_ref.shape
    quart = count // parts // 4
    step = 256
    fetch_pos = pltpu.make_async_copy(pos_hbm, pos_ref, sems.at[0])
    fetch_rows = pltpu.make_async_copy(rows_hbm, rows_ref, sems.at[1])
    fetch_ids = pltpu.make_async_copy(ids_hbm, ids_ref, sems.at[2])
    fetch_pos.start()
    fetch_rows.start()
    fetch_ids.start()
    fetch_pos.wait()
    pos = pos_ref[...].astype(jnp.float32)
    below = jnp.zeros((8, count), jnp.float32)
    for at in range(0, count, step):
        other = spread(pos[:, at : at + step])[:, :1]
        below += jnp.sum(jnp.where(other < pos, 1.0, 0.0).reshape(step // 8, 8, count), axis=0)
    rank = jnp.sum(below, axis=0, keepdims=True).astype(jnp.int32)
    rank_ref[...] = rank
    for at in range(0, count, step):
        slot = lax.broadcasted_iota(jnp.int32, (step, count), 0) + at
        pick[at : at + step, :] = jnp.where(slot == rank, 1.0, 0.0).astype(jnp.bfloat16)
    fetch_rows.wait()
    fetch_ids.wait()
    values = rows_ref[...].astype(jnp.float32)
    total = jnp.sum(values * values, axis=1, keepdims=True)
    unit[...] = (values * lax.rsqrt(total + 1e-06)).astype(jnp.bfloat16)
    for at in range(0, count, step):
        placed[at : at + step, :] = jnp.dot(
            pick[at : at + step, :], unit[...], preferred_element_type=jnp.float32
        ).astype(jnp.bfloat16)
    ids = jnp.broadcast_to((ids_ref[...] + 1).astype(jnp.bfloat16), (16, count))
    sorted_ids = lax.dot_general(
        ids, pick[...], (((1,), (1,)), ((), ())), preferred_element_type=jnp.float32
    )
    for at in range(4 * parts):
        tags[at, :, :quart] = sorted_ids[:, at * quart : (at + 1) * quart]
    for k in range(parts):
        quarter = lax.bitwise_xor(place_ref[0], k)
        side = lax.rem(quarter, 2)
        for index, block in enumerate((3 - 3 * side, 2 - side, 3 * side, 1 + side)):
            which = 4 * quarter + block
            at = index * quart
            outs[k][at : at + quart, :] = placed[pl.ds(pl.multiple_of(which * quart, quart), quart), :]
            outs[k][4 * quart :, at : at + quart] = tags[which, :TAGS, :quart].astype(jnp.bfloat16)


def in_order(place, embeddings, ids, pos, parts):
    count, width = embeddings.shape
    slots = count // parts
    block = jax.ShapeDtypeStruct((slots + TAGS, width), jnp.bfloat16)
    outs = [block] * parts + [jax.ShapeDtypeStruct((1, count), jnp.int32)]
    *blocks, rank = pl.pallas_call(
        functools.partial(order_kernel, parts),
        out_shape=outs,
        in_specs=[SCALARS, REMAINS, REMAINS, REMAINS],
        out_specs=[WHOLE] * len(outs),
        scratch_shapes=[
            pltpu.VMEM((count, width), jnp.bfloat16),
            pltpu.VMEM((count, count), jnp.bfloat16),
            pltpu.VMEM((count, width), jnp.bfloat16),
            pltpu.VMEM((4 * parts, 16, max(slots // 4, LANES)), jnp.float32),
            pltpu.VMEM((count, width), jnp.bfloat16),
            pltpu.VMEM((1, count), jnp.int32),
            pltpu.VMEM((1, count), jnp.int32),
            pltpu.SemaphoreType.DMA((3,)),
        ],
        compiler_params=grant(24),
        name="order",
    )(place, embeddings, ids.reshape(1, count), pos.reshape(1, count))
    return blocks, rank


def pack_kernel(plan, inputs, *refs):
    given, outs = refs[:inputs], refs[-len(plan) :]
    for out, pieces in zip(outs, plan):
        at = 0
        for index, start, rows in pieces:
            ref = given[index]
            out[at : at + rows, :] = ref[start : start + rows, :]
            out[out.shape[0] - TAGS :, at : at + rows] = ref[
                ref.shape[0] - TAGS :, start : start + rows
            ]
            at += rows


def pack(blocks, plan, held=(), earlier=()):
    width = blocks[0].shape[1]
    plan = [list(pieces) for pieces in plan]
    outs = [
        jax.ShapeDtypeStruct((sum(p[2] for p in pieces) + TAGS, width), jnp.bfloat16)
        for pieces in plan
    ]
    kept = [jax.ShapeDtypeStruct(h.shape, h.dtype) for h in held]

    def kernel(*refs):
        given = refs[: len(blocks)]
        made = refs[len(blocks) + 2 * len(held) + len(earlier) :]
        pack_kernel(plan, len(given), *given, *made)

    return pl.pallas_call(
        kernel,
        out_shape=kept + outs,
        in_specs=[WHOLE] * len(blocks) + [ANYWHERE] * (len(held) + len(earlier)),
        out_specs=[ANYWHERE] * len(held) + [WHOLE] * len(outs),
        input_output_aliases={len(blocks) + i: i for i in range(len(held))},
        compiler_params=grant(8),
        name="pack",
    )(*blocks, *held, *earlier)


def after(held, earlier):
    return pl.pallas_call(
        lambda *refs: None,
        out_shape=[jax.ShapeDtypeStruct(h.shape, h.dtype) for h in held],
        in_specs=[ANYWHERE] * (len(held) + len(earlier)),
        out_specs=[ANYWHERE] * len(held),
        input_output_aliases={i: i for i in range(len(held))},
        compiler_params=grant(1),
        name="after",
    )(*held, *earlier)


def overlap(one, other):
    return jnp.logical_and(one[0] <= other[1], other[0] <= one[1])


def meet_kernel(lefts, rights, pairs, inputs, *refs):
    given = refs[:inputs]
    left_out, right_out, left, left_ids, right, right_ids, left_best, right_best = refs[inputs:]

    def ids_of(piece):
        ref, start, rows = given[piece[0]], piece[1], piece[2]
        return ref[ref.shape[0] - TAGS :, start : start + rows].astype(jnp.float32)

    def span(section):
        low, high = None, None
        for piece in section:
            ids = ids_of(piece)
            there = jnp.where(ids > 0.0, ids, 1e6)
            low = there if low is None else jnp.minimum(low, there)
            high = ids if high is None else jnp.maximum(high, ids)
        return jnp.min(low), jnp.max(high)

    tested = [(r, l) for r, l, _, test in pairs if test]
    right_span = {r: span(rights[r]) for r in sorted({r for r, _ in tested})}
    left_span = {l: span(lefts[l]) for l in sorted({l for _, l in tested})}
    wanted = {(r, l): overlap(right_span[r], left_span[l]) for r, l in tested}

    def place_of(sections):
        out, at = [], 0
        for section in sections:
            rows = sum(piece[2] for piece in section)
            out.append((at, rows))
            at += rows
        return out

    left_at, right_at = place_of(lefts), place_of(rights)

    def fill(buffer, section, at):
        for index, start, rows in section:
            buffer[at : at + rows, :] = given[index][start : start + rows, :]
            at += rows

    left_best[...] = jnp.full(left_best.shape, FILL, jnp.float32)
    right_best[...] = jnp.full(right_best.shape, FILL, jnp.float32)
    for section, (at, _) in zip(lefts, left_at):
        for piece in section:
            left_ids[:, at : at + piece[2]] = ids_of(piece)
            at += piece[2]
    for section, (at, _) in zip(rights, right_at):
        for piece in section:
            right_ids[at : at + piece[2], :] = spread(ids_of(piece)[:1, :])
            at += piece[2]
    for which, sections, places, buffer in ((1, lefts, left_at, left), (0, rights, right_at, right)):
        for number, section in enumerate(sections):
            uses = [p for p in pairs if p[which] == number]
            load = functools.partial(fill, buffer, section, places[number][0])
            if all(p[3] for p in uses):
                need = [wanted[p[0], p[1]] for p in uses]
                pl.when(functools.reduce(jnp.logical_or, need))(load)
            else:
                load()

    def score(r, l, diagonal):
        (row, rows), (column, columns) = right_at[r], left_at[l]
        step = rows
        while step * columns > 512 * 1024 and step % 32 == 0:
            step //= 2
        across = slice(column, column + columns)

        def turn(index, _):
            at = pl.multiple_of(row + index * step, 16)
            down = pl.ds(at, step)
            scores = lax.dot_general(
                right[down, :],
                left[across, :],
                (((1,), (1,)), ((), ())),
                preferred_element_type=jnp.float32,
            )
            scores = jnp.where(right_ids[down, :1] == left_ids[:1, across], scores, FILL)
            if diagonal:
                mine = lax.broadcasted_iota(jnp.int32, (step, columns), 0) + index * step
                theirs = lax.broadcasted_iota(jnp.int32, (step, columns), 1)
                scores = jnp.where(mine == theirs, FILL, scores)
            right_best[down, :] = jnp.maximum(right_best[down, :], lane_fold(scores))
            left_best[:, across] = jnp.maximum(left_best[:, across], column_fold(scores))
            return 0

        lax.fori_loop(0, rows // step, turn, 0)

    for r, l, diagonal, test in pairs:
        run = functools.partial(score, r, l, diagonal)
        if test:
            pl.when(wanted[r, l])(run)
        else:
            run()
    left_out[...] = jnp.max(left_best[...], axis=0, keepdims=True)
    right_out[...] = jnp.max(jnp.transpose(right_best[...]), axis=0, keepdims=True)


def meet(lefts, rights, pairs, earlier=()):
    blocks = []

    def plan(sections):
        out = []
        for section in sections:
            pieces = []
            for block, start, rows, _ in section:
                known = [i for i, b in enumerate(blocks) if b is block]
                if not known:
                    blocks.append(block)
                pieces.append((known[0] if known else len(blocks) - 1, start, rows))
            out.append(pieces)
        return out

    def goals(sections):
        return [(p[3], p[2]) for section in sections for p in section]

    plan_left, plan_right = plan(lefts), plan(rights)
    width = blocks[0].shape[1]
    count = sum(n for _, n in goals(lefts))
    total = sum(n for _, n in goals(rights))
    inputs = len(blocks)

    def kernel(*refs):
        meet_kernel(
            plan_left, plan_right, pairs, inputs, *refs[:inputs], *refs[inputs + len(earlier) :]
        )

    left_best, right_best = pl.pallas_call(
        kernel,
        out_shape=[
            jax.ShapeDtypeStruct((1, count), jnp.float32),
            jax.ShapeDtypeStruct((1, total), jnp.float32),
        ],
        in_specs=[WHOLE] * inputs + [ANYWHERE] * len(earlier),
        out_specs=[WHOLE] * 2,
        scratch_shapes=[
            pltpu.VMEM((count, width), jnp.bfloat16),
            pltpu.VMEM((TAGS, count), jnp.float32),
            pltpu.VMEM((total, width), jnp.bfloat16),
            pltpu.VMEM((total, LANES), jnp.float32),
            pltpu.VMEM((8, count), jnp.float32),
            pltpu.VMEM((total, LANES), jnp.float32),
        ],
        compiler_params=grant(24),
        cost_estimate=pl.CostEstimate(flops=0, bytes_accessed=0, transcendentals=0),
        name="meet",
    )(*blocks, *earlier)
    return [(left_best, goals(lefts)), (right_best, goals(rights))]


def route_kernel(plan, parts, members, half, near, place_ref, *refs):
    given, out_ref, gathered = refs[:-2], refs[-2], refs[-1]
    part, me = place_ref[0], place_ref[1]
    slots = 2 * half
    out_ref[...] = jnp.full(out_ref.shape, FILL, jnp.float32)
    gathered[...] = jnp.full(gathered.shape, FILL, jnp.float32)
    starts = {"u": members * parts * slots, "v": members * parts * slots + parts * half}
    for ref, pieces in zip(given, plan):
        at = 0
        for to, entries in pieces:
            gathered[:, to : to + entries] = jnp.maximum(
                gathered[:, to : to + entries], ref[:, at : at + entries]
            )
            at += entries
    for member in range(members):
        whose = lax.bitwise_xor(me, member)
        for k in range(parts):
            at = (member * parts + k) * slots
            source = lax.bitwise_xor(part, k) * members + whose
            out_ref[source, :, :slots] = gathered[:, at : at + slots]
    beyond = lax.rem(part + parts - 1 + 2 * lax.rem(part, 2), parts)
    if near:
        beyond = lax.bitwise_xor(part, 3)
    next_to = lax.bitwise_xor(part, 1)
    from_u = [next_to] + [lax.bitwise_xor(next_to, k) for k in range(2, parts)] + [part]
    from_v = [beyond, lax.bitwise_xor(beyond, 1)]
    from_v += [next_to, part] if near else [lax.bitwise_xor(beyond, k) for k in range(2, parts)]
    for kind, sources, lane in (("u", from_u, slots), ("v", from_v, slots + half)):
        for index, source in enumerate(sources):
            at = starts[kind] + index * half
            out_ref[source * members + me, :, lane : lane + half] = gathered[:, at : at + half]


def back_kernel(parts, members, got_ref, rank_ref, out_ref):
    slots = got_ref.shape[2] // 2
    half = slots // 2
    rows = []
    for part in range(parts):
        best = got_ref[part * members]
        for member in range(1, members):
            best = jnp.maximum(best, got_ref[part * members + member])
        rows.append(best)
    rank = rank_ref[...]
    nothing = jnp.full((1, half), FILL, jnp.float32)
    best = jnp.full((8, rank.shape[1]), FILL, jnp.float32)
    for part in range(parts):
        beyond = part + 1 if part % 2 else part - 1
        there = 0 <= beyond < parts
        faces = jnp.maximum(rows[part][:, :half], rows[part ^ 1][:, slots : slots + half])
        turned = jnp.maximum(
            rows[part][:, half:slots], rows[beyond][:, slots + half :] if there else nothing
        )
        near_u, far_u = faces[:, : half // 2], faces[:, half // 2 :]
        near_v, far_v = turned[:, : half // 2], turned[:, half // 2 :]
        order = [near_u, far_u, far_v, near_v] if part % 2 else [near_v, far_v, far_u, near_u]
        values = spread(jnp.concatenate(order, axis=1))[:, :1]
        slot = lax.broadcasted_iota(jnp.int32, (slots, rank.shape[1]), 0) + part * slots
        best = jnp.maximum(best, column_fold(jnp.where(slot == rank, values, FILL)))
    out_ref[...] = jnp.max(best, axis=0, keepdims=True)


def in_data_order(got, rank, parts, members):
    return pl.pallas_call(
        functools.partial(back_kernel, parts, members),
        out_shape=jax.ShapeDtypeStruct(rank.shape, jnp.float32),
        in_specs=[WHOLE, WHOLE],
        out_specs=WHOLE,
        compiler_params=grant(16),
        name="back",
    )(got, rank)


def body(embeddings, cluster_of, target_pos):
    blocks, cores = lax.axis_size("blk"), lax.axis_size("split")
    rows, width = embeddings.shape
    members = MOST // rows
    chips = members // cores
    parts = blocks // chips
    half = rows // parts // 2
    slots = 2 * half
    chip, core = lax.axis_index("blk"), lax.axis_index("split")
    place = jnp.stack([chip // chips, (chip % chips) * cores + core]).astype(jnp.int32)

    def between(array, pairs, name):
        route = [(s * chips + c, t * chips + c) for s, t in pairs for c in range(chips)]
        with jax.named_scope(name):
            return lax.ppermute(array, "blk", route)

    def swap(array, k, name):
        return between(array, [(part, part ^ k) for part in range(parts)], name)

    def chip_swap(array, name):
        with jax.named_scope(name):
            return lax.ppermute(array, "blk", [(b, b ^ 1) for b in range(blocks)])

    def core_swap(array, name):
        with jax.named_scope(name):
            return lax.ppermute(array, "split", [(c, c ^ 1) for c in range(cores)])

    borders = [(p, p + 1) for p in range(1, parts - 1, 2)]
    borders += [(t, s) for s, t in borders]
    near = all(s ^ t == 3 for s, t in borders)

    quart = half // 2
    middle = (parts + 2) // 2
    second, third = [1, *range(2, middle)], list(range(middle, parts))
    u_goal = members * parts * slots
    v_goal = u_goal + parts * half

    def sides(blocks, ks, member=0):
        out = []
        for side in (0, half):
            for m, block in enumerate(blocks, member):
                for i, k in enumerate(ks):
                    goal = (m * parts + k) * slots + side
                    out.append((block, i * slots + side, half, goal))
        return out[: len(out) // 2], out[len(out) // 2 :]

    def visits(pieces, goal):
        near_rows = [(b, at, quart, goal + i * half) for b, at, i in pieces]
        far_rows = [(b, at + quart, quart, goal + i * half + quart) for b, at, i in pieces]
        return near_rows, far_rows

    sent, rank = in_order(place, embeddings, cluster_of, target_pos, parts)
    own_0 = sent[0]
    got = [swap(sent[k], k, "rows_2") for k in second]
    over_0 = chip_swap(own_0, "over_0")
    beside_0 = core_swap(own_0, "beside_0")

    pieces = [(i, 0, slots) for i in range(len(second))]
    forward = [(len(second), 0, half)] + [(i, 0, half) for i in range(1, len(second))]
    *held, own_2, passing = pack(
        [*got, own_0], [pieces, forward], held=[sent[k] for k in third], earlier=[over_0]
    )
    got = [swap(b, k, "rows_3") for k, b in zip(third, held)]
    over_2 = chip_swap(own_2, "over_2")
    passed_2 = swap(passing, 1, "passed_2")
    across_0 = core_swap(over_0, "across_0")
    beside_2 = core_swap(own_2, "beside_2")
    left_0 = sides([own_0, beside_0, over_0, across_0], [0])
    mine_0, mine_2 = sides([own_0], [0]), sides([own_2], second)
    scores = meet(
        left_0,
        [*mine_0, *mine_2],
        [(0, 0, True, False), (0, 1, False, True), (1, 0, False, True), (1, 1, True, False)]
        + [(2, 0, False, False), (2, 1, False, True), (3, 0, False, True), (3, 1, False, False)],
    )

    last = len(third)
    border = [(last, half, half), (last + 1, half, half)]
    forward = [(i, 0, half) for i in range(last)]
    inputs = [*got, own_0, own_2]
    if near:
        inputs.append(sent[2])
        forward.append((last + 2, half, half))
    else:
        border += [(last + 1, i * slots + half, half) for i in range(1, len(second))]
        border += [(i, half, half) for i in range(last)]
    own_3, border, passing = pack(
        inputs,
        [[(i, 0, slots) for i in range(last)], border, forward],
        earlier=[over_2, passed_2, across_0, beside_2, scores[0][0]],
    )
    over_3 = chip_swap(own_3, "over_3")
    got_border = between(border, borders, "border")
    passed_3 = swap(passing, 1, "passed_3")
    across_2 = core_swap(over_2, "across_2")
    beside_3 = core_swap(own_3, "beside_3")
    left_2 = sides([own_2, beside_2, over_2, across_2], second)
    mine_3 = sides([own_3], third)
    visit_2 = [(passed_2, i * half, i) for i in range(len(second))]
    visit_2 = visits(visit_2 + [(sent[1], 0, parts - 1)], u_goal)
    visit_3 = visits([(passed_3, i * half, len(second) + i) for i in range(last)], u_goal)
    tested = [(r, l, False, True) for r in (4, 5) for l in (0, 1)]
    scores += meet(
        left_2,
        [*mine_2, *mine_3, *visit_2],
        [(0, 0, True, False), (0, 1, False, True), (1, 0, False, True), (1, 1, True, False)]
        + [(2, 0, False, False), (2, 1, False, True), (3, 0, False, True), (3, 1, False, False)]
        + tested,
    )
    scores += meet(
        left_0,
        [*mine_3, *visit_2],
        [(0, 0, False, False), (0, 1, False, True), (1, 0, False, True), (1, 1, False, False)]
        + [(r, l, False, True) for r in (2, 3) for l in (0, 1)],
    )

    visit_v = [(got_border, i * half, i) for i in range(got_border.shape[0] // half)]
    if near:
        visit_v += [(passed_3, last * half, 2), (sent[3], half, 3)]
    visit_v = visits(visit_v, v_goal)
    both = [left_0[0] + left_2[0], left_0[1] + left_2[1]]
    scores += meet(
        both, [*visit_3, *visit_v], [(r, l, False, True) for r in range(4) for l in (0, 1)]
    )
    (over_3,) = after([over_3], [best for best, _ in scores[2:6:2]])
    across_3 = core_swap(over_3, "across_3")
    left_3 = sides([own_3, beside_3, over_3, across_3], third)
    visit_u = [visit_2[0] + visit_3[0], visit_2[1] + visit_3[1]]
    scores += meet(
        left_3,
        [*mine_3, *visit_u, *visit_v],
        [(0, 0, True, False), (0, 1, False, True), (1, 0, False, True), (1, 1, True, False)]
        + [(r, l, False, True) for r in range(2, 6) for l in (0, 1)],
    )
    found = pl.pallas_call(
        functools.partial(
            route_kernel, [goals for _, goals in scores], parts, members, half, near
        ),
        out_shape=jax.ShapeDtypeStruct((parts * members, 1, 2 * slots), jnp.float32),
        in_specs=[SCALARS] + [WHOLE] * len(scores),
        out_specs=WHOLE,
        scratch_shapes=[pltpu.VMEM((1, v_goal + parts * half), jnp.float32)],
        compiler_params=grant(8),
        name="route",
    )(place, *[best for best, _ in scores])
    got = lax.all_to_all(found, ("blk", "split"), split_axis=0, concat_axis=0, tiled=True)
    return in_data_order(got, rank, parts, members).reshape(rows)


def solution(mesh):
    spec = P(("groups", "blk", "split"))
    return jax.shard_map(
        body,
        mesh=mesh,
        in_specs=(P(("groups", "blk", "split"), None), spec, spec),
        out_specs=spec,
        check_vma=False,
    )
```

```python
import functools

import jax
import jax.numpy as jnp
from jax import lax
from jax.experimental import pallas as pl
from jax.experimental.pallas import tpu as pltpu
from jax.sharding import PartitionSpec as P

MOST = 4096
FILL = -4.0
TAGS = 8
LANES = 128
MIB = 1024 * 1024
WHOLE = pl.BlockSpec(memory_space=pltpu.VMEM)
ANYWHERE = pl.BlockSpec(memory_space=pl.ANY)
REMAINS = pl.BlockSpec(memory_space=pltpu.HBM)


def grant(mib):
    return pltpu.CompilerParams(vmem_limit_bytes=mib * MIB)


def spread(row):
    return jnp.transpose(jnp.broadcast_to(row, (LANES, row.shape[1])))


def column_fold(scores):
    rows, columns = scores.shape
    return jnp.max(scores.reshape(rows // 8, 8, columns), axis=0)


def lane_fold(scores):
    best = scores[:, :LANES]
    for at in range(LANES, scores.shape[1], LANES):
        best = jnp.maximum(best, scores[:, at : at + LANES])
    return best


def order_kernel(parts, chips, rows_hbm, marks_hbm, *refs):
    outs, rank_ref = refs[:parts], refs[parts]
    unit, pick, placed, tags, rows_ref, marks_ref, sems = refs[parts + 1 :]
    count, width = rows_ref.shape
    quart = count // parts // 4
    step = 256
    fetch_marks = pltpu.make_async_copy(marks_hbm, marks_ref, sems.at[0])
    fetch_rows = pltpu.make_async_copy(rows_hbm, rows_ref, sems.at[1])
    fetch_marks.start()
    fetch_rows.start()
    fetch_marks.wait()
    pos = marks_ref[1:2, :].astype(jnp.float32)
    below = jnp.zeros((8, count), jnp.float32)
    for at in range(0, count, step):
        other = spread(pos[:, at : at + step])[:, :1]
        below += jnp.sum(jnp.where(other < pos, 1.0, 0.0).reshape(step // 8, 8, count), axis=0)
    rank = jnp.sum(below, axis=0, keepdims=True).astype(jnp.int32)
    rank_ref[...] = rank
    for at in range(0, count, step):
        slot = lax.broadcasted_iota(jnp.int32, (step, count), 0) + at
        pick[at : at + step, :] = jnp.where(slot == rank, 1.0, 0.0).astype(jnp.bfloat16)
    fetch_rows.wait()
    values = rows_ref[...].astype(jnp.float32)
    total = jnp.sum(values * values, axis=1, keepdims=True)
    unit[...] = (values * lax.rsqrt(total + 1e-06)).astype(jnp.bfloat16)
    for at in range(0, count, step):
        placed[at : at + step, :] = jnp.dot(
            pick[at : at + step, :], unit[...], preferred_element_type=jnp.float32
        ).astype(jnp.bfloat16)
    ids = jnp.broadcast_to((marks_ref[:1, :] + 1).astype(jnp.bfloat16), (16, count))
    part = lax.axis_index("blk") // chips
    sorted_ids = lax.dot_general(
        ids, pick[...], (((1,), (1,)), ((), ())), preferred_element_type=jnp.float32
    )
    for at in range(4 * parts):
        tags[at, :, :quart] = sorted_ids[:, at * quart : (at + 1) * quart]
    for k in range(parts):
        quarter = lax.bitwise_xor(part, k)
        side = lax.rem(quarter, 2)
        for index, block in enumerate((3 - 3 * side, 2 - side, 3 * side, 1 + side)):
            which = 4 * quarter + block
            at = index * quart
            outs[k][at : at + quart, :] = placed[pl.ds(pl.multiple_of(which * quart, quart), quart), :]
            outs[k][4 * quart :, at : at + quart] = tags[which, :TAGS, :quart].astype(jnp.bfloat16)


def in_order(embeddings, ids, pos, parts, chips):
    count, width = embeddings.shape
    slots = count // parts
    block = jax.ShapeDtypeStruct((slots + TAGS, width), jnp.bfloat16)
    outs = [block] * parts + [jax.ShapeDtypeStruct((1, count), jnp.int32)]
    *blocks, rank = pl.pallas_call(
        functools.partial(order_kernel, parts, chips),
        out_shape=outs,
        in_specs=[REMAINS, REMAINS],
        out_specs=[WHOLE] * len(outs),
        scratch_shapes=[
            pltpu.VMEM((count, width), jnp.bfloat16),
            pltpu.VMEM((count, count), jnp.bfloat16),
            pltpu.VMEM((count, width), jnp.bfloat16),
            pltpu.VMEM((4 * parts, 16, max(slots // 4, LANES)), jnp.float32),
            pltpu.VMEM((count, width), jnp.bfloat16),
            pltpu.VMEM((2, count), jnp.int32),
            pltpu.SemaphoreType.DMA((2,)),
        ],
        compiler_params=grant(24),
        name="order",
    )(embeddings, jnp.stack([ids, pos]))
    return blocks, rank


def pack_kernel(plan, inputs, *refs):
    given, outs = refs[:inputs], refs[-len(plan) :]
    for out, pieces in zip(outs, plan):
        at = 0
        for index, start, rows in pieces:
            ref = given[index]
            out[at : at + rows, :] = ref[start : start + rows, :]
            out[out.shape[0] - TAGS :, at : at + rows] = ref[
                ref.shape[0] - TAGS :, start : start + rows
            ]
            at += rows


def pack(blocks, plan, held=(), earlier=()):
    width = blocks[0].shape[1]
    plan = [list(pieces) for pieces in plan]
    outs = [
        jax.ShapeDtypeStruct((sum(p[2] for p in pieces) + TAGS, width), jnp.bfloat16)
        for pieces in plan
    ]
    kept = [jax.ShapeDtypeStruct(h.shape, h.dtype) for h in held]

    def kernel(*refs):
        given = refs[: len(blocks)]
        made = refs[len(blocks) + 2 * len(held) + len(earlier) :]
        pack_kernel(plan, len(given), *given, *made)

    return pl.pallas_call(
        kernel,
        out_shape=kept + outs,
        in_specs=[WHOLE] * len(blocks) + [ANYWHERE] * (len(held) + len(earlier)),
        out_specs=[ANYWHERE] * len(held) + [WHOLE] * len(outs),
        input_output_aliases={len(blocks) + i: i for i in range(len(held))},
        compiler_params=grant(8),
        name="pack",
    )(*blocks, *held, *earlier)


def after(held, earlier):
    return pl.pallas_call(
        lambda *refs: None,
        out_shape=[jax.ShapeDtypeStruct(h.shape, h.dtype) for h in held],
        in_specs=[ANYWHERE] * (len(held) + len(earlier)),
        out_specs=[ANYWHERE] * len(held),
        input_output_aliases={i: i for i in range(len(held))},
        compiler_params=grant(1),
        name="after",
    )(*held, *earlier)


def padded(section):
    rows = sum(piece[2] for piece in section)
    return -(-rows // LANES) * LANES


def overlap(one, other):
    return jnp.logical_and(one[0] <= other[1], other[0] <= one[1])


def meet_kernel(lefts, rights, pairs, inputs, *refs):
    given = refs[:inputs]
    left_out, right_out, left, left_ids, right, right_ids, left_best, right_best = refs[inputs:]

    def ids_of(piece):
        ref, start, rows = given[piece[0]], piece[1], piece[2]
        return ref[ref.shape[0] - TAGS :, start : start + rows].astype(jnp.float32)

    def span(section):
        low, high = None, None
        for piece in section:
            ids = ids_of(piece)
            there = jnp.where(ids > 0.0, ids, 1e6)
            low = there if low is None else jnp.minimum(low, there)
            high = ids if high is None else jnp.maximum(high, ids)
        return jnp.min(low), jnp.max(high)

    tested = [(r, l) for r, l, _, test in pairs if test]
    right_span = {r: span(rights[r]) for r in sorted({r for r, _ in tested})}
    left_span = {l: span(sum((lefts[i] for i in l), [])) for l in sorted({l for _, l in tested})}
    wanted = {(r, l): overlap(right_span[r], left_span[l]) for r, l in tested}

    def place_of(sections):
        out, at = [], 0
        for section in sections:
            rows = padded(section)
            out.append((at, rows))
            at += rows
        return out

    left_at, right_at = place_of(lefts), place_of(rights)

    def fill_left(number):
        at = left_at[number][0]
        for piece in lefts[number]:
            index, start, rows = piece
            left[at : at + rows, :] = given[index][start : start + rows, :]
            left_ids[at : at + rows, :TAGS] = jnp.transpose(ids_of(piece))
            at += rows

    def fill_right(number):
        at = right_at[number][0]
        for piece in rights[number]:
            index, start, rows = piece
            right[at : at + rows, :] = given[index][start : start + rows, :]
            right_ids[:, at : at + rows] = ids_of(piece)
            at += rows

    left_best[...] = jnp.full(left_best.shape, FILL, jnp.float32)
    right_best[...] = jnp.full(right_best.shape, FILL, jnp.float32)
    right_ids[...] = jnp.full(right_ids.shape, -1.0, jnp.float32)
    for which, sections, fill in ((1, lefts, fill_left), (0, rights, fill_right)):
        for number in range(len(sections)):
            uses = [p for p in pairs if (number in p[1] if which else number == p[0])]
            load = functools.partial(fill, number)
            if all(p[3] for p in uses):
                need = [wanted[p[0], p[1]] for p in uses]
                pl.when(functools.reduce(jnp.logical_or, need))(load)
            else:
                load()

    def score(r, l, same):
        (lane, lanes), row = right_at[r], left_at[l[0]][0]
        rows = sum(left_at[i][1] for i in l)
        step = rows
        while step * lanes > 512 * 1024 and step % 32 == 0:
            step //= 2
        across = slice(lane, lane + lanes)

        def turn(index, _):
            at = pl.multiple_of(row + index * step, 16)
            down = pl.ds(at, step)
            scores = lax.dot_general(
                left[down, :],
                right[across, :],
                (((1,), (1,)), ((), ())),
                preferred_element_type=jnp.float32,
            )
            scores = jnp.where(left_ids[down, :1] == right_ids[:1, across], scores, FILL)
            if same is not None:
                first, count = same
                theirs = lax.broadcasted_iota(jnp.int32, (step, lanes), 0) + index * step
                mine = lax.broadcasted_iota(jnp.int32, (step, lanes), 1)
                itself = jnp.logical_and(theirs + first == mine, theirs < count)
                scores = jnp.where(itself, FILL, scores)
            left_best[down, :] = jnp.maximum(left_best[down, :], lane_fold(scores))
            right_best[:, across] = jnp.maximum(right_best[:, across], column_fold(scores))
            return 0

        lax.fori_loop(0, rows // step, turn, 0)

    for r, l, same, test in pairs:
        run = functools.partial(score, r, l, same)
        if test:
            pl.when(wanted[r, l])(run)
        else:
            run()
    right_out[...] = jnp.max(right_best[...], axis=0, keepdims=True)
    left_out[...] = jnp.max(jnp.transpose(left_best[...]), axis=0, keepdims=True)


def meet(lefts, rights, pairs, earlier=()):
    blocks = []

    def plan(sections):
        out = []
        for section in sections:
            pieces = []
            for block, start, rows, _ in section:
                known = [i for i, b in enumerate(blocks) if b is block]
                if not known:
                    blocks.append(block)
                pieces.append((known[0] if known else len(blocks) - 1, start, rows))
            out.append(pieces)
        return out

    def goals(sections):
        out = []
        for section in sections:
            out += [(p[3], p[2]) for p in section]
            out.append((None, padded(section) - sum(p[2] for p in section)))
        return out

    plan_left, plan_right = plan(lefts), plan(rights)
    width = blocks[0].shape[1]
    count = sum(n for _, n in goals(lefts))
    total = sum(n for _, n in goals(rights))
    inputs = len(blocks)

    def kernel(*refs):
        meet_kernel(
            plan_left, plan_right, pairs, inputs, *refs[:inputs], *refs[inputs + len(earlier) :]
        )

    left_best, right_best = pl.pallas_call(
        kernel,
        out_shape=[
            jax.ShapeDtypeStruct((1, count), jnp.float32),
            jax.ShapeDtypeStruct((1, total), jnp.float32),
        ],
        in_specs=[WHOLE] * inputs + [ANYWHERE] * len(earlier),
        out_specs=[WHOLE] * 2,
        scratch_shapes=[
            pltpu.VMEM((count, width), jnp.bfloat16),
            pltpu.VMEM((count, LANES), jnp.float32),
            pltpu.VMEM((total, width), jnp.bfloat16),
            pltpu.VMEM((TAGS, total), jnp.float32),
            pltpu.VMEM((count, LANES), jnp.float32),
            pltpu.VMEM((8, total), jnp.float32),
        ],
        compiler_params=grant(28),
        cost_estimate=pl.CostEstimate(flops=0, bytes_accessed=0, transcendentals=0),
        name="meet",
    )(*blocks, *earlier)
    return [(left_best, goals(lefts)), (right_best, goals(rights))]


def route_kernel(plan, parts, chips, cores, half, near, *refs):
    given, out_ref, gathered = refs[:-2], refs[-2], refs[-1]
    chip, members = lax.axis_index("blk"), chips * cores
    part, me = chip // chips, lax.rem(chip, chips) * cores + lax.axis_index("split")
    slots = 2 * half
    out_ref[...] = jnp.full(out_ref.shape, FILL, jnp.float32)
    gathered[...] = jnp.full(gathered.shape, FILL, jnp.float32)
    starts = {"u": members * parts * slots, "v": members * parts * slots + parts * half}
    for ref, pieces in zip(given, plan):
        at = 0
        for to, entries in pieces:
            if to is not None:
                gathered[:, to : to + entries] = jnp.maximum(
                    gathered[:, to : to + entries], ref[:, at : at + entries]
                )
            at += entries
    for member in range(members):
        whose = lax.bitwise_xor(me, member)
        for k in range(parts):
            at = (member * parts + k) * slots
            source = lax.bitwise_xor(part, k) * members + whose
            out_ref[source, :, :slots] = gathered[:, at : at + slots]
    beyond = lax.rem(part + parts - 1 + 2 * lax.rem(part, 2), parts)
    if near:
        beyond = lax.bitwise_xor(part, 3)
    next_to = lax.bitwise_xor(part, 1)
    from_u = [next_to] + [lax.bitwise_xor(next_to, k) for k in range(2, parts)] + [part]
    from_v = [beyond, lax.bitwise_xor(beyond, 1)]
    from_v += [next_to, part] if near else [lax.bitwise_xor(beyond, k) for k in range(2, parts)]
    for kind, sources, lane in (("u", from_u, slots), ("v", from_v, slots + half)):
        for index, source in enumerate(sources):
            at = starts[kind] + index * half
            out_ref[source * members + me, :, lane : lane + half] = gathered[:, at : at + half]


def back_kernel(parts, members, got_ref, rank_ref, out_ref):
    slots = got_ref.shape[2] // 2
    half = slots // 2
    rows = []
    for part in range(parts):
        best = got_ref[part * members]
        for member in range(1, members):
            best = jnp.maximum(best, got_ref[part * members + member])
        rows.append(best)
    rank = rank_ref[...]
    nothing = jnp.full((1, half), FILL, jnp.float32)
    best = jnp.full((8, rank.shape[1]), FILL, jnp.float32)
    for part in range(parts):
        beyond = part + 1 if part % 2 else part - 1
        there = 0 <= beyond < parts
        faces = jnp.maximum(rows[part][:, :half], rows[part ^ 1][:, slots : slots + half])
        turned = jnp.maximum(
            rows[part][:, half:slots], rows[beyond][:, slots + half :] if there else nothing
        )
        near_u, far_u = faces[:, : half // 2], faces[:, half // 2 :]
        near_v, far_v = turned[:, : half // 2], turned[:, half // 2 :]
        order = [near_u, far_u, far_v, near_v] if part % 2 else [near_v, far_v, far_u, near_u]
        values = spread(jnp.concatenate(order, axis=1))[:, :1]
        slot = lax.broadcasted_iota(jnp.int32, (slots, rank.shape[1]), 0) + part * slots
        best = jnp.maximum(best, column_fold(jnp.where(slot == rank, values, FILL)))
    out_ref[...] = jnp.max(best, axis=0, keepdims=True)


def in_data_order(got, rank, parts, members):
    return pl.pallas_call(
        functools.partial(back_kernel, parts, members),
        out_shape=jax.ShapeDtypeStruct(rank.shape, jnp.float32),
        in_specs=[WHOLE, WHOLE],
        out_specs=WHOLE,
        compiler_params=grant(16),
        name="back",
    )(got, rank)


def body(embeddings, cluster_of, target_pos):
    blocks, cores = lax.axis_size("blk"), lax.axis_size("split")
    rows, width = embeddings.shape
    members = MOST // rows
    chips = members // cores
    parts = blocks // chips
    half = rows // parts // 2
    slots = 2 * half
    def between(array, pairs, name):
        route = [(s * chips + c, t * chips + c) for s, t in pairs for c in range(chips)]
        with jax.named_scope(name):
            return lax.ppermute(array, "blk", route)

    def swap(array, k, name):
        return between(array, [(part, part ^ k) for part in range(parts)], name)

    def chip_swap(array, name):
        with jax.named_scope(name):
            return lax.ppermute(array, "blk", [(b, b ^ 1) for b in range(blocks)])

    def core_swap(array, name):
        with jax.named_scope(name):
            return lax.ppermute(array, "split", [(c, c ^ 1) for c in range(cores)])

    borders = [(p, p + 1) for p in range(1, parts - 1, 2)]
    borders += [(t, s) for s, t in borders]
    near = all(s ^ t == 3 for s, t in borders)

    quart = half // 2
    middle = (parts + 2) // 2
    second, third = [1, *range(2, middle)], list(range(middle, parts))
    u_goal = members * parts * slots
    v_goal = u_goal + parts * half

    def sides(blocks, ks, member=0):
        out = []
        for side in (0, half):
            for m, block in enumerate(blocks, member):
                for i, k in enumerate(ks):
                    goal = (m * parts + k) * slots + side
                    out.append((block, i * slots + side, half, goal))
        return out[: len(out) // 2], out[len(out) // 2 :]

    def whole(block, ks):
        return [(block, i * slots, slots, k * slots) for i, k in enumerate(ks)]

    def visits(pieces, goal):
        near_rows = [(b, at, quart, goal + i * half) for b, at, i in pieces]
        far_rows = [(b, at + quart, quart, goal + i * half + quart) for b, at, i in pieces]
        return near_rows, far_rows

    sent, rank = in_order(embeddings, cluster_of, target_pos, parts, chips)
    own_0 = sent[0]
    got = [swap(sent[k], k, "rows_2") for k in second]
    over_0 = chip_swap(own_0, "over_0")
    beside_0 = core_swap(own_0, "beside_0")

    pieces = [(i, 0, slots) for i in range(len(second))]
    forward = [(len(second), 0, half)] + [(i, 0, half) for i in range(1, len(second))]
    *held, own_2, passing = pack(
        [*got, own_0], [pieces, forward], held=[sent[k] for k in third], earlier=[over_0]
    )
    got = [swap(b, k, "rows_3") for k, b in zip(third, held)]
    over_2 = chip_swap(own_2, "over_2")
    passed_2 = swap(passing, 1, "passed_2")
    across_0 = core_swap(over_0, "across_0")
    beside_2 = core_swap(own_2, "beside_2")
    left_0 = sides([own_0, beside_0, over_0, across_0], [0])
    here_2 = sides([own_2, beside_2], second)
    mine_0, mine_2 = whole(own_0, [0]), sum(sides([own_2], second), [])
    some = len(second) * half
    scores = meet(
        [*left_0, *here_2],
        [mine_0, mine_2],
        [(0, (0,), (0, half), False), (0, (1,), (half, half), False)]
        + [(1, (0, 1), None, False)]
        + [(1, (2,), (0, some), False), (1, (3,), (some, some), False)],
    )

    last = len(third)
    border = [(last, half, half), (last + 1, half, half)]
    forward = [(i, 0, half) for i in range(last)]
    inputs = [*got, own_0, own_2]
    if near:
        inputs.append(sent[2])
        forward.append((last + 2, half, half))
    else:
        border += [(last + 1, i * slots + half, half) for i in range(1, len(second))]
        border += [(i, half, half) for i in range(last)]
    own_3, border, passing = pack(
        inputs,
        [[(i, 0, slots) for i in range(last)], border, forward],
        earlier=[scores[0][0]],
    )
    over_3 = chip_swap(own_3, "over_3")
    got_border = between(border, borders, "border")
    passed_3 = swap(passing, 1, "passed_3")
    (over_2,) = after([over_2], [own_3, passed_2])
    across_2 = core_swap(over_2, "across_2")
    beside_3 = core_swap(own_3, "beside_3")
    there_2 = sides([over_2, across_2], second, 2)
    visit_2 = [(passed_2, i * half, i) for i in range(len(second))]
    visit_2 = visits(visit_2 + [(sent[1], 0, parts - 1)], u_goal)
    visit_3 = visits([(passed_3, i * half, len(second) + i) for i in range(last)], u_goal)
    mine_3 = sum(sides([own_3], third), [])
    lefts = [left_0[0], here_2[0], there_2[0], left_0[1], here_2[1], there_2[1]]
    u_half, v_half = (0, 1, 2), (3, 4, 5)
    scores += meet(
        lefts,
        [mine_2, mine_3, *visit_2],
        [(0, (2,), None, False), (0, (5,), None, False), (1, u_half + v_half, None, False)]
        + [(r, l, None, True) for r in (2, 3) for l in (u_half, v_half)],
    )

    visit_v = [(got_border, i * half, i) for i in range(got_border.shape[0] // half)]
    if near:
        visit_v += [(passed_3, last * half, 2), (held[0], half, 3)]
    visit_v = visits(visit_v, v_goal)
    (over_3,) = after([over_3], [scores[2][0]])
    across_3 = core_swap(over_3, "across_3")
    left_3 = sides([own_3, beside_3, over_3, across_3], third)
    some = last * half
    scores += meet(
        [*lefts[:3], left_3[0], left_3[1], *lefts[3:]],
        [mine_3, *visit_2, visit_3[0] + visit_3[1], *visit_v],
        [(0, (3,), (0, some), False), (0, (4,), (some, some), False)]
        + [(r, (l,), None, True) for r in (1, 2) for l in (3, 4)]
        + [(r, l, None, True) for r in (3, 4, 5) for l in ((0, 1, 2, 3), (4, 5, 6, 7))],
    )
    found = pl.pallas_call(
        functools.partial(
            route_kernel, [goals for _, goals in scores], parts, chips, cores, half, near
        ),
        out_shape=jax.ShapeDtypeStruct((parts * members, 1, 2 * slots), jnp.float32),
        in_specs=[WHOLE] * len(scores),
        out_specs=WHOLE,
        scratch_shapes=[pltpu.VMEM((1, v_goal + parts * half), jnp.float32)],
        compiler_params=grant(8),
        name="route",
    )(*[best for best, _ in scores])
    got = lax.all_to_all(found, ("blk", "split"), split_axis=0, concat_axis=0, tiled=True)
    return in_data_order(got, rank, parts, members).reshape(rows)


def solution(mesh):
    spec = P(("groups", "blk", "split"))
    return jax.shard_map(
        body,
        mesh=mesh,
        in_specs=(P(("groups", "blk", "split"), None), spec, spec),
        out_specs=spec,
        check_vma=False,
    )
```

```python
import functools

import jax
import jax.numpy as jnp
from jax import lax
from jax.experimental import pallas as pl
from jax.experimental.pallas import tpu as pltpu
from jax.sharding import PartitionSpec as P

MOST = 4096
FILL = -4.0
TAGS = 8
LANES = 128
MIB = 1024 * 1024
WHOLE = pl.BlockSpec(memory_space=pltpu.VMEM)
ANYWHERE = pl.BlockSpec(memory_space=pl.ANY)
REMAINS = pl.BlockSpec(memory_space=pltpu.HBM)


def grant(mib):
    return pltpu.CompilerParams(vmem_limit_bytes=mib * MIB)


def spread(row):
    return jnp.transpose(jnp.broadcast_to(row, (LANES, row.shape[1])))


def column_fold(scores):
    rows, columns = scores.shape
    return jnp.max(scores.reshape(rows // 8, 8, columns), axis=0)


def lane_fold(scores):
    best = scores[:, :LANES]
    for at in range(LANES, scores.shape[1], LANES):
        best = jnp.maximum(best, scores[:, at : at + LANES])
    return best


def order_kernel(parts, chips, rows_hbm, ids_hbm, pos_hbm, *refs):
    outs, rank_ref = refs[:parts], refs[parts]
    unit, pick, placed, tags, rows_ref, ids_ref, pos_ref, sems = refs[parts + 1 :]
    count, width = rows_ref.shape
    quart = count // parts // 4
    step = 256
    fetch_pos = pltpu.make_async_copy(pos_hbm, pos_ref, sems.at[0])
    fetch_rows = pltpu.make_async_copy(rows_hbm, rows_ref, sems.at[1])
    fetch_ids = pltpu.make_async_copy(ids_hbm, ids_ref, sems.at[2])
    fetch_pos.start()
    fetch_rows.start()
    fetch_ids.start()
    fetch_pos.wait()
    pos = pos_ref[...].astype(jnp.float32)
    below = jnp.zeros((8, count), jnp.float32)
    for at in range(0, count, step):
        other = spread(pos[:, at : at + step])[:, :1]
        below += jnp.sum(jnp.where(other < pos, 1.0, 0.0).reshape(step // 8, 8, count), axis=0)
    rank = jnp.sum(below, axis=0, keepdims=True).astype(jnp.int32)
    rank_ref[...] = rank
    for at in range(0, count, step):
        slot = lax.broadcasted_iota(jnp.int32, (step, count), 0) + at
        pick[at : at + step, :] = jnp.where(slot == rank, 1.0, 0.0).astype(jnp.bfloat16)
    fetch_rows.wait()
    fetch_ids.wait()
    values = rows_ref[...].astype(jnp.float32)
    total = jnp.sum(values * values, axis=1, keepdims=True)
    unit[...] = (values * lax.rsqrt(total + 1e-06)).astype(jnp.bfloat16)
    for at in range(0, count, step):
        placed[at : at + step, :] = jnp.dot(
            pick[at : at + step, :], unit[...], preferred_element_type=jnp.float32
        ).astype(jnp.bfloat16)
    ids = jnp.broadcast_to((ids_ref[...] + 1).astype(jnp.bfloat16), (16, count))
    part = lax.axis_index("blk") // chips
    sorted_ids = lax.dot_general(
        ids, pick[...], (((1,), (1,)), ((), ())), preferred_element_type=jnp.float32
    )
    for at in range(4 * parts):
        tags[at, :, :quart] = sorted_ids[:, at * quart : (at + 1) * quart]
    for k in range(parts):
        quarter = lax.bitwise_xor(part, k)
        side = lax.rem(quarter, 2)
        for index, block in enumerate((3 - 3 * side, 2 - side, 3 * side, 1 + side)):
            which = 4 * quarter + block
            at = index * quart
            outs[k][at : at + quart, :] = placed[pl.ds(pl.multiple_of(which * quart, quart), quart), :]
            outs[k][outs[k].shape[0] - TAGS :, at : at + quart] = tags[which, :TAGS, :quart].astype(jnp.bfloat16)


def in_order(embeddings, ids, pos, tag_rows, chips):
    parts = len(tag_rows)
    count, width = embeddings.shape
    slots = count // parts
    outs = [pltpu.VMEM((slots + tags, width), jnp.bfloat16) for tags in tag_rows]
    outs.append(jax.ShapeDtypeStruct((1, count), jnp.int32))
    *blocks, rank = pl.pallas_call(
        functools.partial(order_kernel, parts, chips),
        out_shape=outs,
        in_specs=[REMAINS, REMAINS, REMAINS],
        out_specs=[WHOLE] * len(outs),
        scratch_shapes=[
            pltpu.VMEM((count, width), jnp.bfloat16),
            pltpu.VMEM((count, count), jnp.bfloat16),
            pltpu.VMEM((count, width), jnp.bfloat16),
            pltpu.VMEM((4 * parts, 16, max(slots // 4, LANES)), jnp.float32),
            pltpu.VMEM((count, width), jnp.bfloat16),
            pltpu.VMEM((1, count), jnp.int32),
            pltpu.VMEM((1, count), jnp.int32),
            pltpu.SemaphoreType.DMA((3,)),
        ],
        compiler_params=grant(24),
        name="order",
    )(*[pltpu.with_memory_space_constraint(x, pltpu.HBM) for x in (embeddings, ids.reshape(1, count), pos.reshape(1, count))])
    return blocks, rank


def pack_kernel(plan, inputs, *refs):
    given, outs = refs[:inputs], refs[-len(plan) :]
    for out, pieces in zip(outs, plan):
        at = 0
        for index, start, rows in pieces:
            ref = given[index]
            out[at : at + rows, :] = ref[start : start + rows, :]
            out[out.shape[0] - TAGS :, at : at + rows] = ref[
                ref.shape[0] - TAGS :, start : start + rows
            ]
            at += rows


def pack(blocks, plan, held=(), earlier=()):
    width = blocks[0].shape[1]
    plan = [list(pieces) for pieces in plan]
    outs = [
        jax.ShapeDtypeStruct((sum(p[2] for p in pieces) + TAGS, width), jnp.bfloat16)
        for pieces in plan
    ]
    kept = [jax.ShapeDtypeStruct(h.shape, h.dtype) for h in held]

    def kernel(*refs):
        given = refs[: len(blocks)]
        made = refs[len(blocks) + 2 * len(held) + len(earlier) :]
        pack_kernel(plan, len(given), *given, *made)

    return pl.pallas_call(
        kernel,
        out_shape=kept + outs,
        in_specs=[WHOLE] * len(blocks) + [ANYWHERE] * (len(held) + len(earlier)),
        out_specs=[ANYWHERE] * len(held) + [WHOLE] * len(outs),
        input_output_aliases={len(blocks) + i: i for i in range(len(held))},
        compiler_params=grant(8),
        name="pack",
    )(*blocks, *held, *earlier)


def after(held, earlier):
    return pl.pallas_call(
        lambda *refs: None,
        out_shape=[jax.ShapeDtypeStruct(h.shape, h.dtype) for h in held],
        in_specs=[ANYWHERE] * (len(held) + len(earlier)),
        out_specs=[ANYWHERE] * len(held),
        input_output_aliases={i: i for i in range(len(held))},
        compiler_params=grant(1),
        name="after",
    )(*held, *earlier)


def padded(section):
    rows = sum(piece[2] for piece in section)
    return -(-rows // LANES) * LANES


def overlap(one, other):
    return jnp.logical_and(one[0] <= other[1], other[0] <= one[1])


def meet_kernel(lefts, rights, pairs, inputs, *refs):
    given = refs[:inputs]
    left_out, right_out, left, left_ids, right, right_ids, left_best, right_best = refs[inputs:]

    def ids_of(piece):
        ref, start, rows = given[piece[0]], piece[1], piece[2]
        return ref[ref.shape[0] - TAGS :, start : start + rows].astype(jnp.float32)

    def span(section):
        low, high = None, None
        for piece in section:
            ids = ids_of(piece)
            there = jnp.where(ids > 0.0, ids, 1e6)
            low = there if low is None else jnp.minimum(low, there)
            high = ids if high is None else jnp.maximum(high, ids)
        return jnp.min(low), jnp.max(high)

    tested = [(r, l) for r, l, _, test in pairs if test]
    right_span = {r: span(rights[r]) for r in sorted({r for r, _ in tested})}
    left_span = {l: span(sum((lefts[i] for i in l), [])) for l in sorted({l for _, l in tested})}
    wanted = {(r, l): overlap(right_span[r], left_span[l]) for r, l in tested}

    def place_of(sections):
        out, at = [], 0
        for section in sections:
            rows = padded(section)
            out.append((at, rows))
            at += rows
        return out

    left_at, right_at = place_of(lefts), place_of(rights)

    def fill_left(number):
        at = left_at[number][0]
        for piece in lefts[number]:
            index, start, rows = piece
            left[at : at + rows, :] = given[index][start : start + rows, :]
            left_ids[at : at + rows, :TAGS] = jnp.transpose(ids_of(piece))
            at += rows

    def fill_right(number):
        at = right_at[number][0]
        for piece in rights[number]:
            index, start, rows = piece
            right[at : at + rows, :] = given[index][start : start + rows, :]
            right_ids[:, at : at + rows] = ids_of(piece)
            at += rows

    left_best[...] = jnp.full(left_best.shape, FILL, jnp.float32)
    right_best[...] = jnp.full(right_best.shape, FILL, jnp.float32)
    right_ids[...] = jnp.full(right_ids.shape, -1.0, jnp.float32)
    for which, sections, fill in ((1, lefts, fill_left), (0, rights, fill_right)):
        for number in range(len(sections)):
            uses = [p for p in pairs if (number in p[1] if which else number == p[0])]
            load = functools.partial(fill, number)
            if all(p[3] for p in uses):
                need = [wanted[p[0], p[1]] for p in uses]
                pl.when(functools.reduce(jnp.logical_or, need))(load)
            else:
                load()

    def score(r, l, same):
        (lane, lanes), row = right_at[r], left_at[l[0]][0]
        rows = sum(left_at[i][1] for i in l)
        step = rows
        while step * lanes > 512 * 1024 and step % 32 == 0:
            step //= 2
        across = slice(lane, lane + lanes)

        def turn(index, _):
            at = pl.multiple_of(row + index * step, 16)
            down = pl.ds(at, step)
            scores = lax.dot_general(
                left[down, :],
                right[across, :],
                (((1,), (1,)), ((), ())),
                preferred_element_type=jnp.float32,
            )
            scores = jnp.where(left_ids[down, :1] == right_ids[:1, across], scores, FILL)
            if same is not None:
                first, count = same
                theirs = lax.broadcasted_iota(jnp.int32, (step, lanes), 0) + index * step
                mine = lax.broadcasted_iota(jnp.int32, (step, lanes), 1)
                itself = jnp.logical_and(theirs + first == mine, theirs < count)
                scores = jnp.where(itself, FILL, scores)
            left_best[down, :] = jnp.maximum(left_best[down, :], lane_fold(scores))
            right_best[:, across] = jnp.maximum(right_best[:, across], column_fold(scores))
            return 0

        lax.fori_loop(0, rows // step, turn, 0)

    for r, l, same, test in pairs:
        run = functools.partial(score, r, l, same)
        if test:
            pl.when(wanted[r, l])(run)
        else:
            run()
    right_out[...] = jnp.max(right_best[...], axis=0, keepdims=True)
    left_out[...] = jnp.max(jnp.transpose(left_best[...]), axis=0, keepdims=True)


def meet(lefts, rights, pairs, earlier=()):
    blocks = []

    def plan(sections):
        out = []
        for section in sections:
            pieces = []
            for block, start, rows, _ in section:
                known = [i for i, b in enumerate(blocks) if b is block]
                if not known:
                    blocks.append(block)
                pieces.append((known[0] if known else len(blocks) - 1, start, rows))
            out.append(pieces)
        return out

    def goals(sections):
        out = []
        for section in sections:
            out += [(p[3], p[2]) for p in section]
            out.append((None, padded(section) - sum(p[2] for p in section)))
        return out

    plan_left, plan_right = plan(lefts), plan(rights)
    width = blocks[0].shape[1]
    count = sum(n for _, n in goals(lefts))
    total = sum(n for _, n in goals(rights))
    inputs = len(blocks)

    def kernel(*refs):
        meet_kernel(
            plan_left, plan_right, pairs, inputs, *refs[:inputs], *refs[inputs + len(earlier) :]
        )

    left_best, right_best = pl.pallas_call(
        kernel,
        out_shape=[
            jax.ShapeDtypeStruct((1, count), jnp.float32),
            jax.ShapeDtypeStruct((1, total), jnp.float32),
        ],
        in_specs=[WHOLE] * inputs + [ANYWHERE] * len(earlier),
        out_specs=[WHOLE] * 2,
        scratch_shapes=[
            pltpu.VMEM((count, width), jnp.bfloat16),
            pltpu.VMEM((count, LANES), jnp.float32),
            pltpu.VMEM((total, width), jnp.bfloat16),
            pltpu.VMEM((TAGS, total), jnp.float32),
            pltpu.VMEM((count, LANES), jnp.float32),
            pltpu.VMEM((8, total), jnp.float32),
        ],
        compiler_params=grant(28),
        cost_estimate=pl.CostEstimate(flops=0, bytes_accessed=0, transcendentals=0),
        name="meet",
    )(*blocks, *earlier)
    return [(left_best, goals(lefts)), (right_best, goals(rights))]


def route_kernel(plan, parts, chips, cores, half, near, *refs):
    given, out_ref, gathered = refs[:-2], refs[-2], refs[-1]
    chip, members = lax.axis_index("blk"), chips * cores
    part, me = chip // chips, lax.rem(chip, chips) * cores + lax.axis_index("split")
    slots = 2 * half
    out_ref[...] = jnp.full(out_ref.shape, FILL, jnp.float32)
    gathered[...] = jnp.full(gathered.shape, FILL, jnp.float32)
    starts = {"u": members * parts * slots, "v": members * parts * slots + parts * half}
    for ref, pieces in zip(given, plan):
        at = 0
        for to, entries in pieces:
            if to is not None:
                gathered[:, to : to + entries] = jnp.maximum(
                    gathered[:, to : to + entries], ref[:, at : at + entries]
                )
            at += entries
    for member in range(members):
        whose = lax.bitwise_xor(me, member)
        for k in range(parts):
            at = (member * parts + k) * slots
            source = lax.bitwise_xor(part, k) * members + whose
            out_ref[source, :, :slots] = gathered[:, at : at + slots]
    beyond = lax.rem(part + parts - 1 + 2 * lax.rem(part, 2), parts)
    if near:
        beyond = lax.bitwise_xor(part, 3)
    next_to = lax.bitwise_xor(part, 1)
    from_u = [next_to] + [lax.bitwise_xor(next_to, k) for k in range(2, parts)] + [part]
    from_v = [beyond, lax.bitwise_xor(beyond, 1)]
    from_v += [next_to, part] if near else [lax.bitwise_xor(beyond, k) for k in range(2, parts)]
    for kind, sources, lane in (("u", from_u, slots), ("v", from_v, slots + half)):
        for index, source in enumerate(sources):
            at = starts[kind] + index * half
            out_ref[source * members + me, :, lane : lane + half] = gathered[:, at : at + half]


def back_kernel(parts, members, got_ref, rank_ref, out_ref):
    slots = got_ref.shape[2] // 2
    half = slots // 2
    rows = []
    for part in range(parts):
        best = got_ref[part * members]
        for member in range(1, members):
            best = jnp.maximum(best, got_ref[part * members + member])
        rows.append(best)
    rank = rank_ref[...]
    nothing = jnp.full((1, half), FILL, jnp.float32)
    best = jnp.full((8, rank.shape[1]), FILL, jnp.float32)
    for part in range(parts):
        beyond = part + 1 if part % 2 else part - 1
        there = 0 <= beyond < parts
        faces = jnp.maximum(rows[part][:, :half], rows[part ^ 1][:, slots : slots + half])
        turned = jnp.maximum(
            rows[part][:, half:slots], rows[beyond][:, slots + half :] if there else nothing
        )
        near_u, far_u = faces[:, : half // 2], faces[:, half // 2 :]
        near_v, far_v = turned[:, : half // 2], turned[:, half // 2 :]
        order = [near_u, far_u, far_v, near_v] if part % 2 else [near_v, far_v, far_u, near_u]
        values = spread(jnp.concatenate(order, axis=1))[:, :1]
        slot = lax.broadcasted_iota(jnp.int32, (slots, rank.shape[1]), 0) + part * slots
        best = jnp.maximum(best, column_fold(jnp.where(slot == rank, values, FILL)))
    out_ref[...] = jnp.max(best, axis=0, keepdims=True)


def in_data_order(got, rank, parts, members):
    return pl.pallas_call(
        functools.partial(back_kernel, parts, members),
        out_shape=jax.ShapeDtypeStruct(rank.shape, jnp.float32),
        in_specs=[WHOLE, WHOLE],
        out_specs=WHOLE,
        compiler_params=grant(16),
        name="back",
    )(got, rank)


def body(embeddings, cluster_of, target_pos):
    blocks, cores = lax.axis_size("blk"), lax.axis_size("split")
    rows, width = embeddings.shape
    members = MOST // rows
    chips = members // cores
    parts = blocks // chips
    half = rows // parts // 2
    slots = 2 * half
    def between(array, pairs, name):
        route = [(s * chips + c, t * chips + c) for s, t in pairs for c in range(chips)]
        with jax.named_scope(name):
            return lax.ppermute(array, "blk", route)

    def swap(array, k, name):
        return between(array, [(part, part ^ k) for part in range(parts)], name)

    def chip_swap(array, name):
        with jax.named_scope(name):
            return lax.ppermute(array, "blk", [(b, b ^ 1) for b in range(blocks)])

    def core_swap(array, name):
        with jax.named_scope(name):
            return lax.ppermute(array, "split", [(c, c ^ 1) for c in range(cores)])

    borders = [(p, p + 1) for p in range(1, parts - 1, 2)]
    borders += [(t, s) for s, t in borders]
    near = all(s ^ t == 3 for s, t in borders)

    quart = half // 2
    middle = (parts + 2) // 2
    second, third = [1, *range(2, middle)], list(range(middle, parts))
    u_goal = members * parts * slots
    v_goal = u_goal + parts * half

    def sides(blocks, ks, member=0):
        out = []
        for side in (0, half):
            for m, block in enumerate(blocks, member):
                for i, k in enumerate(ks):
                    goal = (m * parts + k) * slots + side
                    out.append((block, i * slots + side, half, goal))
        return out[: len(out) // 2], out[len(out) // 2 :]

    def whole(block, ks):
        return [(block, i * slots, slots, k * slots) for i, k in enumerate(ks)]

    def visits(pieces, goal):
        near_rows = [(b, at, quart, goal + i * half) for b, at, i in pieces]
        far_rows = [(b, at + quart, quart, goal + i * half + quart) for b, at, i in pieces]
        return near_rows, far_rows

    sent, rank = in_order(
        embeddings, cluster_of, target_pos, [TAGS if k < middle else 2 * TAGS for k in range(parts)], chips
    )
    own_0 = sent[0]
    got = [swap(sent[k], k, "rows_2") for k in second]
    over_0 = chip_swap(own_0, "over_0")
    beside_0 = core_swap(own_0, "beside_0")

    def joined(got):
        if len(got) == 1:
            return got[0]
        return pack(got, [[(i, 0, slots) for i in range(len(got))]])[0]

    own_1, own_2 = got[0], joined(got[1:])
    forward = [(len(second) - 1, 0, half)] + [(i, 0, half) for i in range(len(second) - 1)]
    *held, passing = pack(
        [*got[1:], own_0], [forward], held=[sent[k] for k in third], earlier=[over_0]
    )
    got_3 = [swap(b, k, "rows_3") for k, b in zip(third, held)]
    over_1, over_2 = chip_swap(own_1, "over_1"), chip_swap(own_2, "over_2")
    passed_2 = swap(passing, 1, "passed_2")
    across_0 = core_swap(over_0, "across_0")
    beside_1, beside_2 = core_swap(own_1, "beside_1"), core_swap(own_2, "beside_2")

    def pair(member, block_1, block_2):
        return [
            a + b for a, b in zip(sides([block_1], [1], member), sides([block_2], second[1:], member))
        ]

    left_0 = sides([own_0, beside_0, over_0, across_0], [0])
    mine_0, mine_2 = whole(own_0, [0]), sum(pair(0, own_1, own_2), [])
    here_2 = [a + b for a, b in zip(pair(0, own_1, own_2), pair(1, beside_1, beside_2))]
    some = len(second) * half
    scores = meet(
        [*left_0, *here_2],
        [mine_0, mine_2],
        [(0, (0,), (0, half), False), (0, (1,), (half, half), False)]
        + [(1, (0, 1), None, False)]
        + [(1, (2,), (0, some), False), (1, (3,), (some, some), False)],
    )

    last = len(third)
    own_3 = joined(got_3)
    border = [(last, half, half), (last + 1, half, half)]
    forward = [(i, 0, half) for i in range(last)]
    inputs = [*got_3, own_0, own_1]
    if near:
        inputs.append(sent[2])
        forward.append((last + 2, half, half))
    else:
        border += [(last + 1 + i, half, half) for i in range(1, len(second))]
        border += [(i, half, half) for i in range(last)]
        inputs += got[1:]
    own_3, border, passing = pack(
        inputs, [border, forward], held=[own_3], earlier=[scores[0][0]]
    )
    over_3 = chip_swap(own_3, "over_3")
    got_border = between(border, borders, "border")
    passed_3 = swap(passing, 1, "passed_3")
    over_1, over_2 = after([over_1, over_2], [own_3, passed_2])
    across_1, across_2 = core_swap(over_1, "across_1"), core_swap(over_2, "across_2")
    beside_3 = core_swap(own_3, "beside_3")
    there_2 = [a + b for a, b in zip(pair(2, over_1, over_2), pair(3, across_1, across_2))]
    visit_2 = [(passed_2, i * half, i) for i in range(len(second))]
    visit_2 = visits(visit_2 + [(sent[1], 0, parts - 1)], u_goal)
    visit_3 = visits([(passed_3, i * half, len(second) + i) for i in range(last)], u_goal)
    mine_3 = sum(sides([own_3], third), [])
    lefts = [left_0[0], here_2[0], there_2[0], there_2[1], left_0[1], here_2[1]]
    u_half, v_half = (0, 1, 2), (3, 4, 5)
    scores += meet(
        lefts,
        [mine_2, mine_3, *visit_2],
        [(0, (2, 3), None, False), (1, u_half + v_half, None, False)]
        + [(r, l, None, True) for r in (2, 3) for l in (u_half, v_half)],
    )

    visit_v = [(got_border, i * half, i) for i in range(got_border.shape[0] // half)]
    if near:
        visit_v += [(passed_3, last * half, 2), (held[0], half, 3)]
    visit_v = visits(visit_v, v_goal)
    (over_3,) = after([over_3], [scores[2][0], got_border, passed_3])
    across_3 = core_swap(over_3, "across_3")
    left_3 = sides([own_3, beside_3, over_3, across_3], third)
    some = last * half
    scores += meet(
        [*lefts[:3], left_3[0], left_3[1], *lefts[3:]],
        [mine_3, *visit_2, visit_3[0] + visit_3[1], *visit_v],
        [(0, (3,), (0, some), False), (0, (4,), (some, some), False)]
        + [(r, (l,), None, True) for r in (1, 2) for l in (3, 4)]
        + [(r, l, None, True) for r in (3, 4, 5) for l in ((0, 1, 2, 3), (4, 5, 6, 7))],
    )
    found = pl.pallas_call(
        functools.partial(
            route_kernel, [goals for _, goals in scores], parts, chips, cores, half, near
        ),
        out_shape=jax.ShapeDtypeStruct((parts * members, 1, 2 * slots), jnp.float32),
        in_specs=[WHOLE] * len(scores),
        out_specs=WHOLE,
        scratch_shapes=[pltpu.VMEM((1, v_goal + parts * half), jnp.float32)],
        compiler_params=grant(8),
        name="route",
    )(*[best for best, _ in scores])
    got = lax.all_to_all(found, ("blk", "split"), split_axis=0, concat_axis=0, tiled=True)
    return in_data_order(got, rank, parts, members).reshape(rows)


def solution(mesh):
    spec = P(("groups", "blk", "split"))
    return jax.shard_map(
        body,
        mesh=mesh,
        in_specs=(P(("groups", "blk", "split"), None), spec, spec),
        out_specs=spec,
        check_vma=False,
    )
```

```python
import functools

import jax
import jax.numpy as jnp
from jax import lax
from jax.experimental import pallas as pl
from jax.experimental.pallas import tpu as pltpu
from jax.sharding import PartitionSpec as P

MOST = 4096
FILL = -4.0
TAGS = 8
LANES = 128
MIB = 1024 * 1024
WHOLE = pl.BlockSpec(memory_space=pltpu.VMEM)
ANYWHERE = pl.BlockSpec(memory_space=pl.ANY)
REMAINS = pl.BlockSpec(memory_space=pltpu.HBM)


def grant(mib):
    return pltpu.CompilerParams(vmem_limit_bytes=mib * MIB)


def spread(row):
    return jnp.transpose(jnp.broadcast_to(row, (LANES, row.shape[1])))


def column_fold(scores):
    rows, columns = scores.shape
    return jnp.max(scores.reshape(rows // 8, 8, columns), axis=0)


def lane_fold(scores):
    best = scores[:, :LANES]
    for at in range(LANES, scores.shape[1], LANES):
        best = jnp.maximum(best, scores[:, at : at + LANES])
    return best


def order_kernel(parts, chips, rows_hbm, ids_hbm, pos_hbm, *refs):
    outs, rank_ref = refs[:parts], refs[parts]
    unit, pick, placed, tags, rows_ref, ids_ref, pos_ref, sems = refs[parts + 1 :]
    count, width = rows_ref.shape
    quart = count // parts // 4
    step = 256
    fetch_pos = pltpu.make_async_copy(pos_hbm, pos_ref, sems.at[0])
    fetch_rows = pltpu.make_async_copy(rows_hbm, rows_ref, sems.at[1])
    fetch_ids = pltpu.make_async_copy(ids_hbm, ids_ref, sems.at[2])
    fetch_pos.start()
    fetch_rows.start()
    fetch_ids.start()
    fetch_pos.wait()
    pos = pos_ref[...].astype(jnp.float32)
    below = jnp.zeros((8, count), jnp.float32)
    for at in range(0, count, step):
        other = spread(pos[:, at : at + step])[:, :1]
        below += jnp.sum(jnp.where(other < pos, 1.0, 0.0).reshape(step // 8, 8, count), axis=0)
    rank = jnp.sum(below, axis=0, keepdims=True).astype(jnp.int32)
    rank_ref[...] = rank
    for at in range(0, count, step):
        slot = lax.broadcasted_iota(jnp.int32, (step, count), 0) + at
        pick[at : at + step, :] = jnp.where(slot == rank, 1.0, 0.0).astype(jnp.bfloat16)
    fetch_rows.wait()
    fetch_ids.wait()
    values = rows_ref[...].astype(jnp.float32)
    total = jnp.sum(values * values, axis=1, keepdims=True)
    unit[...] = (values * lax.rsqrt(total + 1e-06)).astype(jnp.bfloat16)
    placed[...] = jnp.dot(pick[...], unit[...], preferred_element_type=jnp.float32).astype(
        jnp.bfloat16
    )
    ids = jnp.broadcast_to((ids_ref[...] + 1).astype(jnp.bfloat16), (16, count))
    part = lax.axis_index("blk") // chips
    sorted_ids = lax.dot_general(
        ids, pick[...], (((1,), (1,)), ((), ())), preferred_element_type=jnp.float32
    )
    for at in range(4 * parts):
        tags[at, :, :quart] = sorted_ids[:, at * quart : (at + 1) * quart]
    for k in range(parts):
        quarter = lax.bitwise_xor(part, k)
        side = lax.rem(quarter, 2)
        for index, block in enumerate((3 - 3 * side, 2 - side, 3 * side, 1 + side)):
            which = 4 * quarter + block
            at = index * quart
            outs[k][at : at + quart, :] = placed[pl.ds(pl.multiple_of(which * quart, quart), quart), :]
            outs[k][outs[k].shape[0] - TAGS :, at : at + quart] = tags[which, :TAGS, :quart].astype(jnp.bfloat16)


def in_order(embeddings, ids, pos, tag_rows, chips):
    parts = len(tag_rows)
    count, width = embeddings.shape
    slots = count // parts
    outs = [pltpu.VMEM((slots + tags, width), jnp.bfloat16) for tags in tag_rows]
    outs.append(jax.ShapeDtypeStruct((1, count), jnp.int32))
    *blocks, rank = pl.pallas_call(
        functools.partial(order_kernel, parts, chips),
        out_shape=outs,
        in_specs=[REMAINS, REMAINS, REMAINS],
        out_specs=[WHOLE] * len(outs),
        scratch_shapes=[
            pltpu.VMEM((count, width), jnp.bfloat16),
            pltpu.VMEM((count, count), jnp.bfloat16),
            pltpu.VMEM((count, width), jnp.bfloat16),
            pltpu.VMEM((4 * parts, 16, max(slots // 4, LANES)), jnp.float32),
            pltpu.VMEM((count, width), jnp.bfloat16),
            pltpu.VMEM((1, count), jnp.int32),
            pltpu.VMEM((1, count), jnp.int32),
            pltpu.SemaphoreType.DMA((3,)),
        ],
        compiler_params=grant(24),
        name="order",
    )(*[pltpu.with_memory_space_constraint(x, pltpu.HBM) for x in (embeddings, ids.reshape(1, count), pos.reshape(1, count))])
    return blocks, rank


def pack_kernel(plan, inputs, *refs):
    given, outs = refs[:inputs], refs[-len(plan) :]
    for out, pieces in zip(outs, plan):
        at = 0
        for index, start, rows in pieces:
            ref = given[index]
            out[at : at + rows, :] = ref[start : start + rows, :]
            out[out.shape[0] - TAGS :, at : at + rows] = ref[
                ref.shape[0] - TAGS :, start : start + rows
            ]
            at += rows


def pack(blocks, plan, held=(), earlier=(), spare=0):
    width = blocks[0].shape[1]
    plan = [list(pieces) for pieces in plan]
    outs = [
        jax.ShapeDtypeStruct(
            (sum(p[2] for p in pieces) + TAGS + spare, width), jnp.bfloat16
        )
        for pieces in plan
    ]
    kept = [jax.ShapeDtypeStruct(h.shape, h.dtype) for h in held]

    def kernel(*refs):
        given = refs[: len(blocks)]
        made = refs[len(blocks) + 2 * len(held) + len(earlier) :]
        pack_kernel(plan, len(given), *given, *made)

    return pl.pallas_call(
        kernel,
        out_shape=kept + outs,
        in_specs=[WHOLE] * len(blocks) + [ANYWHERE] * (len(held) + len(earlier)),
        out_specs=[ANYWHERE] * len(held) + [WHOLE] * len(outs),
        input_output_aliases={len(blocks) + i: i for i in range(len(held))},
        compiler_params=grant(8),
        name="pack",
    )(*blocks, *held, *earlier)


def after(held, earlier):
    return pl.pallas_call(
        lambda *refs: None,
        out_shape=[jax.ShapeDtypeStruct(h.shape, h.dtype) for h in held],
        in_specs=[ANYWHERE] * (len(held) + len(earlier)),
        out_specs=[ANYWHERE] * len(held),
        input_output_aliases={i: i for i in range(len(held))},
        compiler_params=grant(1),
        name="after",
    )(*held, *earlier)


def padded(section):
    rows = sum(piece[2] for piece in section)
    return -(-rows // LANES) * LANES


def overlap(one, other):
    return jnp.logical_and(one[0] <= other[1], other[0] <= one[1])


def meet_kernel(lefts, rights, pairs, inputs, *refs):
    given = refs[:inputs]
    left_out, right_out, left, left_ids, right, right_ids, left_best, right_best = refs[inputs:]

    def ids_of(piece):
        ref, start, rows = given[piece[0]], piece[1], piece[2]
        return ref[ref.shape[0] - TAGS :, start : start + rows].astype(jnp.float32)

    def span(section):
        low, high = None, None
        for piece in section:
            ids = ids_of(piece)
            there = jnp.where(ids > 0.0, ids, 1e6)
            low = there if low is None else jnp.minimum(low, there)
            high = ids if high is None else jnp.maximum(high, ids)
        return jnp.min(low), jnp.max(high)

    tested = [(r, l) for r, l, _, test in pairs if test]
    right_span = {r: span(rights[r]) for r in sorted({r for r, _ in tested})}
    left_span = {l: span(sum((lefts[i] for i in l), [])) for l in sorted({l for _, l in tested})}
    wanted = {(r, l): overlap(right_span[r], left_span[l]) for r, l in tested}

    def place_of(sections):
        out, at = [], 0
        for section in sections:
            rows = padded(section)
            out.append((at, rows))
            at += rows
        return out

    left_at, right_at = place_of(lefts), place_of(rights)

    def fill_left(number):
        at = left_at[number][0]
        for piece in lefts[number]:
            index, start, rows = piece
            left[at : at + rows, :] = given[index][start : start + rows, :]
            left_ids[at : at + rows, :TAGS] = jnp.transpose(ids_of(piece))
            at += rows

    def fill_right(number):
        at = right_at[number][0]
        for piece in rights[number]:
            index, start, rows = piece
            right[at : at + rows, :] = given[index][start : start + rows, :]
            right_ids[:, at : at + rows] = ids_of(piece)
            at += rows

    left_best[...] = jnp.full(left_best.shape, FILL, jnp.float32)
    right_best[...] = jnp.full(right_best.shape, FILL, jnp.float32)
    right_ids[...] = jnp.full(right_ids.shape, -1.0, jnp.float32)
    for which, sections, fill in ((1, lefts, fill_left), (0, rights, fill_right)):
        for number in range(len(sections)):
            uses = [p for p in pairs if (number in p[1] if which else number == p[0])]
            load = functools.partial(fill, number)
            if all(p[3] for p in uses):
                need = [wanted[p[0], p[1]] for p in uses]
                pl.when(functools.reduce(jnp.logical_or, need))(load)
            else:
                load()

    def score(r, l, same):
        (lane, lanes), row = right_at[r], left_at[l[0]][0]
        rows = sum(left_at[i][1] for i in l)
        step = rows
        while step * lanes > 512 * 1024 and step % 32 == 0:
            step //= 2
        across = slice(lane, lane + lanes)

        def turn(index, _):
            at = pl.multiple_of(row + index * step, 16)
            down = pl.ds(at, step)
            scores = lax.dot_general(
                left[down, :],
                right[across, :],
                (((1,), (1,)), ((), ())),
                preferred_element_type=jnp.float32,
            )
            scores = jnp.where(left_ids[down, :1] == right_ids[:1, across], scores, FILL)
            if same is not None:
                first, count = same
                theirs = lax.broadcasted_iota(jnp.int32, (step, lanes), 0) + index * step
                mine = lax.broadcasted_iota(jnp.int32, (step, lanes), 1)
                itself = jnp.logical_and(theirs + first == mine, theirs < count)
                scores = jnp.where(itself, FILL, scores)
            left_best[down, :] = jnp.maximum(left_best[down, :], lane_fold(scores))
            right_best[:, across] = jnp.maximum(right_best[:, across], column_fold(scores))
            return 0

        lax.fori_loop(0, rows // step, turn, 0)

    for r, l, same, test in pairs:
        run = functools.partial(score, r, l, same)
        if test:
            pl.when(wanted[r, l])(run)
        else:
            run()
    right_out[...] = jnp.max(right_best[...], axis=0, keepdims=True)
    left_out[...] = jnp.max(jnp.transpose(left_best[...]), axis=0, keepdims=True)


def meet(lefts, rights, pairs, earlier=()):
    blocks = []

    def plan(sections):
        out = []
        for section in sections:
            pieces = []
            for block, start, rows, _ in section:
                known = [i for i, b in enumerate(blocks) if b is block]
                if not known:
                    blocks.append(block)
                pieces.append((known[0] if known else len(blocks) - 1, start, rows))
            out.append(pieces)
        return out

    def goals(sections):
        out = []
        for section in sections:
            out += [(p[3], p[2]) for p in section]
            out.append((None, padded(section) - sum(p[2] for p in section)))
        return out

    plan_left, plan_right = plan(lefts), plan(rights)
    width = blocks[0].shape[1]
    count = sum(n for _, n in goals(lefts))
    total = sum(n for _, n in goals(rights))
    inputs = len(blocks)

    def kernel(*refs):
        meet_kernel(
            plan_left, plan_right, pairs, inputs, *refs[:inputs], *refs[inputs + len(earlier) :]
        )

    left_best, right_best = pl.pallas_call(
        kernel,
        out_shape=[
            jax.ShapeDtypeStruct((1, count), jnp.float32),
            jax.ShapeDtypeStruct((1, total), jnp.float32),
        ],
        in_specs=[WHOLE] * inputs + [ANYWHERE] * len(earlier),
        out_specs=[WHOLE] * 2,
        scratch_shapes=[
            pltpu.VMEM((count, width), jnp.bfloat16),
            pltpu.VMEM((count, LANES), jnp.float32),
            pltpu.VMEM((total, width), jnp.bfloat16),
            pltpu.VMEM((TAGS, total), jnp.float32),
            pltpu.VMEM((count, LANES), jnp.float32),
            pltpu.VMEM((8, total), jnp.float32),
        ],
        compiler_params=grant(28),
        cost_estimate=pl.CostEstimate(flops=0, bytes_accessed=0, transcendentals=0),
        name="meet",
    )(*blocks, *earlier)
    return [(left_best, goals(lefts)), (right_best, goals(rights))]


def route_kernel(plan, parts, chips, cores, half, near, *refs):
    given, out_ref, gathered = refs[:-2], refs[-2], refs[-1]
    chip, members = lax.axis_index("blk"), chips * cores
    part, me = chip // chips, lax.rem(chip, chips) * cores + lax.axis_index("split")
    slots = 2 * half
    out_ref[...] = jnp.full(out_ref.shape, FILL, jnp.float32)
    gathered[...] = jnp.full(gathered.shape, FILL, jnp.float32)
    starts = {"u": members * parts * slots, "v": members * parts * slots + parts * half}
    for ref, pieces in zip(given, plan):
        at = 0
        for to, entries in pieces:
            if to is not None:
                gathered[:, to : to + entries] = jnp.maximum(
                    gathered[:, to : to + entries], ref[:, at : at + entries]
                )
            at += entries
    for member in range(members):
        whose = lax.bitwise_xor(me, member)
        for k in range(parts):
            at = (member * parts + k) * slots
            source = lax.bitwise_xor(part, k) * members + whose
            out_ref[source, :, :slots] = gathered[:, at : at + slots]
    beyond = lax.rem(part + parts - 1 + 2 * lax.rem(part, 2), parts)
    if near:
        beyond = lax.bitwise_xor(part, 3)
    next_to = lax.bitwise_xor(part, 1)
    from_u = [next_to] + [lax.bitwise_xor(next_to, k) for k in range(2, parts)] + [part]
    from_v = [beyond, lax.bitwise_xor(beyond, 1)]
    from_v += [next_to, part] if near else [lax.bitwise_xor(beyond, k) for k in range(2, parts)]
    for kind, sources, lane in (("u", from_u, slots), ("v", from_v, slots + half)):
        for index, source in enumerate(sources):
            at = starts[kind] + index * half
            out_ref[source * members + me, :, lane : lane + half] = gathered[:, at : at + half]


def back_kernel(parts, members, got_ref, rank_ref, out_ref):
    slots = got_ref.shape[2] // 2
    half = slots // 2
    rows = []
    for part in range(parts):
        best = got_ref[part * members]
        for member in range(1, members):
            best = jnp.maximum(best, got_ref[part * members + member])
        rows.append(best)
    rank = rank_ref[...]
    nothing = jnp.full((1, half), FILL, jnp.float32)
    best = jnp.full((8, rank.shape[1]), FILL, jnp.float32)
    for part in range(parts):
        beyond = part + 1 if part % 2 else part - 1
        there = 0 <= beyond < parts
        faces = jnp.maximum(rows[part][:, :half], rows[part ^ 1][:, slots : slots + half])
        turned = jnp.maximum(
            rows[part][:, half:slots], rows[beyond][:, slots + half :] if there else nothing
        )
        near_u, far_u = faces[:, : half // 2], faces[:, half // 2 :]
        near_v, far_v = turned[:, : half // 2], turned[:, half // 2 :]
        order = [near_u, far_u, far_v, near_v] if part % 2 else [near_v, far_v, far_u, near_u]
        values = spread(jnp.concatenate(order, axis=1))[:, :1]
        slot = lax.broadcasted_iota(jnp.int32, (slots, rank.shape[1]), 0) + part * slots
        best = jnp.maximum(best, column_fold(jnp.where(slot == rank, values, FILL)))
    out_ref[...] = jnp.max(best, axis=0, keepdims=True)


def in_data_order(got, rank, parts, members):
    return pl.pallas_call(
        functools.partial(back_kernel, parts, members),
        out_shape=jax.ShapeDtypeStruct(rank.shape, jnp.float32),
        in_specs=[WHOLE, WHOLE],
        out_specs=WHOLE,
        compiler_params=grant(16),
        name="back",
    )(got, rank)


def body(embeddings, cluster_of, target_pos):
    blocks, cores = lax.axis_size("blk"), lax.axis_size("split")
    rows, width = embeddings.shape
    members = MOST // rows
    chips = members // cores
    parts = blocks // chips
    half = rows // parts // 2
    slots = 2 * half
    def between(array, pairs, name):
        route = [(s * chips + c, t * chips + c) for s, t in pairs for c in range(chips)]
        with jax.named_scope(name):
            return lax.ppermute(array, "blk", route)

    def swap(array, k, name):
        return between(array, [(part, part ^ k) for part in range(parts)], name)

    def chip_swap(array, name):
        with jax.named_scope(name):
            return lax.ppermute(array, "blk", [(b, b ^ 1) for b in range(blocks)])

    def core_swap(array, name):
        with jax.named_scope(name):
            return lax.ppermute(array, "split", [(c, c ^ 1) for c in range(cores)])

    borders = [(p, p + 1) for p in range(1, parts - 1, 2)]
    borders += [(t, s) for s, t in borders]
    near = all(s ^ t == 3 for s, t in borders)

    quart = half // 2
    middle = (parts + 2) // 2
    second, third = [1, *range(2, middle)], list(range(middle, parts))
    u_goal = members * parts * slots
    v_goal = u_goal + parts * half

    def sides(blocks, ks, member=0):
        out = []
        for side in (0, half):
            for m, block in enumerate(blocks, member):
                for i, k in enumerate(ks):
                    goal = (m * parts + k) * slots + side
                    out.append((block, i * slots + side, half, goal))
        return out[: len(out) // 2], out[len(out) // 2 :]

    def whole(block, ks):
        return [(block, i * slots, slots, k * slots) for i, k in enumerate(ks)]

    def visits(pieces, goal):
        near_rows = [(b, at, quart, goal + i * half) for b, at, i in pieces]
        far_rows = [(b, at + quart, quart, goal + i * half + quart) for b, at, i in pieces]
        return near_rows, far_rows

    sent, rank = in_order(
        embeddings, cluster_of, target_pos, [TAGS if k < middle else 2 * TAGS for k in range(parts)], chips
    )
    own_0 = sent[0]
    got = [swap(sent[k], k, "rows_2") for k in second]
    over_0 = chip_swap(own_0, "over_0")
    beside_0 = core_swap(own_0, "beside_0")

    def joined(got):
        if len(got) == 1:
            return got[0]
        return pack(got, [[(i, 0, slots) for i in range(len(got))]])[0]

    own_1, own_2 = got[0], joined(got[1:])
    forward = [(len(second) - 1, 0, half)] + [(i, 0, half) for i in range(len(second) - 1)]
    *held, passing = pack(
        [*got[1:], own_0], [forward], held=[sent[k] for k in third], earlier=[over_0]
    )
    got_3 = [swap(b, k, "rows_3") for k, b in zip(third, held)]
    over_1, over_2 = chip_swap(own_1, "over_1"), chip_swap(own_2, "over_2")
    passed_2 = swap(passing, 1, "passed_2")
    across_0 = core_swap(over_0, "across_0")
    beside_1, beside_2 = core_swap(own_1, "beside_1"), core_swap(own_2, "beside_2")

    def pair(member, block_1, block_2):
        return [
            a + b for a, b in zip(sides([block_1], [1], member), sides([block_2], second[1:], member))
        ]

    left_0 = sides([own_0, beside_0, over_0, across_0], [0])
    mine_0, mine_2 = whole(own_0, [0]), sum(pair(0, own_1, own_2), [])
    here_2 = [a + b for a, b in zip(pair(0, own_1, own_2), pair(1, beside_1, beside_2))]
    some = len(second) * half
    scores = meet(
        [*left_0, *here_2],
        [mine_0, mine_2],
        [(0, (0,), (0, half), False), (0, (1,), (half, half), False)]
        + [(1, (0, 1), None, False)]
        + [(1, (2,), (0, some), False), (1, (3,), (some, some), False)],
    )

    last = len(third)
    own_3 = joined(got_3)
    border = [(last, half, half), (last + 1, half, half)]
    forward = [(i, 0, half) for i in range(last)]
    inputs = [*got_3, own_0, own_1]
    if near:
        inputs.append(sent[2])
        forward.append((last + 2, half, half))
    else:
        border += [(last + 1 + i, half, half) for i in range(1, len(second))]
        border += [(i, half, half) for i in range(last)]
        inputs += got[1:]
    own_3, border, passing = pack(
        inputs, [border, forward], held=[own_3], earlier=[scores[0][0]], spare=TAGS
    )
    over_3 = chip_swap(own_3, "over_3")
    got_border = between(border, borders, "border")
    passed_3 = swap(passing, 1, "passed_3")
    over_1, over_2 = after([over_1, over_2], [own_3, passed_2])
    across_1, across_2 = core_swap(over_1, "across_1"), core_swap(over_2, "across_2")
    beside_3 = core_swap(own_3, "beside_3")
    there_2 = [a + b for a, b in zip(pair(2, over_1, over_2), pair(3, across_1, across_2))]
    visit_2 = [(passed_2, i * half, i) for i in range(len(second))]
    visit_2 = visits(visit_2 + [(sent[1], 0, parts - 1)], u_goal)
    visit_3 = visits([(passed_3, i * half, len(second) + i) for i in range(last)], u_goal)
    mine_3 = sum(sides([own_3], third), [])
    lefts = [left_0[0], here_2[0], there_2[0], there_2[1], left_0[1], here_2[1]]
    u_half, v_half = (0, 1, 2), (3, 4, 5)
    scores += meet(
        lefts,
        [mine_2, mine_3, *visit_2],
        [(0, (2, 3), None, False), (1, u_half + v_half, None, False)]
        + [(r, l, None, True) for r in (2, 3) for l in (u_half, v_half)],
    )

    visit_v = [(got_border, i * half, i) for i in range(2 if near else parts)]
    if near:
        visit_v += [(passed_3, last * half, 2), (held[0], half, 3)]
    visit_v = visits(visit_v, v_goal)
    (over_3,) = after([over_3], [scores[2][0], got_border, passed_3])
    across_3 = core_swap(over_3, "across_3")
    left_3 = sides([own_3, beside_3, over_3, across_3], third)
    some = last * half
    scores += meet(
        [*lefts[:3], left_3[0], left_3[1], *lefts[3:]],
        [mine_3, *visit_2, visit_3[0] + visit_3[1], *visit_v],
        [(0, (3,), (0, some), False), (0, (4,), (some, some), False)]
        + [(r, (l,), None, True) for r in (1, 2) for l in (3, 4)]
        + [(r, l, None, True) for r in (3, 4, 5) for l in ((0, 1, 2, 3), (4, 5, 6, 7))],
    )
    found = pl.pallas_call(
        functools.partial(
            route_kernel, [goals for _, goals in scores], parts, chips, cores, half, near
        ),
        out_shape=jax.ShapeDtypeStruct((parts * members, 1, 2 * slots), jnp.float32),
        in_specs=[WHOLE] * len(scores),
        out_specs=WHOLE,
        scratch_shapes=[pltpu.VMEM((1, v_goal + parts * half), jnp.float32)],
        compiler_params=grant(8),
        name="route",
    )(*[best for best, _ in scores])
    got = lax.all_to_all(found, ("blk", "split"), split_axis=0, concat_axis=0, tiled=True)
    return in_data_order(got, rank, parts, members).reshape(rows)


def solution(mesh):
    spec = P(("groups", "blk", "split"))
    return jax.shard_map(
        body,
        mesh=mesh,
        in_specs=(P(("groups", "blk", "split"), None), spec, spec),
        out_specs=spec,
        check_vma=False,
    )
```

```python
import functools

import jax
import jax.numpy as jnp
from jax import lax
from jax.experimental import pallas as pl
from jax.experimental.pallas import tpu as pltpu
from jax.sharding import PartitionSpec as P

MOST = 4096
FILL = -4.0
TAGS = 8
LANES = 128
MIB = 1024 * 1024
WHOLE = pl.BlockSpec(memory_space=pltpu.VMEM)
ANYWHERE = pl.BlockSpec(memory_space=pl.ANY)
REMAINS = pl.BlockSpec(memory_space=pltpu.HBM)


def grant(mib):
    return pltpu.CompilerParams(vmem_limit_bytes=mib * MIB)


def spread(row):
    return jnp.transpose(jnp.broadcast_to(row, (LANES, row.shape[1])))


def column_fold(scores):
    rows, columns = scores.shape
    return jnp.max(scores.reshape(rows // 8, 8, columns), axis=0)


def lane_fold(scores):
    best = scores[:, :LANES]
    for at in range(LANES, scores.shape[1], LANES):
        best = jnp.maximum(best, scores[:, at : at + LANES])
    return best


def order_kernel(parts, chips, rows_hbm, ids_hbm, pos_hbm, *refs):
    outs, rank_ref = refs[:parts], refs[parts]
    unit, pick, placed, tags, rows_ref, ids_ref, pos_ref, sems = refs[parts + 1 :]
    count, width = rows_ref.shape
    quart = count // parts // 4
    step = 256
    fetch_pos = pltpu.make_async_copy(pos_hbm, pos_ref, sems.at[0])
    fetch_rows = pltpu.make_async_copy(rows_hbm, rows_ref, sems.at[1])
    fetch_ids = pltpu.make_async_copy(ids_hbm, ids_ref, sems.at[2])
    fetch_pos.start()
    fetch_rows.start()
    fetch_ids.start()
    fetch_pos.wait()
    pos = pos_ref[...].astype(jnp.float32)
    below = jnp.zeros((8, count), jnp.float32)
    for at in range(0, count, step):
        other = spread(pos[:, at : at + step])[:, :1]
        below += jnp.sum(jnp.where(other < pos, 1.0, 0.0).reshape(step // 8, 8, count), axis=0)
    rank = jnp.sum(below, axis=0, keepdims=True).astype(jnp.int32)
    rank_ref[...] = rank
    for at in range(0, count, step):
        slot = lax.broadcasted_iota(jnp.int32, (step, count), 0) + at
        pick[at : at + step, :] = jnp.where(slot == rank, 1.0, 0.0).astype(jnp.bfloat16)
    fetch_rows.wait()
    fetch_ids.wait()
    values = rows_ref[...].astype(jnp.float32)
    total = jnp.sum(values * values, axis=1, keepdims=True)
    unit[...] = (values * lax.rsqrt(total + 1e-06)).astype(jnp.bfloat16)
    placed[...] = jnp.dot(pick[...], unit[...], preferred_element_type=jnp.float32).astype(
        jnp.bfloat16
    )
    ids = jnp.broadcast_to((ids_ref[...] + 1).astype(jnp.bfloat16), (16, count))
    part = lax.axis_index("blk") // chips
    sorted_ids = lax.dot_general(
        ids, pick[...], (((1,), (1,)), ((), ())), preferred_element_type=jnp.float32
    )
    for at in range(4 * parts):
        tags[at, :, :quart] = sorted_ids[:, at * quart : (at + 1) * quart]
    for k in range(parts):
        quarter = lax.bitwise_xor(part, k)
        side = lax.rem(quarter, 2)
        for index, block in enumerate((3 - 3 * side, 2 - side, 3 * side, 1 + side)):
            which = 4 * quarter + block
            at = index * quart
            outs[k][at : at + quart, :] = placed[pl.ds(pl.multiple_of(which * quart, quart), quart), :]
            outs[k][outs[k].shape[0] - TAGS :, at : at + quart] = tags[which, :TAGS, :quart].astype(jnp.bfloat16)


def in_order(embeddings, ids, pos, tag_rows, chips):
    parts = len(tag_rows)
    count, width = embeddings.shape
    slots = count // parts
    outs = [pltpu.VMEM((slots + tags, width), jnp.bfloat16) for tags in tag_rows]
    outs.append(jax.ShapeDtypeStruct((1, count), jnp.int32))
    *blocks, rank = pl.pallas_call(
        functools.partial(order_kernel, parts, chips),
        out_shape=outs,
        in_specs=[REMAINS, REMAINS, REMAINS],
        out_specs=[WHOLE] * len(outs),
        scratch_shapes=[
            pltpu.VMEM((count, width), jnp.bfloat16),
            pltpu.VMEM((count, count), jnp.bfloat16),
            pltpu.VMEM((count, width), jnp.bfloat16),
            pltpu.VMEM((4 * parts, 16, max(slots // 4, LANES)), jnp.float32),
            pltpu.VMEM((count, width), jnp.bfloat16),
            pltpu.VMEM((1, count), jnp.int32),
            pltpu.VMEM((1, count), jnp.int32),
            pltpu.SemaphoreType.DMA((3,)),
        ],
        compiler_params=grant(24),
        name="order",
    )(*[pltpu.with_memory_space_constraint(x, pltpu.HBM) for x in (embeddings, ids.reshape(1, count), pos.reshape(1, count))])
    return blocks, rank


def pack_kernel(plan, inputs, *refs):
    given, outs = refs[:inputs], refs[-len(plan) :]
    for out, pieces in zip(outs, plan):
        at = 0
        for index, start, rows in pieces:
            ref = given[index]
            out[at : at + rows, :] = ref[start : start + rows, :]
            out[out.shape[0] - TAGS :, at : at + rows] = ref[
                ref.shape[0] - TAGS :, start : start + rows
            ]
            at += rows


def pack(blocks, plan, held=(), earlier=(), spare=0):
    width = blocks[0].shape[1]
    plan = [list(pieces) for pieces in plan]
    outs = [
        jax.ShapeDtypeStruct(
            (sum(p[2] for p in pieces) + TAGS + spare, width), jnp.bfloat16
        )
        for pieces in plan
    ]
    kept = [jax.ShapeDtypeStruct(h.shape, h.dtype) for h in held]

    def kernel(*refs):
        given = refs[: len(blocks)]
        made = refs[len(blocks) + 2 * len(held) + len(earlier) :]
        pack_kernel(plan, len(given), *given, *made)

    return pl.pallas_call(
        kernel,
        out_shape=kept + outs,
        in_specs=[WHOLE] * len(blocks) + [ANYWHERE] * (len(held) + len(earlier)),
        out_specs=[ANYWHERE] * len(held) + [WHOLE] * len(outs),
        input_output_aliases={len(blocks) + i: i for i in range(len(held))},
        compiler_params=grant(8),
        name="pack",
    )(*blocks, *held, *earlier)


def after(held, earlier):
    return pl.pallas_call(
        lambda *refs: None,
        out_shape=[jax.ShapeDtypeStruct(h.shape, h.dtype) for h in held],
        in_specs=[ANYWHERE] * (len(held) + len(earlier)),
        out_specs=[ANYWHERE] * len(held),
        input_output_aliases={i: i for i in range(len(held))},
        compiler_params=grant(1),
        name="after",
    )(*held, *earlier)


def padded(section):
    rows = sum(piece[2] for piece in section)
    return -(-rows // LANES) * LANES


def overlap(one, other):
    return jnp.logical_and(one[0] <= other[1], other[0] <= one[1])


def meet_kernel(table, fresh, rights, pairs, inputs, first, last, *refs):
    given, outs = refs[:inputs], refs[inputs:]
    left, left_ids, left_best, right_out = outs[:4]
    right, right_ids, right_best = outs[5:] if last else outs[4:]

    def ids_of(piece):
        ref, start, rows = given[piece[0]], piece[1], piece[2]
        return ref[ref.shape[0] - TAGS :, start : start + rows].astype(jnp.float32)

    def span_right(section):
        low, high = None, None
        for piece in section:
            ids = ids_of(piece)
            there = jnp.where(ids > 0.0, ids, 1e6)
            low = there if low is None else jnp.minimum(low, there)
            high = ids if high is None else jnp.maximum(high, ids)
        return jnp.min(low), jnp.max(high)

    def span_left(sections):
        at, rows = table[sections[0]][0], sum(table[l][1] for l in sections)
        ids = left_ids[at : at + rows, :TAGS]
        return jnp.min(ids), jnp.max(ids)

    if first:
        left_best[...] = jnp.full(left_best.shape, FILL, jnp.float32)
    for number, section in fresh.items():
        at = table[number][0]
        for piece in section:
            index, start, rows = piece
            left[at : at + rows, :] = given[index][start : start + rows, :]
            left_ids[at : at + rows, :TAGS] = jnp.transpose(ids_of(piece))
            at += rows

    tested = [(r, l) for r, l, _, test in pairs if test]
    right_span = {r: span_right(rights[r[0]]) for r in sorted({r for r, _ in tested})}
    left_span = {l: span_left(l) for l in sorted({l for _, l in tested})}
    wanted = {(r, l): overlap(right_span[r], left_span[l]) for r, l in tested}

    right_at, at = [], 0
    for section in rights:
        right_at.append((at, padded(section)))
        at += padded(section)

    def fill_right(number):
        at = right_at[number][0]
        for piece in rights[number]:
            index, start, rows = piece
            right[at : at + rows, :] = given[index][start : start + rows, :]
            right_ids[:, at : at + rows] = ids_of(piece)
            at += rows

    right_best[...] = jnp.full(right_best.shape, FILL, jnp.float32)
    right_ids[...] = jnp.full(right_ids.shape, -1.0, jnp.float32)
    for number in range(len(rights)):
        uses = [p for p in pairs if number in p[0]]
        load = functools.partial(fill_right, number)
        if all(p[3] for p in uses):
            pl.when(functools.reduce(jnp.logical_or, [wanted[p[0], p[1]] for p in uses]))(load)
        else:
            load()

    def score(r, l, same):
        lane, row = right_at[r[0]][0], table[l[0]][0]
        lanes = sum(right_at[i][1] for i in r)
        rows = sum(table[i][1] for i in l)
        step = rows
        while step * lanes > 512 * 1024 and step % 32 == 0:
            step //= 2
        across = slice(lane, lane + lanes)

        def turn(index, _):
            at = pl.multiple_of(row + index * step, 16)
            down = pl.ds(at, step)
            scores = lax.dot_general(
                left[down, :],
                right[across, :],
                (((1,), (1,)), ((), ())),
                preferred_element_type=jnp.float32,
            )
            scores = jnp.where(left_ids[down, :1] == right_ids[:1, across], scores, FILL)
            if same is not None:
                skip, start, count = same
                theirs = lax.broadcasted_iota(jnp.int32, (step, lanes), 0) + (index * step - skip)
                mine = lax.broadcasted_iota(jnp.int32, (step, lanes), 1) - start
                inside = jnp.logical_and(mine >= 0, mine < count)
                scores = jnp.where(jnp.logical_and(theirs == mine, inside), FILL, scores)
            left_best[down, :] = jnp.maximum(left_best[down, :], lane_fold(scores))
            right_best[:, across] = jnp.maximum(right_best[:, across], column_fold(scores))
            return 0

        lax.fori_loop(0, rows // step, turn, 0)

    for r, l, same, test in pairs:
        run = functools.partial(score, r, l, same)
        if test:
            pl.when(wanted[r, l])(run)
        else:
            run()
    right_out[...] = jnp.max(right_best[...], axis=0, keepdims=True)
    if last:
        outs[4][...] = jnp.max(jnp.transpose(left_best[...]), axis=0, keepdims=True)


def meet(table, state, fresh, rights, pairs, last=False, earlier=()):
    blocks = []

    def plan(section):
        pieces = []
        for block, start, rows, _ in section:
            known = [i for i, b in enumerate(blocks) if b is block]
            if not known:
                blocks.append(block)
            pieces.append((known[0] if known else len(blocks) - 1, start, rows))
        return pieces

    def goals(section):
        filler = padded(section) - sum(p[2] for p in section)
        return [(p[3], p[2]) for p in section] + [(None, filler)]

    plan_left = {number: plan(section) for number, section in fresh.items()}
    plan_right = [plan(section) for section in rights]
    width = blocks[0].shape[1]
    count = sum(rows for _, rows in table)
    total = sum(padded(section) for section in rights)
    inputs, first = len(blocks), not state
    unread = len(state) + len(earlier)

    def kernel(*refs):
        meet_kernel(
            table, plan_left, plan_right, pairs, inputs, first, last,
            *refs[:inputs], *refs[inputs + unread :]
        )

    outs = [
        pltpu.VMEM((count, width), jnp.bfloat16),
        pltpu.VMEM((count, LANES), jnp.float32),
        pltpu.VMEM((count, LANES), jnp.float32),
        jax.ShapeDtypeStruct((1, total), jnp.float32),
    ]
    if last:
        outs.append(jax.ShapeDtypeStruct((1, count), jnp.float32))
    *state, right_best = pl.pallas_call(
        kernel,
        out_shape=outs,
        in_specs=[WHOLE] * (inputs + len(state)) + [ANYWHERE] * len(earlier),
        out_specs=[WHOLE] * len(outs),
        input_output_aliases={inputs + i: i for i in range(len(state))},
        scratch_shapes=[
            pltpu.VMEM((total, width), jnp.bfloat16),
            pltpu.VMEM((TAGS, total), jnp.float32),
            pltpu.VMEM((8, total), jnp.float32),
        ],
        compiler_params=grant(24),
        cost_estimate=pl.CostEstimate(flops=0, bytes_accessed=0, transcendentals=0),
        name="meet",
    )(*blocks, *state, *earlier)
    found = []
    if last:
        left_best, right_best = right_best, state.pop()
        found = [(left_best, None)]
    return state, [*found, (right_best, sum((goals(section) for section in rights), []))]


def route_kernel(plan, parts, chips, cores, half, near, *refs):
    given, out_ref, gathered = refs[:-2], refs[-2], refs[-1]
    chip, members = lax.axis_index("blk"), chips * cores
    part, me = chip // chips, lax.rem(chip, chips) * cores + lax.axis_index("split")
    slots = 2 * half
    out_ref[...] = jnp.full(out_ref.shape, FILL, jnp.float32)
    gathered[...] = jnp.full(gathered.shape, FILL, jnp.float32)
    starts = {"u": members * parts * slots, "v": members * parts * slots + parts * half}
    for ref, pieces in zip(given, plan):
        at = 0
        for to, entries in pieces:
            if to is not None:
                gathered[:, to : to + entries] = jnp.maximum(
                    gathered[:, to : to + entries], ref[:, at : at + entries]
                )
            at += entries
    for member in range(members):
        whose = lax.bitwise_xor(me, member)
        for k in range(parts):
            at = (member * parts + k) * slots
            source = lax.bitwise_xor(part, k) * members + whose
            out_ref[source, :, :slots] = gathered[:, at : at + slots]
    beyond = lax.rem(part + parts - 1 + 2 * lax.rem(part, 2), parts)
    if near:
        beyond = lax.bitwise_xor(part, 3)
    next_to = lax.bitwise_xor(part, 1)
    from_u = [next_to] + [lax.bitwise_xor(next_to, k) for k in range(2, parts)] + [part]
    from_v = [beyond, lax.bitwise_xor(beyond, 1)]
    from_v += [next_to, part] if near else [lax.bitwise_xor(beyond, k) for k in range(2, parts)]
    for kind, sources, lane in (("u", from_u, slots), ("v", from_v, slots + half)):
        for index, source in enumerate(sources):
            at = starts[kind] + index * half
            out_ref[source * members + me, :, lane : lane + half] = gathered[:, at : at + half]


def back_kernel(parts, members, got_ref, rank_ref, out_ref):
    slots = got_ref.shape[2] // 2
    half = slots // 2
    rows = []
    for part in range(parts):
        best = got_ref[part * members]
        for member in range(1, members):
            best = jnp.maximum(best, got_ref[part * members + member])
        rows.append(best)
    rank = rank_ref[...]
    nothing = jnp.full((1, half), FILL, jnp.float32)
    best = jnp.full((8, rank.shape[1]), FILL, jnp.float32)
    for part in range(parts):
        beyond = part + 1 if part % 2 else part - 1
        there = 0 <= beyond < parts
        faces = jnp.maximum(rows[part][:, :half], rows[part ^ 1][:, slots : slots + half])
        turned = jnp.maximum(
            rows[part][:, half:slots], rows[beyond][:, slots + half :] if there else nothing
        )
        near_u, far_u = faces[:, : half // 2], faces[:, half // 2 :]
        near_v, far_v = turned[:, : half // 2], turned[:, half // 2 :]
        order = [near_u, far_u, far_v, near_v] if part % 2 else [near_v, far_v, far_u, near_u]
        values = spread(jnp.concatenate(order, axis=1))[:, :1]
        slot = lax.broadcasted_iota(jnp.int32, (slots, rank.shape[1]), 0) + part * slots
        best = jnp.maximum(best, column_fold(jnp.where(slot == rank, values, FILL)))
    out_ref[...] = jnp.max(best, axis=0, keepdims=True)


def in_data_order(got, rank, parts, members):
    return pl.pallas_call(
        functools.partial(back_kernel, parts, members),
        out_shape=jax.ShapeDtypeStruct(rank.shape, jnp.float32),
        in_specs=[WHOLE, WHOLE],
        out_specs=WHOLE,
        compiler_params=grant(16),
        name="back",
    )(got, rank)


def body(embeddings, cluster_of, target_pos):
    blocks, cores = lax.axis_size("blk"), lax.axis_size("split")
    rows, width = embeddings.shape
    members = MOST // rows
    chips = members // cores
    parts = blocks // chips
    half = rows // parts // 2
    slots = 2 * half
    def between(array, pairs, name):
        route = [(s * chips + c, t * chips + c) for s, t in pairs for c in range(chips)]
        with jax.named_scope(name):
            return lax.ppermute(array, "blk", route)

    def swap(array, k, name):
        return between(array, [(part, part ^ k) for part in range(parts)], name)

    def chip_swap(array, name):
        with jax.named_scope(name):
            return lax.ppermute(array, "blk", [(b, b ^ 1) for b in range(blocks)])

    def core_swap(array, name):
        with jax.named_scope(name):
            return lax.ppermute(array, "split", [(c, c ^ 1) for c in range(cores)])

    borders = [(p, p + 1) for p in range(1, parts - 1, 2)]
    borders += [(t, s) for s, t in borders]
    near = all(s ^ t == 3 for s, t in borders)

    quart = half // 2
    middle = (parts + 2) // 2
    second, third = [1, *range(2, middle)], list(range(middle, parts))
    u_goal = members * parts * slots
    v_goal = u_goal + parts * half

    def sides(blocks, ks, member=0):
        out = []
        for side in (0, half):
            for m, block in enumerate(blocks, member):
                for i, k in enumerate(ks):
                    goal = (m * parts + k) * slots + side
                    out.append((block, i * slots + side, half, goal))
        return out[: len(out) // 2], out[len(out) // 2 :]

    def whole(block, ks):
        return [(block, i * slots, slots, k * slots) for i, k in enumerate(ks)]

    def visits(pieces, goal):
        near_rows = [(b, at, quart, goal + i * half) for b, at, i in pieces]
        far_rows = [(b, at + quart, quart, goal + i * half + quart) for b, at, i in pieces]
        return near_rows, far_rows

    sent, rank = in_order(
        embeddings, cluster_of, target_pos, [TAGS if k < middle else 2 * TAGS for k in range(parts)], chips
    )
    own_0 = sent[0]
    got = [swap(sent[k], k, "rows_2") for k in second]
    over_0 = chip_swap(own_0, "over_0")
    beside_0 = core_swap(own_0, "beside_0")

    def joined(got):
        if len(got) == 1:
            return got[0]
        return pack(got, [[(i, 0, slots) for i in range(len(got))]])[0]

    own_1, own_2 = got[0], joined(got[1:])
    forward = [(len(second) - 1, 0, half)] + [(i, 0, half) for i in range(len(second) - 1)]
    *held, passing = pack(
        [*got[1:], own_0], [forward], held=[sent[k] for k in third], earlier=[over_0]
    )
    got_3 = [swap(b, k, "rows_3") for k, b in zip(third, held)]
    over_1, over_2 = chip_swap(own_1, "over_1"), chip_swap(own_2, "over_2")
    passed_2 = swap(passing, 1, "passed_2")
    across_0 = core_swap(over_0, "across_0")
    beside_1, beside_2 = core_swap(own_1, "beside_1"), core_swap(own_2, "beside_2")

    def pair(member, block_1, block_2):
        return [
            a + b for a, b in zip(sides([block_1], [1], member), sides([block_2], second[1:], member))
        ]

    left_0 = sides([own_0, beside_0, over_0, across_0], [0])
    mine_0, mine_2 = whole(own_0, [0]), sum(pair(0, own_1, own_2), [])
    here_2 = [a + b for a, b in zip(pair(0, own_1, own_2), pair(1, beside_1, beside_2))]
    sizes = [len(third) * members, members, 2 * len(second), 2 * len(second)]
    sizes += [sizes[3], sizes[1], sizes[2], sizes[0]]
    table = [(sum(sizes[:i]) * half, size * half) for i, size in enumerate(sizes)]
    some, mates = len(second) * half, members * half
    state, scores = meet(
        table,
        [],
        {1: left_0[0], 2: here_2[0], 5: left_0[1], 6: here_2[1]},
        [mine_0, mine_2],
        [((0,), (1,), (0, 0, half), False), ((0,), (5,), (0, half, half), False)]
        + [((1,), (1, 2), (mates, 0, some), False), ((1,), (5, 6), (mates, some, some), False)],
    )

    last = len(third)
    own_3 = joined(got_3)
    border = [(last, half, half), (last + 1, half, half)]
    forward = [(i, 0, half) for i in range(last)]
    inputs = [*got_3, own_0, own_1]
    if near:
        inputs.append(sent[2])
        forward.append((last + 2, half, half))
    else:
        border += [(last + 1 + i, half, half) for i in range(1, len(second))]
        border += [(i, half, half) for i in range(last)]
        inputs += got[1:]
    own_3, border, passing = pack(
        inputs, [border, forward], held=[own_3], earlier=[scores[0][0]], spare=TAGS
    )
    over_3 = chip_swap(own_3, "over_3")
    got_border = between(border, borders, "border")
    passed_3 = swap(passing, 1, "passed_3")
    over_1, over_2 = after([over_1, over_2], [own_3, passed_2])
    across_1, across_2 = core_swap(over_1, "across_1"), core_swap(over_2, "across_2")
    beside_3 = core_swap(own_3, "beside_3")
    there_2 = [a + b for a, b in zip(pair(2, over_1, over_2), pair(3, across_1, across_2))]
    visit_2 = [(passed_2, i * half, half, u_goal + i * half) for i in range(len(second))]
    visit_3 = [(sent[1], 0, half, u_goal + (parts - 1) * half)]
    visit_3 += [(passed_3, i * half, half, u_goal + (len(second) + i) * half) for i in range(last)]
    mine_3 = sum(sides([own_3], third), [])
    state, more_scores = meet(
        table,
        state,
        {3: there_2[0], 4: there_2[1]},
        [mine_2, mine_3, visit_2],
        [((0,), (3, 4), None, False), ((1,), (1, 2, 3, 4, 5, 6), None, False)]
        + [((2,), l, None, True) for l in ((1, 2, 3), (4, 5, 6))],
    )
    scores += more_scores

    visit_v = [(got_border, i * half, i) for i in range(2 if near else parts)]
    if near:
        visit_v += [(passed_3, last * half, 2), (held[0], half, 3)]
    visit_v = visits(visit_v, v_goal)
    (over_3,) = after([over_3], [scores[1][0], got_border, passed_3])
    across_3 = core_swap(over_3, "across_3")
    left_3 = sides([own_3, beside_3, over_3, across_3], third)
    some = last * half
    _, more_scores = meet(
        table,
        state,
        {0: left_3[0], 7: left_3[1]},
        [mine_3, visit_2, visit_3, *visit_v],
        [((0, 1, 2), (0,), (0, 0, some), False), ((0, 1, 2), (7,), (0, some, some), False)]
        + [((2,), l, None, True) for l in ((1, 2, 3), (4, 5, 6))]
        + [((r,), l, None, True) for r in (3, 4) for l in ((0, 1, 2, 3), (4, 5, 6, 7))],
        last=True,
    )
    rows_in = [left_3[0], left_0[0], here_2[0], there_2[0], there_2[1], left_0[1], here_2[1], left_3[1]]
    everywhere = [(p[3], p[2]) for section in rows_in for p in section]
    scores += [(best, goals or everywhere) for best, goals in more_scores]
    found = pl.pallas_call(
        functools.partial(
            route_kernel, [goals for _, goals in scores], parts, chips, cores, half, near
        ),
        out_shape=jax.ShapeDtypeStruct((parts * members, 1, 2 * slots), jnp.float32),
        in_specs=[WHOLE] * len(scores),
        out_specs=WHOLE,
        scratch_shapes=[pltpu.VMEM((1, v_goal + parts * half), jnp.float32)],
        compiler_params=grant(8),
        name="route",
    )(*[best for best, _ in scores])
    got = lax.all_to_all(found, ("blk", "split"), split_axis=0, concat_axis=0, tiled=True)
    return in_data_order(got, rank, parts, members).reshape(rows)


def solution(mesh):
    spec = P(("groups", "blk", "split"))
    return jax.shard_map(
        body,
        mesh=mesh,
        in_specs=(P(("groups", "blk", "split"), None), spec, spec),
        out_specs=spec,
        check_vma=False,
    )
```

```python
import functools

import jax
import jax.numpy as jnp
from jax import lax
from jax.experimental import pallas as pl
from jax.experimental.pallas import tpu as pltpu
from jax.sharding import PartitionSpec as P

MOST = 4096
FILL = -4.0
TAGS = 8
LANES = 128
MIB = 1024 * 1024
WHOLE = pl.BlockSpec(memory_space=pltpu.VMEM)
ANYWHERE = pl.BlockSpec(memory_space=pl.ANY)
REMAINS = pl.BlockSpec(memory_space=pltpu.HBM)


def grant(mib):
    return pltpu.CompilerParams(vmem_limit_bytes=mib * MIB)


def spread(row):
    return jnp.transpose(jnp.broadcast_to(row, (LANES, row.shape[1])))


def column_fold(scores):
    rows, columns = scores.shape
    return jnp.max(scores.reshape(rows // 8, 8, columns), axis=0)


def lane_fold(scores):
    best = scores[:, :LANES]
    for at in range(LANES, scores.shape[1], LANES):
        best = jnp.maximum(best, scores[:, at : at + LANES])
    return best


def place_blocks(ks, chips, parts, rank, ids, unit, pick, outs):
    count = unit.shape[0]
    slots = count // parts
    quart = slots // 4
    part = lax.axis_index("blk") // chips
    for j, k in enumerate(ks):
        quarter = lax.bitwise_xor(part, k)
        side = lax.rem(quarter, 2)
        for index, block in enumerate((3 - 3 * side, 2 - side, 3 * side, 1 + side)):
            slot = lax.broadcasted_iota(jnp.int32, (quart, count), 0) + (4 * quarter + block) * quart
            at = j * slots + index * quart
            pick[at : at + quart, :] = jnp.where(slot == rank, 1.0, 0.0).astype(jnp.bfloat16)
    rows = jnp.dot(pick[...], unit[...], preferred_element_type=jnp.float32).astype(jnp.bfloat16)
    marks = jnp.broadcast_to((ids + 1).astype(jnp.bfloat16), (16, count))
    tags = lax.dot_general(
        marks, pick[...], (((1,), (1,)), ((), ())), preferred_element_type=jnp.float32
    ).astype(jnp.bfloat16)
    for j, out in enumerate(outs):
        out[:slots, :] = rows[j * slots : (j + 1) * slots, :]
        out[out.shape[0] - TAGS :, :slots] = tags[:TAGS, j * slots : (j + 1) * slots]


def order_kernel(ks, chips, parts, rows_hbm, ids_hbm, pos_hbm, *refs):
    outs = refs[: len(ks)]
    unit, rank_ref, ids_ref, pick, rows_ref, pos_ref, sems = refs[len(ks) :]
    count = unit.shape[0]
    step = 256
    fetch_pos = pltpu.make_async_copy(pos_hbm, pos_ref, sems.at[0])
    fetch_rows = pltpu.make_async_copy(rows_hbm, rows_ref, sems.at[1])
    fetch_ids = pltpu.make_async_copy(ids_hbm, ids_ref, sems.at[2])
    fetch_pos.start()
    fetch_rows.start()
    fetch_ids.start()
    fetch_pos.wait()
    pos = pos_ref[...].astype(jnp.float32)
    below = jnp.zeros((8, count), jnp.float32)
    for at in range(0, count, step):
        other = spread(pos[:, at : at + step])[:, :1]
        below += jnp.sum(jnp.where(other < pos, 1.0, 0.0).reshape(step // 8, 8, count), axis=0)
    rank = jnp.sum(below, axis=0, keepdims=True).astype(jnp.int32)
    rank_ref[...] = rank
    fetch_rows.wait()
    fetch_ids.wait()
    values = rows_ref[...].astype(jnp.float32)
    total = jnp.sum(values * values, axis=1, keepdims=True)
    unit[...] = (values * lax.rsqrt(total + 1e-06)).astype(jnp.bfloat16)
    place_blocks(ks, chips, parts, rank, ids_ref[...], unit, pick, outs)


def rest_kernel(ks, chips, parts, unit, rank_ref, ids_ref, *refs):
    place_blocks(ks, chips, parts, rank_ref[...], ids_ref[...], unit, refs[-1], refs[:-1])


def in_order(embeddings, ids, pos, tag_rows, chips, soon):
    parts = len(tag_rows)
    count, width = embeddings.shape
    slots = count // parts
    others = [k for k in range(parts) if k not in soon]

    def blocks(ks):
        return [pltpu.VMEM((slots + tag_rows[k], width), jnp.bfloat16) for k in ks]

    given = [embeddings, ids.reshape(1, count), pos.reshape(1, count)]
    row = pltpu.VMEM((1, count), jnp.int32)
    *early, unit, rank, marks = pl.pallas_call(
        functools.partial(order_kernel, soon, chips, parts),
        out_shape=[*blocks(soon), pltpu.VMEM((count, width), jnp.bfloat16), row, row],
        in_specs=[REMAINS] * 3,
        out_specs=[WHOLE] * (len(soon) + 3),
        scratch_shapes=[
            pltpu.VMEM((len(soon) * slots, count), jnp.bfloat16),
            pltpu.VMEM((count, width), jnp.bfloat16),
            pltpu.VMEM((1, count), jnp.int32),
            pltpu.SemaphoreType.DMA((3,)),
        ],
        compiler_params=grant(24),
        name="order",
    )(*[pltpu.with_memory_space_constraint(x, pltpu.HBM) for x in given])
    late = pl.pallas_call(
        functools.partial(rest_kernel, others, chips, parts),
        out_shape=blocks(others),
        in_specs=[WHOLE] * 3,
        out_specs=[WHOLE] * len(others),
        scratch_shapes=[pltpu.VMEM((len(others) * slots, count), jnp.bfloat16)],
        compiler_params=grant(24),
        cost_estimate=pl.CostEstimate(flops=0, bytes_accessed=0, transcendentals=0),
        name="rest",
    )(unit, rank, marks)
    found = dict(zip(soon + others, early + list(late)))
    return [found[k] for k in range(parts)], rank


def pack_kernel(plan, inputs, *refs):
    given, outs = refs[:inputs], refs[-len(plan) :]
    for out, pieces in zip(outs, plan):
        at = 0
        for index, start, rows in pieces:
            ref = given[index]
            out[at : at + rows, :] = ref[start : start + rows, :]
            out[out.shape[0] - TAGS :, at : at + rows] = ref[
                ref.shape[0] - TAGS :, start : start + rows
            ]
            at += rows


def pack(blocks, plan, held=(), earlier=(), spare=0):
    width = blocks[0].shape[1]
    plan = [list(pieces) for pieces in plan]
    outs = [
        jax.ShapeDtypeStruct(
            (sum(p[2] for p in pieces) + TAGS + spare, width), jnp.bfloat16
        )
        for pieces in plan
    ]
    kept = [jax.ShapeDtypeStruct(h.shape, h.dtype) for h in held]

    def kernel(*refs):
        given = refs[: len(blocks)]
        made = refs[len(blocks) + 2 * len(held) + len(earlier) :]
        pack_kernel(plan, len(given), *given, *made)

    return pl.pallas_call(
        kernel,
        out_shape=kept + outs,
        in_specs=[WHOLE] * len(blocks) + [ANYWHERE] * (len(held) + len(earlier)),
        out_specs=[ANYWHERE] * len(held) + [WHOLE] * len(outs),
        input_output_aliases={len(blocks) + i: i for i in range(len(held))},
        compiler_params=grant(8),
        name="pack",
    )(*blocks, *held, *earlier)


def after(held, earlier):
    return pl.pallas_call(
        lambda *refs: None,
        out_shape=[jax.ShapeDtypeStruct(h.shape, h.dtype) for h in held],
        in_specs=[ANYWHERE] * (len(held) + len(earlier)),
        out_specs=[ANYWHERE] * len(held),
        input_output_aliases={i: i for i in range(len(held))},
        compiler_params=grant(1),
        name="after",
    )(*held, *earlier)


def padded(section):
    rows = sum(piece[2] for piece in section)
    return -(-rows // LANES) * LANES


def overlap(one, other):
    return jnp.logical_and(one[0] <= other[1], other[0] <= one[1])


def meet_kernel(table, fresh, rights, pairs, inputs, first, last, *refs):
    given, outs = refs[:inputs], refs[inputs:]
    left, left_ids, left_best, right_out = outs[:4]
    right, right_ids, right_best = outs[5:] if last else outs[4:]

    def ids_of(piece):
        ref, start, rows = given[piece[0]], piece[1], piece[2]
        return ref[ref.shape[0] - TAGS :, start : start + rows].astype(jnp.float32)

    def span_right(section):
        low, high = None, None
        for piece in section:
            ids = ids_of(piece)
            there = jnp.where(ids > 0.0, ids, 1e6)
            low = there if low is None else jnp.minimum(low, there)
            high = ids if high is None else jnp.maximum(high, ids)
        return jnp.min(low), jnp.max(high)

    def span_left(sections):
        at, rows = table[sections[0]][0], sum(table[l][1] for l in sections)
        ids = left_ids[at : at + rows, :TAGS]
        return jnp.min(ids), jnp.max(ids)

    if first:
        left_best[...] = jnp.full(left_best.shape, FILL, jnp.float32)
    for number, section in fresh.items():
        at = table[number][0]
        for piece in section:
            index, start, rows = piece
            left[at : at + rows, :] = given[index][start : start + rows, :]
            left_ids[at : at + rows, :TAGS] = jnp.transpose(ids_of(piece))
            at += rows

    tested = [(r, l) for r, l, _, test in pairs if test]
    right_span = {r: span_right(rights[r[0]]) for r in sorted({r for r, _ in tested})}
    left_span = {l: span_left(l) for l in sorted({l for _, l in tested})}
    wanted = {(r, l): overlap(right_span[r], left_span[l]) for r, l in tested}

    right_at, at = [], 0
    for section in rights:
        right_at.append((at, padded(section)))
        at += padded(section)

    def fill_right(number):
        at = right_at[number][0]
        for piece in rights[number]:
            index, start, rows = piece
            right[at : at + rows, :] = given[index][start : start + rows, :]
            right_ids[:, at : at + rows] = ids_of(piece)
            at += rows

    right_best[...] = jnp.full(right_best.shape, FILL, jnp.float32)
    right_ids[...] = jnp.full(right_ids.shape, -1.0, jnp.float32)
    for number in range(len(rights)):
        uses = [p for p in pairs if number in p[0]]
        load = functools.partial(fill_right, number)
        if all(p[3] for p in uses):
            pl.when(functools.reduce(jnp.logical_or, [wanted[p[0], p[1]] for p in uses]))(load)
        else:
            load()

    def score(r, l, same):
        lane, row = right_at[r[0]][0], table[l[0]][0]
        lanes = sum(right_at[i][1] for i in r)
        rows = sum(table[i][1] for i in l)
        step = rows
        while step * lanes > 512 * 1024 and step % 32 == 0:
            step //= 2
        across = slice(lane, lane + lanes)

        def turn(index, _):
            at = pl.multiple_of(row + index * step, 16)
            down = pl.ds(at, step)
            scores = lax.dot_general(
                left[down, :],
                right[across, :],
                (((1,), (1,)), ((), ())),
                preferred_element_type=jnp.float32,
            )
            scores = jnp.where(left_ids[down, :1] == right_ids[:1, across], scores, FILL)
            if same is not None:
                skip, start, count = same
                theirs = lax.broadcasted_iota(jnp.int32, (step, lanes), 0) + (index * step - skip)
                mine = lax.broadcasted_iota(jnp.int32, (step, lanes), 1) - start
                inside = jnp.logical_and(mine >= 0, mine < count)
                scores = jnp.where(jnp.logical_and(theirs == mine, inside), FILL, scores)
            left_best[down, :] = jnp.maximum(left_best[down, :], lane_fold(scores))
            right_best[:, across] = jnp.maximum(right_best[:, across], column_fold(scores))
            return 0

        lax.fori_loop(0, rows // step, turn, 0)

    for r, l, same, test in pairs:
        run = functools.partial(score, r, l, same)
        if test:
            pl.when(wanted[r, l])(run)
        else:
            run()
    right_out[...] = jnp.max(right_best[...], axis=0, keepdims=True)
    if last:
        outs[4][...] = jnp.max(jnp.transpose(left_best[...]), axis=0, keepdims=True)


def meet(table, state, fresh, rights, pairs, last=False, earlier=()):
    blocks = []

    def plan(section):
        pieces = []
        for block, start, rows, _ in section:
            known = [i for i, b in enumerate(blocks) if b is block]
            if not known:
                blocks.append(block)
            pieces.append((known[0] if known else len(blocks) - 1, start, rows))
        return pieces

    def goals(section):
        filler = padded(section) - sum(p[2] for p in section)
        return [(p[3], p[2]) for p in section] + [(None, filler)]

    plan_left = {number: plan(section) for number, section in fresh.items()}
    plan_right = [plan(section) for section in rights]
    width = blocks[0].shape[1]
    count = sum(rows for _, rows in table)
    total = sum(padded(section) for section in rights)
    inputs, first = len(blocks), not state
    unread = len(state) + len(earlier)

    def kernel(*refs):
        meet_kernel(
            table, plan_left, plan_right, pairs, inputs, first, last,
            *refs[:inputs], *refs[inputs + unread :]
        )

    outs = [
        pltpu.VMEM((count, width), jnp.bfloat16),
        pltpu.VMEM((count, LANES), jnp.float32),
        pltpu.VMEM((count, LANES), jnp.float32),
        jax.ShapeDtypeStruct((1, total), jnp.float32),
    ]
    if last:
        outs.append(jax.ShapeDtypeStruct((1, count), jnp.float32))
    *state, right_best = pl.pallas_call(
        kernel,
        out_shape=outs,
        in_specs=[WHOLE] * (inputs + len(state)) + [ANYWHERE] * len(earlier),
        out_specs=[WHOLE] * len(outs),
        input_output_aliases={inputs + i: i for i in range(len(state))},
        scratch_shapes=[
            pltpu.VMEM((total, width), jnp.bfloat16),
            pltpu.VMEM((TAGS, total), jnp.float32),
            pltpu.VMEM((8, total), jnp.float32),
        ],
        compiler_params=grant(24),
        cost_estimate=pl.CostEstimate(flops=0, bytes_accessed=0, transcendentals=0),
        name="meet",
    )(*blocks, *state, *earlier)
    found = []
    if last:
        left_best, right_best = right_best, state.pop()
        found = [(left_best, None)]
    return state, [*found, (right_best, sum((goals(section) for section in rights), []))]


def route_kernel(plan, parts, chips, cores, half, near, *refs):
    given, out_ref, gathered = refs[:-2], refs[-2], refs[-1]
    chip, members = lax.axis_index("blk"), chips * cores
    part, me = chip // chips, lax.rem(chip, chips) * cores + lax.axis_index("split")
    slots = 2 * half
    out_ref[...] = jnp.full(out_ref.shape, FILL, jnp.float32)
    gathered[...] = jnp.full(gathered.shape, FILL, jnp.float32)
    starts = {"u": members * parts * slots, "v": members * parts * slots + parts * half}
    for ref, pieces in zip(given, plan):
        at = 0
        for to, entries in pieces:
            if to is not None:
                gathered[:, to : to + entries] = jnp.maximum(
                    gathered[:, to : to + entries], ref[:, at : at + entries]
                )
            at += entries
    for member in range(members):
        whose = lax.bitwise_xor(me, member)
        for k in range(parts):
            at = (member * parts + k) * slots
            source = lax.bitwise_xor(part, k) * members + whose
            out_ref[source, :, :slots] = gathered[:, at : at + slots]
    beyond = lax.rem(part + parts - 1 + 2 * lax.rem(part, 2), parts)
    if near:
        beyond = lax.bitwise_xor(part, 3)
    next_to = lax.bitwise_xor(part, 1)
    from_u = [next_to] + [lax.bitwise_xor(next_to, k) for k in range(2, parts)] + [part]
    from_v = [beyond, lax.bitwise_xor(beyond, 1)]
    from_v += [next_to, part] if near else [lax.bitwise_xor(beyond, k) for k in range(2, parts)]
    for kind, sources, lane in (("u", from_u, slots), ("v", from_v, slots + half)):
        for index, source in enumerate(sources):
            at = starts[kind] + index * half
            out_ref[source * members + me, :, lane : lane + half] = gathered[:, at : at + half]


def back_kernel(parts, members, got_ref, rank_ref, out_ref):
    slots = got_ref.shape[2] // 2
    half = slots // 2
    rows = []
    for part in range(parts):
        best = got_ref[part * members]
        for member in range(1, members):
            best = jnp.maximum(best, got_ref[part * members + member])
        rows.append(best)
    rank = rank_ref[...]
    nothing = jnp.full((1, half), FILL, jnp.float32)
    best = jnp.full((8, rank.shape[1]), FILL, jnp.float32)
    for part in range(parts):
        beyond = part + 1 if part % 2 else part - 1
        there = 0 <= beyond < parts
        faces = jnp.maximum(rows[part][:, :half], rows[part ^ 1][:, slots : slots + half])
        turned = jnp.maximum(
            rows[part][:, half:slots], rows[beyond][:, slots + half :] if there else nothing
        )
        near_u, far_u = faces[:, : half // 2], faces[:, half // 2 :]
        near_v, far_v = turned[:, : half // 2], turned[:, half // 2 :]
        order = [near_u, far_u, far_v, near_v] if part % 2 else [near_v, far_v, far_u, near_u]
        values = spread(jnp.concatenate(order, axis=1))[:, :1]
        slot = lax.broadcasted_iota(jnp.int32, (slots, rank.shape[1]), 0) + part * slots
        best = jnp.maximum(best, column_fold(jnp.where(slot == rank, values, FILL)))
    out_ref[...] = jnp.max(best, axis=0, keepdims=True)


def in_data_order(got, rank, parts, members):
    return pl.pallas_call(
        functools.partial(back_kernel, parts, members),
        out_shape=jax.ShapeDtypeStruct(rank.shape, jnp.float32),
        in_specs=[WHOLE, WHOLE],
        out_specs=WHOLE,
        compiler_params=grant(16),
        name="back",
    )(got, rank)


def body(embeddings, cluster_of, target_pos):
    blocks, cores = lax.axis_size("blk"), lax.axis_size("split")
    rows, width = embeddings.shape
    members = MOST // rows
    chips = members // cores
    parts = blocks // chips
    half = rows // parts // 2
    slots = 2 * half
    def between(array, pairs, name):
        route = [(s * chips + c, t * chips + c) for s, t in pairs for c in range(chips)]
        with jax.named_scope(name):
            return lax.ppermute(array, "blk", route)

    def swap(array, k, name):
        return between(array, [(part, part ^ k) for part in range(parts)], name)

    def chip_swap(array, name):
        with jax.named_scope(name):
            return lax.ppermute(array, "blk", [(b, b ^ 1) for b in range(blocks)])

    def core_swap(array, name):
        with jax.named_scope(name):
            return lax.ppermute(array, "split", [(c, c ^ 1) for c in range(cores)])

    borders = [(p, p + 1) for p in range(1, parts - 1, 2)]
    borders += [(t, s) for s, t in borders]
    near = all(s ^ t == 3 for s, t in borders)

    quart = half // 2
    middle = (parts + 2) // 2
    second, third = [1, *range(2, middle)], list(range(middle, parts))
    u_goal = members * parts * slots
    v_goal = u_goal + parts * half

    def sides(blocks, ks, member=0):
        out = []
        for side in (0, half):
            for m, block in enumerate(blocks, member):
                for i, k in enumerate(ks):
                    goal = (m * parts + k) * slots + side
                    out.append((block, i * slots + side, half, goal))
        return out[: len(out) // 2], out[len(out) // 2 :]

    def whole(block, ks):
        return [(block, i * slots, slots, k * slots) for i, k in enumerate(ks)]

    def visits(pieces, goal):
        near_rows = [(b, at, quart, goal + i * half) for b, at, i in pieces]
        far_rows = [(b, at + quart, quart, goal + i * half + quart) for b, at, i in pieces]
        return near_rows, far_rows

    tag_rows = [TAGS if k < middle else 2 * TAGS for k in range(parts)]
    sent, rank = in_order(embeddings, cluster_of, target_pos, tag_rows, chips, second)
    own_0 = sent[0]
    got = [swap(sent[k], k, "rows_2") for k in second]
    over_0 = chip_swap(own_0, "over_0")
    beside_0 = core_swap(own_0, "beside_0")

    def joined(got):
        if len(got) == 1:
            return got[0]
        return pack(got, [[(i, 0, slots) for i in range(len(got))]])[0]

    own_1, own_2 = got[0], joined(got[1:])
    forward = [(len(second) - 1, 0, half)] + [(i, 0, half) for i in range(len(second) - 1)]
    *held, passing = pack(
        [*got[1:], own_0], [forward], held=[sent[k] for k in third], earlier=[over_0]
    )
    got_3 = [swap(b, k, "rows_3") for k, b in zip(third, held)]
    over_1, over_2 = chip_swap(own_1, "over_1"), chip_swap(own_2, "over_2")
    passed_2 = swap(passing, 1, "passed_2")
    across_0 = core_swap(over_0, "across_0")
    beside_1, beside_2 = core_swap(own_1, "beside_1"), core_swap(own_2, "beside_2")

    def pair(member, block_1, block_2):
        return [
            a + b for a, b in zip(sides([block_1], [1], member), sides([block_2], second[1:], member))
        ]

    left_0 = sides([own_0, beside_0, over_0, across_0], [0])
    mine_0, mine_2 = whole(own_0, [0]), sum(pair(0, own_1, own_2), [])
    here_2 = [a + b for a, b in zip(pair(0, own_1, own_2), pair(1, beside_1, beside_2))]
    sizes = [len(third) * members, members, 2 * len(second), 2 * len(second)]
    sizes += [sizes[3], sizes[1], sizes[2], sizes[0]]
    table = [(sum(sizes[:i]) * half, size * half) for i, size in enumerate(sizes)]
    some, mates = len(second) * half, members * half
    state, scores = meet(
        table,
        [],
        {1: left_0[0], 2: here_2[0], 5: left_0[1], 6: here_2[1]},
        [mine_0, mine_2],
        [((0,), (1,), (0, 0, half), False), ((0,), (5,), (0, half, half), False)]
        + [((1,), (1, 2), (mates, 0, some), False), ((1,), (5, 6), (mates, some, some), False)],
    )

    last = len(third)
    own_3 = joined(got_3)
    border = [(last, half, half), (last + 1, half, half)]
    forward = [(i, 0, half) for i in range(last)]
    inputs = [*got_3, own_0, own_1]
    if near:
        inputs.append(sent[2])
        forward.append((last + 2, half, half))
    else:
        border += [(last + 1 + i, half, half) for i in range(1, len(second))]
        border += [(i, half, half) for i in range(last)]
        inputs += got[1:]
    own_3, border, passing = pack(
        inputs, [border, forward], held=[own_3], earlier=[scores[0][0]], spare=TAGS
    )
    over_3 = chip_swap(own_3, "over_3")
    got_border = between(border, borders, "border")
    passed_3 = swap(passing, 1, "passed_3")
    over_1, over_2 = after([over_1, over_2], [own_3, passed_2])
    across_1, across_2 = core_swap(over_1, "across_1"), core_swap(over_2, "across_2")
    beside_3 = core_swap(own_3, "beside_3")
    there_2 = [a + b for a, b in zip(pair(2, over_1, over_2), pair(3, across_1, across_2))]
    visit_2 = [(passed_2, i * half, half, u_goal + i * half) for i in range(len(second))]
    visit_3 = [(sent[1], 0, half, u_goal + (parts - 1) * half)]
    visit_3 += [(passed_3, i * half, half, u_goal + (len(second) + i) * half) for i in range(last)]
    mine_3 = sum(sides([own_3], third), [])
    state, more_scores = meet(
        table,
        state,
        {3: there_2[0], 4: there_2[1]},
        [mine_2, mine_3, visit_2],
        [((0,), (3, 4), None, False), ((1,), (1, 2, 3, 4, 5, 6), None, False)]
        + [((2,), l, None, True) for l in ((1, 2, 3), (4, 5, 6))],
    )
    scores += more_scores

    visit_v = [(got_border, i * half, i) for i in range(2 if near else parts)]
    if near:
        visit_v += [(passed_3, last * half, 2), (held[0], half, 3)]
    visit_v = visits(visit_v, v_goal)
    (over_3,) = after([over_3], [scores[1][0], got_border, passed_3])
    across_3 = core_swap(over_3, "across_3")
    left_3 = sides([own_3, beside_3, over_3, across_3], third)
    some = last * half
    _, more_scores = meet(
        table,
        state,
        {0: left_3[0], 7: left_3[1]},
        [mine_3, visit_2, visit_3, *visit_v],
        [((0, 1, 2), (0,), (0, 0, some), False), ((0, 1, 2), (7,), (0, some, some), False)]
        + [((2,), l, None, True) for l in ((1, 2, 3), (4, 5, 6))]
        + [((r,), l, None, True) for r in (3, 4) for l in ((0, 1, 2, 3), (4, 5, 6, 7))],
        last=True,
    )
    rows_in = [left_3[0], left_0[0], here_2[0], there_2[0], there_2[1], left_0[1], here_2[1], left_3[1]]
    everywhere = [(p[3], p[2]) for section in rows_in for p in section]
    scores += [(best, goals or everywhere) for best, goals in more_scores]
    found = pl.pallas_call(
        functools.partial(
            route_kernel, [goals for _, goals in scores], parts, chips, cores, half, near
        ),
        out_shape=jax.ShapeDtypeStruct((parts * members, 1, 2 * slots), jnp.float32),
        in_specs=[WHOLE] * len(scores),
        out_specs=WHOLE,
        scratch_shapes=[pltpu.VMEM((1, v_goal + parts * half), jnp.float32)],
        compiler_params=grant(8),
        name="route",
    )(*[best for best, _ in scores])
    got = lax.all_to_all(found, ("blk", "split"), split_axis=0, concat_axis=0, tiled=True)
    return in_data_order(got, rank, parts, members).reshape(rows)


def solution(mesh):
    spec = P(("groups", "blk", "split"))
    return jax.shard_map(
        body,
        mesh=mesh,
        in_specs=(P(("groups", "blk", "split"), None), spec, spec),
        out_specs=spec,
        check_vma=False,
    )
```

```python
import functools

import jax
import jax.numpy as jnp
from jax import lax
from jax.experimental import pallas as pl
from jax.experimental.pallas import tpu as pltpu
from jax.sharding import PartitionSpec as P

MOST = 4096
FILL = -4.0
TAGS = 8
LANES = 128
MIB = 1024 * 1024
WHOLE = pl.BlockSpec(memory_space=pltpu.VMEM)
ANYWHERE = pl.BlockSpec(memory_space=pl.ANY)
REMAINS = pl.BlockSpec(memory_space=pltpu.HBM)


def grant(mib):
    return pltpu.CompilerParams(vmem_limit_bytes=mib * MIB)


def spread(row):
    return jnp.transpose(jnp.broadcast_to(row, (LANES, row.shape[1])))


def column_fold(scores):
    rows, columns = scores.shape
    return jnp.max(scores.reshape(rows // 8, 8, columns), axis=0)


def lane_fold(scores):
    best = scores[:, :LANES]
    for at in range(LANES, scores.shape[1], LANES):
        best = jnp.maximum(best, scores[:, at : at + LANES])
    return best


def place_blocks(ks, chips, parts, rank, ids, unit, pick, outs):
    count = unit.shape[0]
    slots = count // parts
    quart = slots // 4
    part = lax.axis_index("blk") // chips
    for j, k in enumerate(ks):
        quarter = lax.bitwise_xor(part, k)
        side = lax.rem(quarter, 2)
        for index, block in enumerate((3 - 3 * side, 2 - side, 3 * side, 1 + side)):
            slot = lax.broadcasted_iota(jnp.int32, (quart, count), 0) + (4 * quarter + block) * quart
            at = j * slots + index * quart
            pick[at : at + quart, :] = jnp.where(slot == rank, 1.0, 0.0).astype(jnp.bfloat16)
    rows = jnp.dot(pick[...], unit[...], preferred_element_type=jnp.float32).astype(jnp.bfloat16)
    marks = jnp.broadcast_to((ids + 1).astype(jnp.bfloat16), (16, count))
    tags = lax.dot_general(
        marks, pick[...], (((1,), (1,)), ((), ())), preferred_element_type=jnp.float32
    ).astype(jnp.bfloat16)
    for j, out in enumerate(outs):
        out[:slots, :] = rows[j * slots : (j + 1) * slots, :]
        out[out.shape[0] - TAGS :, :slots] = tags[:TAGS, j * slots : (j + 1) * slots]


def order_kernel(ks, chips, parts, rows_hbm, ids_hbm, pos_hbm, *refs):
    outs = refs[: len(ks)]
    unit, rank_ref, ids_ref, pick, rows_ref, pos_ref, sems = refs[len(ks) :]
    count = unit.shape[0]
    step = 256
    fetch_pos = pltpu.make_async_copy(pos_hbm, pos_ref, sems.at[0])
    fetch_rows = pltpu.make_async_copy(rows_hbm, rows_ref, sems.at[1])
    fetch_ids = pltpu.make_async_copy(ids_hbm, ids_ref, sems.at[2])
    fetch_pos.start()
    fetch_rows.start()
    fetch_ids.start()
    fetch_pos.wait()
    pos = pos_ref[...].astype(jnp.float32)
    below = jnp.zeros((8, count), jnp.float32)
    for at in range(0, count, step):
        other = spread(pos[:, at : at + step])[:, :1]
        below += jnp.sum(jnp.where(other < pos, 1.0, 0.0).reshape(step // 8, 8, count), axis=0)
    rank = jnp.sum(below, axis=0, keepdims=True).astype(jnp.int32)
    rank_ref[...] = rank
    fetch_rows.wait()
    fetch_ids.wait()
    values = rows_ref[...].astype(jnp.float32)
    total = jnp.sum(values * values, axis=1, keepdims=True)
    unit[...] = (values * lax.rsqrt(total + 1e-06)).astype(jnp.bfloat16)
    place_blocks(ks, chips, parts, rank, ids_ref[...], unit, pick, outs)


def rest_kernel(ks, chips, parts, unit, rank_ref, ids_ref, *refs):
    place_blocks(ks, chips, parts, rank_ref[...], ids_ref[...], unit, refs[-1], refs[:-1])


def in_order(embeddings, ids, pos, tag_rows, chips, soon):
    parts = len(tag_rows)
    count, width = embeddings.shape
    slots = count // parts
    others = [k for k in range(parts) if k not in soon]

    def blocks(ks):
        return [pltpu.VMEM((slots + tag_rows[k], width), jnp.bfloat16) for k in ks]

    given = [embeddings, ids.reshape(1, count), pos.reshape(1, count)]
    row = pltpu.VMEM((1, count), jnp.int32)
    *early, unit, rank, marks = pl.pallas_call(
        functools.partial(order_kernel, soon, chips, parts),
        out_shape=[*blocks(soon), pltpu.VMEM((count, width), jnp.bfloat16), row, row],
        in_specs=[REMAINS] * 3,
        out_specs=[WHOLE] * (len(soon) + 3),
        scratch_shapes=[
            pltpu.VMEM((len(soon) * slots, count), jnp.bfloat16),
            pltpu.VMEM((count, width), jnp.bfloat16),
            pltpu.VMEM((1, count), jnp.int32),
            pltpu.SemaphoreType.DMA((3,)),
        ],
        compiler_params=grant(24),
        name="order",
    )(*[pltpu.with_memory_space_constraint(x, pltpu.HBM) for x in given])
    late = pl.pallas_call(
        functools.partial(rest_kernel, others, chips, parts),
        out_shape=blocks(others),
        in_specs=[WHOLE] * 3,
        out_specs=[WHOLE] * len(others),
        scratch_shapes=[pltpu.VMEM((len(others) * slots, count), jnp.bfloat16)],
        compiler_params=grant(24),
        cost_estimate=pl.CostEstimate(flops=0, bytes_accessed=0, transcendentals=0),
        name="rest",
    )(unit, rank, marks)
    found = dict(zip(soon + others, early + list(late)))
    return [found[k] for k in range(parts)], rank


def pack_kernel(plan, inputs, *refs):
    given, outs = refs[:inputs], refs[-len(plan) :]
    for out, pieces in zip(outs, plan):
        at = 0
        for index, start, rows in pieces:
            ref = given[index]
            out[at : at + rows, :] = ref[start : start + rows, :]
            out[out.shape[0] - TAGS :, at : at + rows] = ref[
                ref.shape[0] - TAGS :, start : start + rows
            ]
            at += rows


def pack(blocks, plan, held=(), earlier=(), spare=0):
    width = blocks[0].shape[1]
    plan = [list(pieces) for pieces in plan]
    outs = [
        jax.ShapeDtypeStruct(
            (sum(p[2] for p in pieces) + TAGS + spare, width), jnp.bfloat16
        )
        for pieces in plan
    ]
    kept = [jax.ShapeDtypeStruct(h.shape, h.dtype) for h in held]

    def kernel(*refs):
        given = refs[: len(blocks)]
        made = refs[len(blocks) + 2 * len(held) + len(earlier) :]
        pack_kernel(plan, len(given), *given, *made)

    return pl.pallas_call(
        kernel,
        out_shape=kept + outs,
        in_specs=[WHOLE] * len(blocks) + [ANYWHERE] * (len(held) + len(earlier)),
        out_specs=[ANYWHERE] * len(held) + [WHOLE] * len(outs),
        input_output_aliases={len(blocks) + i: i for i in range(len(held))},
        compiler_params=grant(8),
        name="pack",
    )(*blocks, *held, *earlier)


def after(held, earlier):
    return pl.pallas_call(
        lambda *refs: None,
        out_shape=[jax.ShapeDtypeStruct(h.shape, h.dtype) for h in held],
        in_specs=[ANYWHERE] * (len(held) + len(earlier)),
        out_specs=[ANYWHERE] * len(held),
        input_output_aliases={i: i for i in range(len(held))},
        compiler_params=grant(1),
        name="after",
    )(*held, *earlier)


def padded(section):
    rows = sum(piece[2] for piece in section)
    return -(-rows // LANES) * LANES


def overlap(one, other):
    return jnp.logical_and(one[0] <= other[1], other[0] <= one[1])


def meet_kernel(table, fresh, rights, pairs, inputs, first, last, *refs):
    given, outs = refs[:inputs], refs[inputs:]
    left, left_ids, left_best, right_out = outs[:4]
    right, right_ids, right_best = outs[5:] if last else outs[4:]

    def ids_of(piece):
        ref, start, rows = given[piece[0]], piece[1], piece[2]
        return ref[ref.shape[0] - TAGS :, start : start + rows].astype(jnp.float32)

    def span_right(section):
        low, high = None, None
        for piece in section:
            ids = ids_of(piece)
            there = jnp.where(ids > 0.0, ids, 1e6)
            low = there if low is None else jnp.minimum(low, there)
            high = ids if high is None else jnp.maximum(high, ids)
        return jnp.min(low), jnp.max(high)

    def span_left(sections):
        lows, highs = zip(*[section_span[l] for l in sections])
        return functools.reduce(jnp.minimum, lows), functools.reduce(jnp.maximum, highs)

    if first:
        left_best[...] = jnp.full(left_best.shape, FILL, jnp.float32)
    for number, section in fresh.items():
        at = table[number][0]
        for piece in section:
            index, start, rows = piece
            left[at : at + rows, :] = given[index][start : start + rows, :]
            left_ids[at : at + rows, :TAGS] = jnp.transpose(ids_of(piece))
            at += rows

    tested = [(r, l) for r, l, _, test in pairs if test]
    right_span = {r: span_right(rights[r[0]]) for r in sorted({r for r, _ in tested})}
    section_span = {}
    for l in sorted({i for _, group in tested for i in group}):
        at, rows = table[l]
        ids = left_ids[at : at + rows, :TAGS]
        section_span[l] = jnp.min(ids), jnp.max(ids)
    left_span = {l: span_left(l) for l in sorted({l for _, l in tested})}
    wanted = {(r, l): overlap(right_span[r], left_span[l]) for r, l in tested}

    right_at, at = [], 0
    for section in rights:
        right_at.append((at, padded(section)))
        at += padded(section)

    def fill_right(number):
        at = right_at[number][0]
        for piece in rights[number]:
            index, start, rows = piece
            right[at : at + rows, :] = given[index][start : start + rows, :]
            right_ids[:, at : at + rows] = ids_of(piece)
            at += rows

    right_best[...] = jnp.full(right_best.shape, FILL, jnp.float32)
    right_ids[...] = jnp.full(right_ids.shape, -1.0, jnp.float32)
    for number in range(len(rights)):
        uses = [p for p in pairs if number in p[0]]
        load = functools.partial(fill_right, number)
        if all(p[3] for p in uses):
            pl.when(functools.reduce(jnp.logical_or, [wanted[p[0], p[1]] for p in uses]))(load)
        else:
            load()

    def score(r, l, same):
        lane, row = right_at[r[0]][0], table[l[0]][0]
        lanes = sum(right_at[i][1] for i in r)
        rows = sum(table[i][1] for i in l)
        step = rows
        while step * lanes > 512 * 1024 and step % 32 == 0:
            step //= 2
        across = slice(lane, lane + lanes)

        def turn(index, _):
            at = pl.multiple_of(row + index * step, 16)
            down = pl.ds(at, step)
            scores = lax.dot_general(
                left[down, :],
                right[across, :],
                (((1,), (1,)), ((), ())),
                preferred_element_type=jnp.float32,
            )
            scores = jnp.where(left_ids[down, :1] == right_ids[:1, across], scores, FILL)
            if same is not None:
                skip, start, count = same
                theirs = lax.broadcasted_iota(jnp.int32, (step, lanes), 0) + (index * step - skip)
                mine = lax.broadcasted_iota(jnp.int32, (step, lanes), 1) - start
                inside = jnp.logical_and(mine >= 0, mine < count)
                scores = jnp.where(jnp.logical_and(theirs == mine, inside), FILL, scores)
            left_best[down, :] = jnp.maximum(left_best[down, :], lane_fold(scores))
            right_best[:, across] = jnp.maximum(right_best[:, across], column_fold(scores))
            return 0

        lax.fori_loop(0, rows // step, turn, 0)

    for r, l, same, test in pairs:
        run = functools.partial(score, r, l, same)
        if test:
            pl.when(wanted[r, l])(run)
        else:
            run()
    right_out[...] = jnp.max(right_best[...], axis=0, keepdims=True)
    if last:
        outs[4][...] = jnp.max(jnp.transpose(left_best[...]), axis=0, keepdims=True)


def meet(table, state, fresh, rights, pairs, last=False, earlier=()):
    blocks = []

    def plan(section):
        pieces = []
        for block, start, rows, _ in section:
            known = [i for i, b in enumerate(blocks) if b is block]
            if not known:
                blocks.append(block)
            pieces.append((known[0] if known else len(blocks) - 1, start, rows))
        return pieces

    def goals(section):
        filler = padded(section) - sum(p[2] for p in section)
        return [(p[3], p[2]) for p in section] + [(None, filler)]

    plan_left = {number: plan(section) for number, section in fresh.items()}
    plan_right = [plan(section) for section in rights]
    width = blocks[0].shape[1]
    count = sum(rows for _, rows in table)
    total = sum(padded(section) for section in rights)
    inputs, first = len(blocks), not state
    unread = len(state) + len(earlier)

    def kernel(*refs):
        meet_kernel(
            table, plan_left, plan_right, pairs, inputs, first, last,
            *refs[:inputs], *refs[inputs + unread :]
        )

    outs = [
        pltpu.VMEM((count, width), jnp.bfloat16),
        pltpu.VMEM((count, LANES), jnp.float32),
        pltpu.VMEM((count, LANES), jnp.float32),
        jax.ShapeDtypeStruct((1, total), jnp.float32),
    ]
    if last:
        outs.append(jax.ShapeDtypeStruct((1, count), jnp.float32))
    *state, right_best = pl.pallas_call(
        kernel,
        out_shape=outs,
        in_specs=[WHOLE] * (inputs + len(state)) + [ANYWHERE] * len(earlier),
        out_specs=[WHOLE] * len(outs),
        input_output_aliases={inputs + i: i for i in range(len(state))},
        scratch_shapes=[
            pltpu.VMEM((total, width), jnp.bfloat16),
            pltpu.VMEM((TAGS, total), jnp.float32),
            pltpu.VMEM((8, total), jnp.float32),
        ],
        compiler_params=grant(24),
        cost_estimate=pl.CostEstimate(flops=0, bytes_accessed=0, transcendentals=0),
        name="meet",
    )(*blocks, *state, *earlier)
    found = []
    if last:
        left_best, right_best = right_best, state.pop()
        found = [(left_best, None)]
    return state, [*found, (right_best, sum((goals(section) for section in rights), []))]


def route_kernel(plan, parts, chips, cores, half, near, *refs):
    given, out_ref, gathered = refs[:-2], refs[-2], refs[-1]
    chip, members = lax.axis_index("blk"), chips * cores
    part, me = chip // chips, lax.rem(chip, chips) * cores + lax.axis_index("split")
    slots = 2 * half
    out_ref[...] = jnp.full(out_ref.shape, FILL, jnp.float32)
    gathered[...] = jnp.full(gathered.shape, FILL, jnp.float32)
    starts = {"u": members * parts * slots, "v": members * parts * slots + parts * half}
    for ref, pieces in zip(given, plan):
        at = 0
        for to, entries in pieces:
            if to is not None:
                gathered[:, to : to + entries] = jnp.maximum(
                    gathered[:, to : to + entries], ref[:, at : at + entries]
                )
            at += entries
    for member in range(members):
        whose = lax.bitwise_xor(me, member)
        for k in range(parts):
            at = (member * parts + k) * slots
            source = lax.bitwise_xor(part, k) * members + whose
            out_ref[source, :, :slots] = gathered[:, at : at + slots]
    beyond = lax.rem(part + parts - 1 + 2 * lax.rem(part, 2), parts)
    if near:
        beyond = lax.bitwise_xor(part, 3)
    next_to = lax.bitwise_xor(part, 1)
    from_u = [next_to] + [lax.bitwise_xor(next_to, k) for k in range(2, parts)] + [part]
    from_v = [beyond, lax.bitwise_xor(beyond, 1)]
    from_v += [next_to, part] if near else [lax.bitwise_xor(beyond, k) for k in range(2, parts)]
    for kind, sources, lane in (("u", from_u, slots), ("v", from_v, slots + half)):
        for index, source in enumerate(sources):
            at = starts[kind] + index * half
            out_ref[source * members + me, :, lane : lane + half] = gathered[:, at : at + half]


def back_kernel(parts, members, got_ref, rank_ref, out_ref):
    slots = got_ref.shape[2] // 2
    half = slots // 2
    rows = []
    for part in range(parts):
        best = got_ref[part * members]
        for member in range(1, members):
            best = jnp.maximum(best, got_ref[part * members + member])
        rows.append(best)
    rank = rank_ref[...]
    nothing = jnp.full((1, half), FILL, jnp.float32)
    best = jnp.full((8, rank.shape[1]), FILL, jnp.float32)
    for part in range(parts):
        beyond = part + 1 if part % 2 else part - 1
        there = 0 <= beyond < parts
        faces = jnp.maximum(rows[part][:, :half], rows[part ^ 1][:, slots : slots + half])
        turned = jnp.maximum(
            rows[part][:, half:slots], rows[beyond][:, slots + half :] if there else nothing
        )
        near_u, far_u = faces[:, : half // 2], faces[:, half // 2 :]
        near_v, far_v = turned[:, : half // 2], turned[:, half // 2 :]
        order = [near_u, far_u, far_v, near_v] if part % 2 else [near_v, far_v, far_u, near_u]
        values = spread(jnp.concatenate(order, axis=1))[:, :1]
        slot = lax.broadcasted_iota(jnp.int32, (slots, rank.shape[1]), 0) + part * slots
        best = jnp.maximum(best, column_fold(jnp.where(slot == rank, values, FILL)))
    out_ref[...] = jnp.max(best, axis=0, keepdims=True)


def in_data_order(got, rank, parts, members):
    return pl.pallas_call(
        functools.partial(back_kernel, parts, members),
        out_shape=jax.ShapeDtypeStruct(rank.shape, jnp.float32),
        in_specs=[WHOLE, WHOLE],
        out_specs=WHOLE,
        compiler_params=grant(16),
        name="back",
    )(got, rank)


def body(embeddings, cluster_of, target_pos):
    blocks, cores = lax.axis_size("blk"), lax.axis_size("split")
    rows, width = embeddings.shape
    members = MOST // rows
    chips = members // cores
    parts = blocks // chips
    half = rows // parts // 2
    slots = 2 * half
    def between(array, pairs, name):
        route = [(s * chips + c, t * chips + c) for s, t in pairs for c in range(chips)]
        with jax.named_scope(name):
            return lax.ppermute(array, "blk", route)

    def swap(array, k, name):
        return between(array, [(part, part ^ k) for part in range(parts)], name)

    def chip_swap(array, name):
        with jax.named_scope(name):
            return lax.ppermute(array, "blk", [(b, b ^ 1) for b in range(blocks)])

    def core_swap(array, name):
        with jax.named_scope(name):
            return lax.ppermute(array, "split", [(c, c ^ 1) for c in range(cores)])

    borders = [(p, p + 1) for p in range(1, parts - 1, 2)]
    borders += [(t, s) for s, t in borders]
    near = all(s ^ t == 3 for s, t in borders)

    quart = half // 2
    middle = (parts + 2) // 2
    second, third = [1, *range(2, middle)], list(range(middle, parts))
    u_goal = members * parts * slots
    v_goal = u_goal + parts * half

    def sides(blocks, ks, member=0):
        out = []
        for side in (0, half):
            for m, block in enumerate(blocks, member):
                for i, k in enumerate(ks):
                    goal = (m * parts + k) * slots + side
                    out.append((block, i * slots + side, half, goal))
        return out[: len(out) // 2], out[len(out) // 2 :]

    def whole(block, ks):
        return [(block, i * slots, slots, k * slots) for i, k in enumerate(ks)]

    def visits(pieces, goal):
        near_rows = [(b, at, quart, goal + i * half) for b, at, i in pieces]
        far_rows = [(b, at + quart, quart, goal + i * half + quart) for b, at, i in pieces]
        return near_rows, far_rows

    tag_rows = [TAGS if k < middle else 2 * TAGS for k in range(parts)]
    sent, rank = in_order(embeddings, cluster_of, target_pos, tag_rows, chips, [*second, *third])
    own_0 = sent[0]
    got = [swap(sent[k], k, "rows_2") for k in second]
    over_0 = chip_swap(own_0, "over_0")
    beside_0 = core_swap(own_0, "beside_0")

    def joined(got):
        if len(got) == 1:
            return got[0]
        return pack(got, [[(i, 0, slots) for i in range(len(got))]])[0]

    own_1, own_2 = got[0], joined(got[1:])
    forward = [(len(second) - 1, 0, half)] + [(i, 0, half) for i in range(len(second) - 1)]
    *held, passing = pack(
        [*got[1:], own_0], [forward], held=[sent[k] for k in third], earlier=[over_0]
    )
    got_3 = [swap(b, k, "rows_3") for k, b in zip(third, held)]
    over_1, over_2 = chip_swap(own_1, "over_1"), chip_swap(own_2, "over_2")
    passed_2 = swap(passing, 1, "passed_2")
    across_0 = core_swap(over_0, "across_0")
    beside_1, beside_2 = core_swap(own_1, "beside_1"), core_swap(own_2, "beside_2")

    def pair(member, block_1, block_2):
        return [
            a + b for a, b in zip(sides([block_1], [1], member), sides([block_2], second[1:], member))
        ]

    left_0 = sides([own_0, beside_0, over_0, across_0], [0])
    mine_0, mine_2 = whole(own_0, [0]), sum(pair(0, own_1, own_2), [])
    here_2 = [a + b for a, b in zip(pair(0, own_1, own_2), pair(1, beside_1, beside_2))]
    sizes = [len(third) * members, members, 2 * len(second), 2 * len(second)]
    sizes += [sizes[3], sizes[1], sizes[2], sizes[0]]
    table = [(sum(sizes[:i]) * half, size * half) for i, size in enumerate(sizes)]
    some, mates = len(second) * half, members * half
    state, scores = meet(
        table,
        [],
        {1: left_0[0], 2: here_2[0], 5: left_0[1], 6: here_2[1]},
        [mine_0, mine_2],
        [((0,), (1,), (0, 0, half), False), ((0,), (5,), (0, half, half), False)]
        + [((1,), (1, 2), (mates, 0, some), False), ((1,), (5, 6), (mates, some, some), False)],
    )

    last = len(third)
    own_3 = joined(got_3)
    border = [(last, half, half), (last + 1, half, half)]
    forward = [(i, 0, half) for i in range(last)]
    inputs = [*got_3, own_0, own_1]
    if near:
        inputs.append(sent[2])
        forward.append((last + 2, half, half))
    else:
        border += [(last + 1 + i, half, half) for i in range(1, len(second))]
        border += [(i, half, half) for i in range(last)]
        inputs += got[1:]
    own_3, border, passing = pack(
        inputs, [border, forward], held=[own_3], earlier=[scores[0][0]], spare=TAGS
    )
    over_3 = chip_swap(own_3, "over_3")
    got_border = between(border, borders, "border")
    passed_3 = swap(passing, 1, "passed_3")
    over_1, over_2 = after([over_1, over_2], [own_3, passed_2])
    across_1, across_2 = core_swap(over_1, "across_1"), core_swap(over_2, "across_2")
    beside_3 = core_swap(own_3, "beside_3")
    there_2 = [a + b for a, b in zip(pair(2, over_1, over_2), pair(3, across_1, across_2))]
    visit_2 = [(passed_2, i * half, half, u_goal + i * half) for i in range(len(second))]
    visit_3 = [(sent[1], 0, half, u_goal + (parts - 1) * half)]
    visit_3 += [(passed_3, i * half, half, u_goal + (len(second) + i) * half) for i in range(last)]
    mine_3 = sum(sides([own_3], third), [])
    state, more_scores = meet(
        table,
        state,
        {3: there_2[0], 4: there_2[1]},
        [mine_2, mine_3, visit_2],
        [((0,), (3, 4), None, False), ((1,), (1, 2, 3, 4, 5, 6), None, False)]
        + [((2,), l, None, True) for l in ((1, 2, 3), (4, 5, 6))],
    )
    scores += more_scores

    visit_v = [(got_border, i * half, i) for i in range(2 if near else parts)]
    if near:
        visit_v += [(passed_3, last * half, 2), (held[0], half, 3)]
    visit_v = visits(visit_v, v_goal)
    (over_3,) = after([over_3], [scores[1][0], got_border, passed_3])
    across_3 = core_swap(over_3, "across_3")
    left_3 = sides([own_3, beside_3, over_3, across_3], third)
    some = last * half
    _, more_scores = meet(
        table,
        state,
        {0: left_3[0], 7: left_3[1]},
        [mine_3, visit_2, visit_3, *visit_v],
        [((0, 1, 2), (0,), (0, 0, some), False), ((0, 1, 2), (7,), (0, some, some), False)]
        + [((2,), l, None, True) for l in ((1, 2, 3), (4, 5, 6))]
        + [((r,), l, None, True) for r in (3, 4) for l in ((0, 1, 2, 3), (4, 5, 6, 7))],
        last=True,
    )
    rows_in = [left_3[0], left_0[0], here_2[0], there_2[0], there_2[1], left_0[1], here_2[1], left_3[1]]
    everywhere = [(p[3], p[2]) for section in rows_in for p in section]
    scores += [(best, goals or everywhere) for best, goals in more_scores]
    found = pl.pallas_call(
        functools.partial(
            route_kernel, [goals for _, goals in scores], parts, chips, cores, half, near
        ),
        out_shape=jax.ShapeDtypeStruct((parts * members, 1, 2 * slots), jnp.float32),
        in_specs=[WHOLE] * len(scores),
        out_specs=WHOLE,
        scratch_shapes=[pltpu.VMEM((1, v_goal + parts * half), jnp.float32)],
        compiler_params=grant(8),
        name="route",
    )(*[best for best, _ in scores])
    got = lax.all_to_all(found, ("blk", "split"), split_axis=0, concat_axis=0, tiled=True)
    return in_data_order(got, rank, parts, members).reshape(rows)


def solution(mesh):
    spec = P(("groups", "blk", "split"))
    return jax.shard_map(
        body,
        mesh=mesh,
        in_specs=(P(("groups", "blk", "split"), None), spec, spec),
        out_specs=spec,
        check_vma=False,
    )
```

```python
import functools

import jax
import jax.numpy as jnp
from jax import lax
from jax.experimental import pallas as pl
from jax.experimental.pallas import tpu as pltpu
from jax.sharding import PartitionSpec as P

MOST = 4096
FILL = -4.0
TAGS = 8
LANES = 128
MIB = 1024 * 1024
WHOLE = pl.BlockSpec(memory_space=pltpu.VMEM)
ANYWHERE = pl.BlockSpec(memory_space=pl.ANY)
REMAINS = pl.BlockSpec(memory_space=pltpu.HBM)


def grant(mib):
    return pltpu.CompilerParams(vmem_limit_bytes=mib * MIB)


def spread(row):
    return jnp.transpose(jnp.broadcast_to(row, (LANES, row.shape[1])))


def column_fold(scores):
    rows, columns = scores.shape
    return jnp.max(scores.reshape(rows // 8, 8, columns), axis=0)


def lane_fold(scores):
    best = scores[:, :LANES]
    for at in range(LANES, scores.shape[1], LANES):
        best = jnp.maximum(best, scores[:, at : at + LANES])
    return best


def place_blocks(ks, chips, parts, rank, ids, unit, pick, outs):
    count = unit.shape[0]
    slots = count // parts
    quart = slots // 4
    part = lax.axis_index("blk") // chips
    for j, k in enumerate(ks):
        quarter = lax.bitwise_xor(part, k)
        side = lax.rem(quarter, 2)
        for index, block in enumerate((3 - 3 * side, 2 - side, 3 * side, 1 + side)):
            slot = lax.broadcasted_iota(jnp.int32, (quart, count), 0) + (4 * quarter + block) * quart
            at = j * slots + index * quart
            pick[at : at + quart, :] = jnp.where(slot == rank, 1.0, 0.0).astype(jnp.bfloat16)
    rows = jnp.dot(pick[...], unit[...], preferred_element_type=jnp.float32).astype(jnp.bfloat16)
    marks = jnp.broadcast_to((ids + 1).astype(jnp.bfloat16), (16, count))
    tags = lax.dot_general(
        marks, pick[...], (((1,), (1,)), ((), ())), preferred_element_type=jnp.float32
    ).astype(jnp.bfloat16)
    for j, out in enumerate(outs):
        out[:slots, :] = rows[j * slots : (j + 1) * slots, :]
        out[out.shape[0] - TAGS :, :slots] = tags[:TAGS, j * slots : (j + 1) * slots]


def order_kernel(ks, chips, parts, rows_hbm, ids_hbm, pos_hbm, *refs):
    outs = refs[: len(ks)]
    unit, rank_ref, ids_ref, pick, rows_ref, pos_ref, sems = refs[len(ks) :]
    count = unit.shape[0]
    step = 256
    fetch_pos = pltpu.make_async_copy(pos_hbm, pos_ref, sems.at[0])
    fetch_rows = pltpu.make_async_copy(rows_hbm, rows_ref, sems.at[1])
    fetch_ids = pltpu.make_async_copy(ids_hbm, ids_ref, sems.at[2])
    fetch_pos.start()
    fetch_rows.start()
    fetch_ids.start()
    fetch_pos.wait()
    pos = pos_ref[...].astype(jnp.float32)
    below = jnp.zeros((8, count), jnp.float32)
    for at in range(0, count, step):
        other = spread(pos[:, at : at + step])[:, :1]
        below += jnp.sum(jnp.where(other < pos, 1.0, 0.0).reshape(step // 8, 8, count), axis=0)
    rank = jnp.sum(below, axis=0, keepdims=True).astype(jnp.int32)
    rank_ref[...] = rank
    fetch_rows.wait()
    fetch_ids.wait()
    values = rows_ref[...].astype(jnp.float32)
    total = jnp.sum(values * values, axis=1, keepdims=True)
    unit[...] = (values * lax.rsqrt(total + 1e-06)).astype(jnp.bfloat16)
    place_blocks(ks, chips, parts, rank, ids_ref[...], unit, pick, outs)


def rest_kernel(ks, chips, parts, unit, rank_ref, ids_ref, *refs):
    place_blocks(ks, chips, parts, rank_ref[...], ids_ref[...], unit, refs[-1], refs[:-1])


def in_order(embeddings, ids, pos, tag_rows, chips, soon):
    parts = len(tag_rows)
    count, width = embeddings.shape
    slots = count // parts
    others = [k for k in range(parts) if k not in soon]

    def blocks(ks):
        return [pltpu.VMEM((slots + tag_rows[k], width), jnp.bfloat16) for k in ks]

    given = [embeddings, ids.reshape(1, count), pos.reshape(1, count)]
    row = pltpu.VMEM((1, count), jnp.int32)
    *early, unit, rank, marks = pl.pallas_call(
        functools.partial(order_kernel, soon, chips, parts),
        out_shape=[*blocks(soon), pltpu.VMEM((count, width), jnp.bfloat16), row, row],
        in_specs=[REMAINS] * 3,
        out_specs=[WHOLE] * (len(soon) + 3),
        scratch_shapes=[
            pltpu.VMEM((len(soon) * slots, count), jnp.bfloat16),
            pltpu.VMEM((count, width), jnp.bfloat16),
            pltpu.VMEM((1, count), jnp.int32),
            pltpu.SemaphoreType.DMA((3,)),
        ],
        compiler_params=grant(24),
        name="order",
    )(*[pltpu.with_memory_space_constraint(x, pltpu.HBM) for x in given])
    late = pl.pallas_call(
        functools.partial(rest_kernel, others, chips, parts),
        out_shape=blocks(others),
        in_specs=[WHOLE] * 3,
        out_specs=[WHOLE] * len(others),
        scratch_shapes=[pltpu.VMEM((len(others) * slots, count), jnp.bfloat16)],
        compiler_params=grant(24),
        cost_estimate=pl.CostEstimate(flops=0, bytes_accessed=0, transcendentals=0),
        name="rest",
    )(unit, rank, marks)
    found = dict(zip(soon + others, early + list(late)))
    return [found[k] for k in range(parts)], rank


def pack_kernel(plan, inputs, *refs):
    given, outs = refs[:inputs], refs[-len(plan) :]
    for out, pieces in zip(outs, plan):
        at = 0
        for index, start, rows in pieces:
            ref = given[index]
            out[at : at + rows, :] = ref[start : start + rows, :]
            out[out.shape[0] - TAGS :, at : at + rows] = ref[
                ref.shape[0] - TAGS :, start : start + rows
            ]
            at += rows


def pack(blocks, plan, held=(), earlier=(), spare=0):
    width = blocks[0].shape[1]
    plan = [list(pieces) for pieces in plan]
    outs = [
        jax.ShapeDtypeStruct(
            (sum(p[2] for p in pieces) + TAGS + spare, width), jnp.bfloat16
        )
        for pieces in plan
    ]
    kept = [jax.ShapeDtypeStruct(h.shape, h.dtype) for h in held]

    def kernel(*refs):
        given = refs[: len(blocks)]
        made = refs[len(blocks) + 2 * len(held) + len(earlier) :]
        pack_kernel(plan, len(given), *given, *made)

    return pl.pallas_call(
        kernel,
        out_shape=kept + outs,
        in_specs=[WHOLE] * len(blocks) + [ANYWHERE] * (len(held) + len(earlier)),
        out_specs=[ANYWHERE] * len(held) + [WHOLE] * len(outs),
        input_output_aliases={len(blocks) + i: i for i in range(len(held))},
        compiler_params=grant(8),
        name="pack",
    )(*blocks, *held, *earlier)


def after(held, earlier):
    return pl.pallas_call(
        lambda *refs: None,
        out_shape=[jax.ShapeDtypeStruct(h.shape, h.dtype) for h in held],
        in_specs=[ANYWHERE] * (len(held) + len(earlier)),
        out_specs=[ANYWHERE] * len(held),
        input_output_aliases={i: i for i in range(len(held))},
        compiler_params=grant(1),
        name="after",
    )(*held, *earlier)


def padded(section):
    rows = sum(piece[2] for piece in section)
    return -(-rows // LANES) * LANES


def overlap(one, other):
    return jnp.logical_and(one[0] <= other[1], other[0] <= one[1])


def meet_kernel(table, fresh, rights, pairs, inputs, first, last, *refs):
    given, outs = refs[:inputs], refs[inputs:]
    left, left_ids, left_best, right_out = outs[:4]
    right, right_ids, right_best = outs[5:] if last else outs[4:]

    def ids_of(piece):
        ref, start, rows = given[piece[0]], piece[1], piece[2]
        return ref[ref.shape[0] - TAGS :, start : start + rows].astype(jnp.float32)

    def span_right(section):
        low, high = None, None
        for piece in section:
            ids = ids_of(piece)
            there = jnp.where(ids > 0.0, ids, 1e6)
            low = there if low is None else jnp.minimum(low, there)
            high = ids if high is None else jnp.maximum(high, ids)
        return jnp.min(low), jnp.max(high)

    def span_left(sections):
        lows, highs = zip(*[section_span[l] for l in sections])
        return functools.reduce(jnp.minimum, lows), functools.reduce(jnp.maximum, highs)

    if first:
        left_best[...] = jnp.full(left_best.shape, FILL, jnp.float32)
    for number, section in fresh.items():
        at = table[number][0]
        for piece in section:
            index, start, rows = piece
            left[at : at + rows, :] = given[index][start : start + rows, :]
            left_ids[at : at + rows, :TAGS] = jnp.transpose(ids_of(piece))
            at += rows

    tested = [(r, l) for r, l, _, test in pairs if test]
    right_span = {r: span_right(rights[r[0]]) for r in sorted({r for r, _ in tested})}
    section_span = {}
    for l in sorted({i for _, group in tested for i in group}):
        at, rows = table[l]
        ids = left_ids[at : at + rows, :TAGS]
        section_span[l] = jnp.min(ids), jnp.max(ids)
    left_span = {l: span_left(l) for l in sorted({l for _, l in tested})}
    wanted = {(r, l): overlap(right_span[r], left_span[l]) for r, l in tested}

    right_at, at = [], 0
    for section in rights:
        right_at.append((at, padded(section)))
        at += padded(section)

    def fill_right(number):
        at = right_at[number][0]
        for piece in rights[number]:
            index, start, rows = piece
            right[at : at + rows, :] = given[index][start : start + rows, :]
            right_ids[:, at : at + rows] = ids_of(piece)
            at += rows

    right_best[...] = jnp.full(right_best.shape, FILL, jnp.float32)
    right_ids[...] = jnp.full(right_ids.shape, -1.0, jnp.float32)
    for number in range(len(rights)):
        uses = [p for p in pairs if number in p[0]]
        load = functools.partial(fill_right, number)
        if all(p[3] for p in uses):
            pl.when(functools.reduce(jnp.logical_or, [wanted[p[0], p[1]] for p in uses]))(load)
        else:
            load()

    def score(r, l, same):
        lane, row = right_at[r[0]][0], table[l[0]][0]
        lanes = sum(right_at[i][1] for i in r)
        rows = sum(table[i][1] for i in l)
        step = rows
        while step * lanes > 512 * 1024 and step % 32 == 0:
            step //= 2
        across = slice(lane, lane + lanes)

        def turn(index, _):
            at = row if rows == step else pl.multiple_of(row + index * step, 16)
            down = pl.ds(at, step)
            scores = lax.dot_general(
                left[down, :],
                right[across, :],
                (((1,), (1,)), ((), ())),
                preferred_element_type=jnp.float32,
            )
            scores = jnp.where(left_ids[down, :1] == right_ids[:1, across], scores, FILL)
            if same is not None:
                skip, start, count = same
                theirs = lax.broadcasted_iota(jnp.int32, (step, lanes), 0) + (index * step - skip)
                mine = lax.broadcasted_iota(jnp.int32, (step, lanes), 1) - start
                inside = jnp.logical_and(mine >= 0, mine < count)
                scores = jnp.where(jnp.logical_and(theirs == mine, inside), FILL, scores)
            left_best[down, :] = jnp.maximum(left_best[down, :], lane_fold(scores))
            right_best[:, across] = jnp.maximum(right_best[:, across], column_fold(scores))
            return 0

        if rows == step:
            turn(0, 0)
        else:
            lax.fori_loop(0, rows // step, turn, 0)

    for r, l, same, test in pairs:
        run = functools.partial(score, r, l, same)
        if test:
            pl.when(wanted[r, l])(run)
        else:
            run()
    right_out[...] = jnp.max(right_best[...], axis=0, keepdims=True)
    if last:
        outs[4][...] = jnp.max(jnp.transpose(left_best[...]), axis=0, keepdims=True)


def meet(table, state, fresh, rights, pairs, last=False, earlier=()):
    blocks = []

    def plan(section):
        pieces = []
        for block, start, rows, _ in section:
            known = [i for i, b in enumerate(blocks) if b is block]
            if not known:
                blocks.append(block)
            pieces.append((known[0] if known else len(blocks) - 1, start, rows))
        return pieces

    def goals(section):
        filler = padded(section) - sum(p[2] for p in section)
        return [(p[3], p[2]) for p in section] + [(None, filler)]

    plan_left = {number: plan(section) for number, section in fresh.items()}
    plan_right = [plan(section) for section in rights]
    width = blocks[0].shape[1]
    count = sum(rows for _, rows in table)
    total = sum(padded(section) for section in rights)
    inputs, first = len(blocks), not state
    unread = len(state) + len(earlier)

    def kernel(*refs):
        meet_kernel(
            table, plan_left, plan_right, pairs, inputs, first, last,
            *refs[:inputs], *refs[inputs + unread :]
        )

    outs = [
        pltpu.VMEM((count, width), jnp.bfloat16),
        pltpu.VMEM((count, LANES), jnp.float32),
        pltpu.VMEM((count, LANES), jnp.float32),
        jax.ShapeDtypeStruct((1, total), jnp.float32),
    ]
    if last:
        outs.append(jax.ShapeDtypeStruct((1, count), jnp.float32))
    *state, right_best = pl.pallas_call(
        kernel,
        out_shape=outs,
        in_specs=[WHOLE] * (inputs + len(state)) + [ANYWHERE] * len(earlier),
        out_specs=[WHOLE] * len(outs),
        input_output_aliases={inputs + i: i for i in range(len(state))},
        scratch_shapes=[
            pltpu.VMEM((total, width), jnp.bfloat16),
            pltpu.VMEM((TAGS, total), jnp.float32),
            pltpu.VMEM((8, total), jnp.float32),
        ],
        compiler_params=grant(24),
        cost_estimate=pl.CostEstimate(flops=0, bytes_accessed=0, transcendentals=0),
        name="meet",
    )(*blocks, *state, *earlier)
    found = []
    if last:
        left_best, right_best = right_best, state.pop()
        found = [(left_best, None)]
    return state, [*found, (right_best, sum((goals(section) for section in rights), []))]


def route_kernel(plan, parts, chips, cores, half, near, *refs):
    given, out_ref, gathered = refs[:-2], refs[-2], refs[-1]
    chip, members = lax.axis_index("blk"), chips * cores
    part, me = chip // chips, lax.rem(chip, chips) * cores + lax.axis_index("split")
    slots = 2 * half
    out_ref[...] = jnp.full(out_ref.shape, FILL, jnp.float32)
    gathered[...] = jnp.full(gathered.shape, FILL, jnp.float32)
    starts = {"u": members * parts * slots, "v": members * parts * slots + parts * half}
    for ref, pieces in zip(given, plan):
        at = 0
        for to, entries in pieces:
            if to is not None:
                gathered[:, to : to + entries] = jnp.maximum(
                    gathered[:, to : to + entries], ref[:, at : at + entries]
                )
            at += entries
    for member in range(members):
        whose = lax.bitwise_xor(me, member)
        for k in range(parts):
            at = (member * parts + k) * slots
            source = lax.bitwise_xor(part, k) * members + whose
            out_ref[source, :, :slots] = gathered[:, at : at + slots]
    beyond = lax.rem(part + parts - 1 + 2 * lax.rem(part, 2), parts)
    if near:
        beyond = lax.bitwise_xor(part, 3)
    next_to = lax.bitwise_xor(part, 1)
    from_u = [next_to] + [lax.bitwise_xor(next_to, k) for k in range(2, parts)] + [part]
    from_v = [beyond, lax.bitwise_xor(beyond, 1)]
    from_v += [next_to, part] if near else [lax.bitwise_xor(beyond, k) for k in range(2, parts)]
    for kind, sources, lane in (("u", from_u, slots), ("v", from_v, slots + half)):
        for index, source in enumerate(sources):
            at = starts[kind] + index * half
            out_ref[source * members + me, :, lane : lane + half] = gathered[:, at : at + half]


def back_kernel(parts, members, got_ref, rank_ref, out_ref):
    slots = got_ref.shape[2] // 2
    half = slots // 2
    rows = []
    for part in range(parts):
        best = got_ref[part * members]
        for member in range(1, members):
            best = jnp.maximum(best, got_ref[part * members + member])
        rows.append(best)
    rank = rank_ref[...]
    nothing = jnp.full((1, half), FILL, jnp.float32)
    best = jnp.full((8, rank.shape[1]), FILL, jnp.float32)
    for part in range(parts):
        beyond = part + 1 if part % 2 else part - 1
        there = 0 <= beyond < parts
        faces = jnp.maximum(rows[part][:, :half], rows[part ^ 1][:, slots : slots + half])
        turned = jnp.maximum(
            rows[part][:, half:slots], rows[beyond][:, slots + half :] if there else nothing
        )
        near_u, far_u = faces[:, : half // 2], faces[:, half // 2 :]
        near_v, far_v = turned[:, : half // 2], turned[:, half // 2 :]
        order = [near_u, far_u, far_v, near_v] if part % 2 else [near_v, far_v, far_u, near_u]
        values = spread(jnp.concatenate(order, axis=1))[:, :1]
        slot = lax.broadcasted_iota(jnp.int32, (slots, rank.shape[1]), 0) + part * slots
        best = jnp.maximum(best, column_fold(jnp.where(slot == rank, values, FILL)))
    out_ref[...] = jnp.max(best, axis=0, keepdims=True)


def in_data_order(got, rank, parts, members):
    return pl.pallas_call(
        functools.partial(back_kernel, parts, members),
        out_shape=jax.ShapeDtypeStruct(rank.shape, jnp.float32),
        in_specs=[WHOLE, WHOLE],
        out_specs=WHOLE,
        compiler_params=grant(16),
        name="back",
    )(got, rank)


def body(embeddings, cluster_of, target_pos):
    blocks, cores = lax.axis_size("blk"), lax.axis_size("split")
    rows, width = embeddings.shape
    members = MOST // rows
    chips = members // cores
    parts = blocks // chips
    half = rows // parts // 2
    slots = 2 * half
    def between(array, pairs, name):
        route = [(s * chips + c, t * chips + c) for s, t in pairs for c in range(chips)]
        with jax.named_scope(name):
            return lax.ppermute(array, "blk", route)

    def swap(array, k, name):
        return between(array, [(part, part ^ k) for part in range(parts)], name)

    def chip_swap(array, name):
        with jax.named_scope(name):
            return lax.ppermute(array, "blk", [(b, b ^ 1) for b in range(blocks)])

    def core_swap(array, name):
        with jax.named_scope(name):
            return lax.ppermute(array, "split", [(c, c ^ 1) for c in range(cores)])

    borders = [(p, p + 1) for p in range(1, parts - 1, 2)]
    borders += [(t, s) for s, t in borders]
    near = all(s ^ t == 3 for s, t in borders)

    quart = half // 2
    middle = (parts + 2) // 2
    second, third = [1, *range(2, middle)], list(range(middle, parts))
    u_goal = members * parts * slots
    v_goal = u_goal + parts * half

    def sides(blocks, ks, member=0):
        out = []
        for side in (0, half):
            for m, block in enumerate(blocks, member):
                for i, k in enumerate(ks):
                    goal = (m * parts + k) * slots + side
                    out.append((block, i * slots + side, half, goal))
        return out[: len(out) // 2], out[len(out) // 2 :]

    def whole(block, ks):
        return [(block, i * slots, slots, k * slots) for i, k in enumerate(ks)]

    def visits(pieces, goal):
        near_rows = [(b, at, quart, goal + i * half) for b, at, i in pieces]
        far_rows = [(b, at + quart, quart, goal + i * half + quart) for b, at, i in pieces]
        return near_rows, far_rows

    tag_rows = [TAGS if k < middle else 2 * TAGS for k in range(parts)]
    sent, rank = in_order(embeddings, cluster_of, target_pos, tag_rows, chips, [*second, *third])
    own_0 = sent[0]
    got = [swap(sent[k], k, "rows_2") for k in second]
    over_0 = chip_swap(own_0, "over_0")
    beside_0 = core_swap(own_0, "beside_0")

    def joined(got):
        if len(got) == 1:
            return got[0]
        return pack(got, [[(i, 0, slots) for i in range(len(got))]])[0]

    own_1, own_2 = got[0], joined(got[1:])
    forward = [(len(second) - 1, 0, half)] + [(i, 0, half) for i in range(len(second) - 1)]
    *held, passing = pack(
        [*got[1:], own_0], [forward], held=[sent[k] for k in third], earlier=[over_0]
    )
    got_3 = [swap(b, k, "rows_3") for k, b in zip(third, held)]
    over_1, over_2 = chip_swap(own_1, "over_1"), chip_swap(own_2, "over_2")
    passed_2 = swap(passing, 1, "passed_2")
    across_0 = core_swap(over_0, "across_0")
    beside_1, beside_2 = core_swap(own_1, "beside_1"), core_swap(own_2, "beside_2")

    def pair(member, block_1, block_2):
        return [
            a + b for a, b in zip(sides([block_1], [1], member), sides([block_2], second[1:], member))
        ]

    left_0 = sides([own_0, beside_0, over_0, across_0], [0])
    mine_0, mine_2 = whole(own_0, [0]), sum(pair(0, own_1, own_2), [])
    here_2 = [a + b for a, b in zip(pair(0, own_1, own_2), pair(1, beside_1, beside_2))]
    sizes = [len(third) * members, members, 2 * len(second), 2 * len(second)]
    sizes += [sizes[3], sizes[1], sizes[2], sizes[0]]
    table = [(sum(sizes[:i]) * half, size * half) for i, size in enumerate(sizes)]
    some, mates = len(second) * half, members * half
    state, scores = meet(
        table,
        [],
        {1: left_0[0], 2: here_2[0], 5: left_0[1], 6: here_2[1]},
        [mine_0, mine_2],
        [((0,), (1,), (0, 0, half), False), ((0,), (5,), (0, half, half), False)]
        + [((1,), (1, 2), (mates, 0, some), False), ((1,), (5, 6), (mates, some, some), False)],
    )

    last = len(third)
    own_3 = joined(got_3)
    border = [(last, half, half), (last + 1, half, half)]
    forward = [(i, 0, half) for i in range(last)]
    inputs = [*got_3, own_0, own_1]
    if near:
        inputs.append(sent[2])
        forward.append((last + 2, half, half))
    else:
        border += [(last + 1 + i, half, half) for i in range(1, len(second))]
        border += [(i, half, half) for i in range(last)]
        inputs += got[1:]
    own_3, border, passing = pack(
        inputs, [border, forward], held=[own_3], earlier=[scores[0][0]], spare=TAGS
    )
    over_3 = chip_swap(own_3, "over_3")
    got_border = between(border, borders, "border")
    passed_3 = swap(passing, 1, "passed_3")
    over_1, over_2 = after([over_1, over_2], [own_3, passed_2])
    across_1, across_2 = core_swap(over_1, "across_1"), core_swap(over_2, "across_2")
    beside_3 = core_swap(own_3, "beside_3")
    there_2 = [a + b for a, b in zip(pair(2, over_1, over_2), pair(3, across_1, across_2))]
    visit_2 = [(passed_2, i * half, half, u_goal + i * half) for i in range(len(second))]
    visit_3 = [(sent[1], 0, half, u_goal + (parts - 1) * half)]
    visit_3 += [(passed_3, i * half, half, u_goal + (len(second) + i) * half) for i in range(last)]
    mine_3 = sum(sides([own_3], third), [])
    state, more_scores = meet(
        table,
        state,
        {3: there_2[0], 4: there_2[1]},
        [mine_2, mine_3, visit_2],
        [((0,), (3, 4), None, False), ((1,), (1, 2, 3, 4, 5, 6), None, False)]
        + [((2,), l, None, True) for l in ((1, 2, 3), (4, 5, 6))],
    )
    scores += more_scores

    visit_v = [(got_border, i * half, i) for i in range(2 if near else parts)]
    if near:
        visit_v += [(passed_3, last * half, 2), (held[0], half, 3)]
    visit_v = visits(visit_v, v_goal)
    (over_3,) = after([over_3], [scores[1][0], got_border, passed_3])
    across_3 = core_swap(over_3, "across_3")
    left_3 = sides([own_3, beside_3, over_3, across_3], third)
    some = last * half
    _, more_scores = meet(
        table,
        state,
        {0: left_3[0], 7: left_3[1]},
        [mine_3, visit_2, visit_3, *visit_v],
        [((0, 1, 2), (0,), (0, 0, some), False), ((0, 1, 2), (7,), (0, some, some), False)]
        + [((2,), l, None, True) for l in ((1, 2, 3), (4, 5, 6))]
        + [((r,), l, None, True) for r in (3, 4) for l in ((0, 1, 2, 3), (4, 5, 6, 7))],
        last=True,
    )
    rows_in = [left_3[0], left_0[0], here_2[0], there_2[0], there_2[1], left_0[1], here_2[1], left_3[1]]
    everywhere = [(p[3], p[2]) for section in rows_in for p in section]
    scores += [(best, goals or everywhere) for best, goals in more_scores]
    found = pl.pallas_call(
        functools.partial(
            route_kernel, [goals for _, goals in scores], parts, chips, cores, half, near
        ),
        out_shape=jax.ShapeDtypeStruct((parts * members, 1, 2 * slots), jnp.float32),
        in_specs=[WHOLE] * len(scores),
        out_specs=WHOLE,
        scratch_shapes=[pltpu.VMEM((1, v_goal + parts * half), jnp.float32)],
        compiler_params=grant(8),
        name="route",
    )(*[best for best, _ in scores])
    got = lax.all_to_all(found, ("blk", "split"), split_axis=0, concat_axis=0, tiled=True)
    return in_data_order(got, rank, parts, members).reshape(rows)


def solution(mesh):
    spec = P(("groups", "blk", "split"))
    return jax.shard_map(
        body,
        mesh=mesh,
        in_specs=(P(("groups", "blk", "split"), None), spec, spec),
        out_specs=spec,
        check_vma=False,
    )
```
